32 devices in a mesh: dp: 4 (over y, x), seq: 8 (over z, core).
Axes of the slice: x: 2, y: 2, z: 4, core: 2. Of those that a mesh axis runs over, the one named last changes fastest.
Arguments:
- inputs: bfloat16 [2, 4, 2048, 1024], P(None, 'dp', 'seq'), may hold values from -6 to 6
- doc_flags: int32 [2, 4, 2048], P(None, 'dp', 'seq'), may hold values from 0 to 1, as said below
- first_gain: bfloat16 [1024], P(('dp', 'seq')), may hold values from 0.25 to 1.75
- first_bias: bfloat16 [1024], P(('dp', 'seq')), may hold values from -3 to 3
- w_query: bfloat16 [1024, 1024], P(('dp', 'seq')), may hold values from -0.1875 to 0.1875
- w_key: bfloat16 [1024, 1024], P(('dp', 'seq')), may hold values from -0.1875 to 0.1875
- w_value: bfloat16 [1024, 2048], P(('dp', 'seq')), may hold values from -0.1875 to 0.1875
- w_gate: bfloat16 [1024, 2048], P(('dp', 'seq')), may hold values from -0.1875 to 0.1875
- group_gain: bfloat16 [2048], P(('dp', 'seq')), may hold values from 0.25 to 1.75
- w_output: bfloat16 [2048, 1024], P(('dp', 'seq')), may hold values from -0.25 to 0.25
- second_gain: bfloat16 [1024], P(('dp', 'seq')), may hold values from 0.25 to 1.75
- second_bias: bfloat16 [1024], P(('dp', 'seq')), may hold values from -3 to 3
- w_up: bfloat16 [1024, 2048], P(('dp', 'seq')), may hold values from -0.1875 to 0.1875
- w_down: bfloat16 [2048, 1024], P(('dp', 'seq')), may hold values from -0.1875 to 0.1875
- cotangent: bfloat16 [2, 4, 2048, 1024], P(None, 'dp', 'seq'), may hold values from -6 to 6
Outputs:
- output: bfloat16 [2, 4, 2048, 1024], P(None, 'dp', 'seq')
- input_grad: float32 [2, 4, 2048, 1024], P(None, 'dp', 'seq')
- grad_first_gain: float32 [1024], P(('dp', 'seq'))
- grad_first_bias: float32 [1024], P(('dp', 'seq'))
- grad_w_query: float32 [1024, 1024], P(('dp', 'seq'))
- grad_w_key: float32 [1024, 1024], P(('dp', 'seq'))
- grad_w_value: float32 [1024, 2048], P(('dp', 'seq'))
- grad_w_gate: float32 [1024, 2048], P(('dp', 'seq'))
- grad_group_gain: float32 [2048], P(('dp', 'seq'))
- grad_w_output: float32 [2048, 1024], P(('dp', 'seq'))
- grad_second_gain: float32 [1024], P(('dp', 'seq'))
- grad_second_bias: float32 [1024], P(('dp', 'seq'))
- grad_w_up: float32 [1024, 2048], P(('dp', 'seq'))
- grad_w_down: float32 [2048, 1024], P(('dp', 'seq'))
The draws below stay inside these ranges and needn't reach their ends.
Inputs may be any that keep to these rules, and one draw needn't show every extreme that they name: `doc_flags`: position 0 of every row holds 1. Of the 2 rows that one index of dp holds over all micro-batches, one holds no other 1, and each of the others holds one to three more.
All inputs are finite; a program needn't handle non-finite values.
Results may differ from the reference program's by a relative error of at most 0.013.
The reference program's roundings to bfloat16 on the way count: a program that leaves them out, or rounds other values in their place, can miss the bound.
Values may be sent and summed in bfloat16 or wider, within the bound.
No kernel may reach another device: no remote copies, remote signals or barrier semaphores. Data moves between devices by JAX's collectives and lax.ppermute only.
A program may use at most 320 MiB of HBM per device.

```python
import jax
import jax.numpy as jnp
from jax import lax

D = 1024
H = 4
QK = 256
VH = 512
FF = 2048
MB = 2
ROWS_DEV = 1
SPAN = 256
VW = 2048
ROWS = 4
LENGTH = 2048


def draw_doc_flags(key, part):
    key = jax.random.fold_in(key, 7)
    keys = jax.random.split(key, 3)
    index = jnp.arange(LENGTH, dtype=jnp.int32)
    starts = jax.random.randint(keys[0], (MB, ROWS, 3), 1, LENGTH)
    number = jax.random.randint(keys[1], (MB, ROWS, 1), 1, 4)
    used = jnp.arange(3, dtype=jnp.int32)[None, None, :] < number
    hits = jnp.any((index[None, None, None, :] == starts[..., None]) & used[..., None], axis=2)
    picked = jax.random.randint(keys[2], (ROWS // ROWS_DEV,), 0, MB * ROWS_DEV)
    row_index = jnp.arange(ROWS, dtype=jnp.int32)
    slot = jnp.arange(MB, dtype=jnp.int32)[:, None] * ROWS_DEV + (row_index % ROWS_DEV)[None, :]
    whole = slot == picked[row_index // ROWS_DEV][None, :]
    flags = jnp.where(whole[..., None], False, hits) | (index == 0)[None, None, :]
    return flags.astype(jnp.int32)


def block_levels(own_key, shape, cuts, low, largest):
    def one(position, blocks):
        steps = jax.random.uniform(jax.random.fold_in(jax.random.fold_in(own_key, 6), position), (blocks,), jnp.float32, low / len(cuts), largest / len(cuts))
        return jnp.repeat(jnp.exp(steps), shape[position] // blocks).reshape((-1,) + (1,) * (len(shape) - position - 1))

    loudness = one(*cuts[0])
    for cut in cuts[1:]:
        loudness = loudness * one(*cut)
    return loudness


def bell_draw(stream_key, shape, scale, bound, cuts=(), held_as=jnp.bfloat16):
    array = scale * jax.random.normal(stream_key, shape, jnp.float32)
    if cuts:
        array = array * block_levels(stream_key, shape, cuts, -0.22, 0.18)
    return jnp.clip(array, -bound, bound).astype(held_as)


def setup_inputs(seed: int = 0) -> dict:
    key_list = jax.random.split(jax.random.key(seed), 16)
    inputs = bell_draw(key_list[0], (MB, ROWS, LENGTH, D), 1.0, 6.0, ((1, 4), (2, 8)))
    doc_flags = draw_doc_flags(jax.random.fold_in(key_list[15], 71), 0)
    first_gain = jnp.clip(1.0 + 0.15 * jax.random.normal(key_list[2], (D,), jnp.float32), 0.25, 1.75).astype(jnp.bfloat16)
    first_bias = bell_draw(key_list[3], (D,), 0.5, 3.0, ((0, 32),))
    w_query = bell_draw(key_list[4], (D, D), D ** -0.5, 0.1875, ((0, 32),))
    w_key = bell_draw(key_list[5], (D, D), D ** -0.5, 0.1875, ((0, 32),))
    w_value = bell_draw(key_list[6], (D, VW), D ** -0.5, 0.1875, ((0, 32),))
    w_gate = bell_draw(key_list[7], (D, VW), D ** -0.5, 0.1875, ((0, 32),))
    group_gain = jnp.clip(1.0 + 0.15 * jax.random.normal(key_list[8], (VW,), jnp.float32), 0.25, 1.75).astype(jnp.bfloat16)
    w_output = bell_draw(key_list[9], (VW, D), (VW // 4) ** -0.5, 0.25, ((0, 32),))
    second_gain = jnp.clip(1.0 + 0.15 * jax.random.normal(key_list[10], (D,), jnp.float32), 0.25, 1.75).astype(jnp.bfloat16)
    second_bias = bell_draw(key_list[11], (D,), 0.5, 3.0, ((0, 32),))
    w_up = bell_draw(key_list[12], (D, FF), D ** -0.5, 0.1875, ((0, 32),))
    w_down = bell_draw(key_list[13], (FF, D), (FF // 2) ** -0.5, 0.1875, ((0, 32),))
    cotangent = bell_draw(key_list[14], (MB, ROWS, LENGTH, D), 1.0, 6.0, ((1, 4), (2, 8)))
    return {"inputs": inputs, "doc_flags": doc_flags, "first_gain": first_gain, "first_bias": first_bias, "w_query": w_query, "w_key": w_key, "w_value": w_value, "w_gate": w_gate, "group_gain": group_gain, "w_output": w_output, "second_gain": second_gain, "second_bias": second_bias, "w_up": w_up, "w_down": w_down, "cotangent": cotangent}


HIGHEST = lax.Precision.HIGHEST

@jax.custom_vjp
def low(v):
    return lax.optimization_barrier(v.astype(jnp.bfloat16)).astype(jnp.float32)

@jax.custom_vjp
def low_back(v):
    return v

def low_keep(v):
    return (low(v), None)

def low_pass(kept, grad):
    return (grad,)

def back_keep(v):
    return (v, None)

def back_low(kept, grad):
    return (low(grad),)
low.defvjp(low_keep, low_pass)
low_back.defvjp(back_keep, back_low)

def product(left, right):
    return jnp.dot(left, right, precision=HIGHEST)

def layer_norm(values, gain, shift):
    average = lax.optimization_barrier(jnp.mean(values, axis=-1, keepdims=True))
    centred = values - average
    spread = lax.optimization_barrier(jnp.mean(centred * centred, axis=-1, keepdims=True))
    return centred * lax.rsqrt(spread + 1e-05) * gain + shift

def rotate(values, positions):
    half = values.shape[-1] // 2
    frequency = 10000.0 ** (-jnp.arange(half, dtype=jnp.float32) / half)
    angles = positions.astype(jnp.float32)[:, None] * frequency[None, :]
    cosine = jnp.cos(angles)[:, None, :]
    sine = jnp.sin(angles)[:, None, :]
    first = values[..., :half]
    second = values[..., half:]
    return jnp.concatenate([first * cosine - second * sine, second * cosine + first * sine], axis=-1)

def norm_gate(retained, gate_pre, gain):
    grouped = retained.reshape(retained.shape[0], H, VH)
    average = lax.optimization_barrier(jnp.mean(grouped, axis=-1, keepdims=True))
    centred = grouped - average
    spread = lax.optimization_barrier(jnp.mean(centred * centred, axis=-1, keepdims=True))
    normal = (centred * lax.rsqrt(spread + 1.0)).reshape(retained.shape) * gain
    return jax.nn.silu(gate_pre) * normal

def decay_rates():
    return jnp.log1p(-2.0 ** (-5.0 - 3.0 * jnp.arange(H, dtype=jnp.float32)))

def decay_tables(flags, rates):
    length = flags.shape[-1]
    counts = jnp.cumsum(flags.astype(jnp.int32), axis=-1, dtype=jnp.int32)
    index = jnp.arange(length, dtype=jnp.int32)
    spacing = (index[:, None] - index[None, :]).astype(jnp.float32)
    same = (counts[:, :, None] == counts[:, None, :]) & (index[:, None] >= index[None, :])[None]
    zero = jnp.zeros((), rates.dtype)
    mask = jnp.where(same[:, None], jnp.exp(spacing[None, None] * rates[None, :, None, None]), zero)
    enter = jnp.where((counts == 0)[:, None, :], jnp.exp((index + 1).astype(jnp.float32)[None, None, :] * rates[None, :, None]), zero)
    leave = jnp.where((counts == counts[:, -1:])[:, None, :], jnp.exp((length - 1 - index).astype(jnp.float32)[None, None, :] * rates[None, :, None]), zero)
    carry = jnp.where((counts[:, -1] == 0)[:, None], jnp.exp(rates * float(length))[None, :], zero)
    return (mask, enter, leave, carry)

def retain(query_r, key_r, value_r, flags):
    blocks = query_r.shape[0] // SPAN
    rates = decay_rates()

    def split(values):
        return values.reshape(blocks, SPAN, H, values.shape[-1]).transpose(0, 2, 1, 3)

    def one_block(state, pieces):
        query_c, key_c, value_c, flag_c = pieces
        mask, enter, leave, carry = decay_tables(flag_c[None], rates)
        scores = low_back(jnp.einsum('hcd,hsd->hcs', query_c, key_c, precision=HIGHEST))
        mixing = low(scores * mask[0])
        inner = jnp.einsum('hcs,hse->hce', mixing, value_c, precision=HIGHEST)
        query_entered = low(query_c * enter[0][..., None])
        cross = jnp.einsum('hcd,hde->hce', query_entered, low(state), precision=HIGHEST)
        weighted_keys = low(key_c * leave[0][..., None])
        summary = low_back(jnp.einsum('hsd,hse->hde', weighted_keys, value_c, precision=HIGHEST))
        new_state = (carry[0][:, None, None] * state + summary).astype(state.dtype)
        return (new_state, low_back(inner + cross))
    start = jnp.zeros((H, QK, VH), query_r.dtype)
    _, outputs = lax.scan(jax.checkpoint(one_block), start, (split(query_r), split(key_r), split(value_r), flags.astype(jnp.int32).reshape(blocks, SPAN)))
    return outputs.transpose(0, 2, 1, 3).reshape(blocks * SPAN, H * VH)

def block_forward(sequence, flags, first_gain, first_bias, w_query, w_key, w_value, w_gate, group_gain, w_output, second_gain, second_bias, w_up, w_down):
    length = sequence.shape[0]
    positions = jnp.arange(length, dtype=jnp.int32)
    normed = low(layer_norm(sequence, first_gain, first_bias))
    query_pre = low_back(product(normed, w_query))
    key_pre = low_back(product(normed, w_key))
    value_pre = low_back(product(normed, w_value))
    gate_pre = low_back(product(normed, w_gate))
    query_r = low(rotate(query_pre.reshape(length, H, QK), positions))
    key_r = low(rotate(key_pre.reshape(length, H, QK), positions) * QK ** (-0.5))
    value_r = low(value_pre.reshape(length, H, VH))
    retained = retain(query_r, key_r, value_r, flags)
    mixed = low(norm_gate(retained, gate_pre, group_gain))
    hidden_in = sequence + low_back(product(mixed, w_output))
    normed_second = low(layer_norm(hidden_in, second_gain, second_bias))
    upward = low_back(product(normed_second, w_up))
    activated = low(jax.nn.gelu(upward, approximate=True))
    return hidden_in + low_back(product(activated, w_down))

def reference(inputs, doc_flags, first_gain, first_bias, w_query, w_key, w_value, w_gate, group_gain, w_output, second_gain, second_bias, w_up, w_down, cotangent):
    params = tuple((weight.astype(jnp.float32) for weight in (first_gain, first_bias, w_query, w_key, w_value, w_gate, group_gain, w_output, second_gain, second_bias, w_up, w_down)))
    all_rows = inputs.reshape(MB * ROWS, LENGTH, D).astype(jnp.float32)
    all_flags = doc_flags.reshape(MB * ROWS, LENGTH).astype(jnp.int32)
    all_grads = cotangent.reshape(MB * ROWS, LENGTH, D).astype(jnp.float32)

    def row_step(totals, pieces):
        sequence, flags, grad_out = pieces

        def forward(row_in, *weights):
            return block_forward(row_in, flags, *weights)
        result, pull = jax.vjp(forward, sequence, *params)
        pulled = pull(grad_out)
        totals = tuple(((total + grad).astype(total.dtype) for total, grad in zip(totals, pulled[1:])))
        return (totals, (result.astype(jnp.bfloat16), pulled[0].astype(jnp.float32)))
    start = tuple((jnp.zeros(weight.shape, jnp.float32) for weight in params))
    totals, (outputs, input_grads) = lax.scan(row_step, start, (all_rows, all_flags, all_grads))
    shape = (MB, ROWS, LENGTH, D)
    return (outputs.reshape(shape), input_grads.reshape(shape), totals[0], totals[1], totals[2], totals[3], totals[4], totals[5], totals[6], totals[7], totals[8], totals[9], totals[10], totals[11])
```

```python
import jax
import jax.numpy as jnp
from jax import lax
from jax.sharding import PartitionSpec as P

H = 4
QK = 256
VH = 512


AXES = ("dp", "seq")


def devices():
    return lax.axis_size("dp") * lax.axis_size("seq")


def place():
    return lax.axis_index("dp") * lax.axis_size("seq") + lax.axis_index("seq")


def swap(values, bit):
    return lax.ppermute(values, AXES, [(i, i ^ bit) for i in range(devices())])


def side(bit):
    return (place() // bit) % 2 == 1


def chip_bits():
    return [1 << k for k in range(1, devices().bit_length() - 1)]


def orders():
    bits = chip_bits()
    far = 4
    near = [bit for bit in bits if bit != far and bit != 2] + [2]
    return [near[turn:] + near[:turn] + [far] for turn in range(3)]


def cut(width):
    tiles = width // 128
    sizes = [tiles // 3 + (1 if k < tiles % 3 else 0) for k in range(3)]
    edges = [0]
    for size in sizes:
        edges.append(edges[-1] + 128 * size)
    return list(zip(edges[:-1], edges[1:]))


def halves(values):
    half = values.shape[-1] // 2
    upper = side(1)
    low, high = values[..., :half], values[..., half:]
    return jnp.where(upper, high, low), jnp.where(upper, low, high)


def spread_class(piece, order):
    held = []
    for bit in order[::-1]:
        spot = sum(1 for other in held if other > bit)
        other = swap(piece, bit)
        upper = side(bit)
        piece = jnp.stack(
            [jnp.where(upper, other, piece), jnp.where(upper, piece, other)], axis=spot
        )
        held.append(bit)
    return piece


def spread(shard):
    rows, width = shard.shape
    keep, give = halves(shard)
    got = swap(give, 1)
    upper = side(1)
    piece = jnp.concatenate([jnp.where(upper, got, keep), jnp.where(upper, keep, got)], axis=0)
    parts = []
    others = []
    for (start, stop), order in zip(cut(width // 2), orders()):
        part = spread_class(piece[:, start:stop], order).reshape(-1, stop - start)
        parts.append(part)
        others.append(swap(part, 1))
    upper = side(1)
    first = [jnp.where(upper, b, a) for a, b in zip(parts, others)]
    second = [jnp.where(upper, a, b) for a, b in zip(parts, others)]
    return jnp.concatenate(first + second, axis=1)


def collect_class(total, order):
    count = devices() // 2
    rows = total.shape[0] // count
    held = sorted(order, reverse=True)
    total = total.reshape((2,) * len(held) + (rows, total.shape[-1]))
    for bit in order:
        spot = held.index(bit)
        upper = side(bit)
        low = lax.index_in_dim(total, 0, spot, False)
        high = lax.index_in_dim(total, 1, spot, False)
        got = swap(jnp.where(upper, low, high), bit)
        total = jnp.where(upper, high, low).astype(jnp.float32) + got.astype(jnp.float32)
        held.remove(bit)
        if held:
            total = total.astype(jnp.bfloat16)
    return total


def collect(left, right):
    keep, give = halves(right)
    got = swap(weight_grad(left, give).astype(jnp.bfloat16), 1)
    total = (weight_grad(left, keep) + got.astype(jnp.float32)).astype(jnp.bfloat16)
    parts = [
        collect_class(total[:, start:stop], order)
        for (start, stop), order in zip(cut(total.shape[-1]), orders())
    ]
    whole = jnp.concatenate(parts, axis=1)
    rows = whole.shape[0] // 2
    upper = side(1)
    mine = jnp.where(upper, whole[rows:], whole[:rows])
    got = swap(jnp.where(upper, whole[:rows], whole[rows:]), 1)
    return jnp.concatenate([jnp.where(upper, got, mine), jnp.where(upper, mine, got)], axis=1)


def collect_vector(values):
    count = devices()
    total = values.reshape((2,) * (count.bit_length() - 1) + (-1,))
    for bit in [1 << k for k in range(count.bit_length() - 1)][::-1]:
        upper = side(bit)
        got = swap(jnp.where(upper, total[0], total[1]), bit)
        total = jnp.where(upper, total[1], total[0]) + got
    return total


def spread_vector(piece):
    for bit in [1 << k for k in range(devices().bit_length() - 1)]:
        other = swap(piece, bit)
        upper = side(bit)
        piece = jnp.concatenate(
            [jnp.where(upper, other, piece), jnp.where(upper, piece, other)], axis=0
        )
    return piece


def scaled(carry, state):
    return carry[:, None, None] * state


def pass_states(carry, part, reverse):
    count = lax.axis_size("seq")
    chips = count // 2
    upper = lax.axis_index("seq") % 2 == 1
    own_carry = jnp.where(upper, carry[1], carry[0])
    near_carry = swap(jnp.where(upper, carry[0], carry[1])[None], 1)[0]
    own = jnp.where(upper, part[1], part[0])
    near = swap(jnp.where(upper, part[0], part[1]), 1)
    turned = upper if not reverse else jnp.logical_not(upper)
    first_carry = jnp.where(turned, near_carry, own_carry)
    last_carry = jnp.where(turned, own_carry, near_carry)
    first = jnp.where(turned, near, own)
    last = jnp.where(turned, own, near)
    joined = scaled(last_carry, first) + last
    both = first_carry * last_carry
    entering = jnp.zeros_like(joined)
    for step in range(1, chips):
        message = (joined + scaled(both, entering)).astype(jnp.bfloat16)
        source, target = (step - 1, step) if not reverse else (chips - step, chips - step - 1)
        pairs = [(2 * source + core, 2 * target + core) for core in range(2)]
        entering = entering + lax.ppermute(message, "seq", pairs).astype(jnp.float32)
    middle = scaled(first_carry, entering) + first
    mine = jnp.where(turned, middle, entering).astype(jnp.bfloat16)
    theirs = swap(jnp.where(turned, entering, middle).astype(jnp.bfloat16), 1)
    return jnp.stack([jnp.where(upper, theirs, mine), jnp.where(upper, mine, theirs)])


def layer_norm(values, gain, shift):
    average = jnp.mean(values, axis=-1, keepdims=True)
    centred = values - average
    spread = jnp.mean(centred * centred, axis=-1, keepdims=True)
    return centred * lax.rsqrt(spread + 1e-05) * gain + shift


def rotate(values, positions):
    half = values.shape[-1] // 2
    frequency = 10000.0 ** (-jnp.arange(half, dtype=jnp.float32) / half)
    angles = positions.astype(jnp.float32)[:, None] * frequency[None, :]
    cosine = jnp.cos(angles)[:, None, :]
    sine = jnp.sin(angles)[:, None, :]
    first = values[..., :half]
    second = values[..., half:]
    return jnp.concatenate(
        [first * cosine - second * sine, second * cosine + first * sine], axis=-1
    )


def unrotate(grad, positions, factor):
    _, pull = jax.vjp(lambda values: rotate(values, positions) * factor, jnp.zeros_like(grad))
    return pull(grad)[0]


def norm_gate(retained, gate_pre, gain):
    grouped = retained.reshape(retained.shape[0], H, VH)
    average = jnp.mean(grouped, axis=-1, keepdims=True)
    centred = grouped - average
    spread = jnp.mean(centred * centred, axis=-1, keepdims=True)
    normal = (centred * lax.rsqrt(spread + 1.0)).reshape(retained.shape) * gain
    return jax.nn.silu(gate_pre) * normal


def decay_rates():
    return jnp.log1p(-(2.0 ** (-5.0 - 3.0 * jnp.arange(H, dtype=jnp.float32))))


def decay_tables(flags, rates):
    length = flags.shape[-1]
    counts = jnp.cumsum(flags, axis=-1, dtype=jnp.int32)
    index = jnp.arange(length, dtype=jnp.int32)
    spacing = (index[:, None] - index[None, :]).astype(jnp.float32)
    same = (counts[:, :, None] == counts[:, None, :]) & (index[:, None] >= index[None, :])[None]
    zero = jnp.zeros((), rates.dtype)
    mask = jnp.where(same[:, None], jnp.exp(spacing[None, None] * rates[None, :, None, None]), zero)
    enter = jnp.where(
        (counts == 0)[:, None, :],
        jnp.exp((index + 1).astype(jnp.float32)[None, None, :] * rates[None, :, None]),
        zero,
    )
    leave = jnp.where(
        (counts == counts[:, -1:])[:, None, :],
        jnp.exp((length - 1 - index).astype(jnp.float32)[None, None, :] * rates[None, :, None]),
        zero,
    )
    carry = jnp.where((counts[:, -1] == 0)[:, None], jnp.exp(rates * float(length))[None, :], zero)
    return (mask, enter, leave, carry)


def project(left, right):
    return jnp.dot(left, right, preferred_element_type=jnp.float32)


def weight_grad(left, right):
    return lax.dot_general(
        left, right, (((0,), (0,)), ((), ())), preferred_element_type=jnp.float32
    )


def back_project(grad, weight):
    return lax.dot_general(
        grad, weight, (((1,), (1,)), ((), ())), preferred_element_type=jnp.float32
    )


def to_heads(values, rows, width):
    return values.reshape(rows, -1, H, width).transpose(0, 2, 1, 3)


def from_heads(values):
    rows, heads, length, width = values.shape
    return values.transpose(0, 2, 1, 3).reshape(rows * length, heads * width)


def attention_forward(weights, inputs, flags, positions):
    first_gain, first_bias, w_query, w_key, w_value, w_gate, group_gain, w_output = weights
    rows = inputs.shape[0]
    flat = inputs.reshape(-1, inputs.shape[-1]).astype(jnp.float32)
    normed = layer_norm(
        flat, first_gain.astype(jnp.float32), first_bias.astype(jnp.float32)
    ).astype(jnp.bfloat16)
    query_pre = project(normed, w_query)
    key_pre = project(normed, w_key)
    value_r = to_heads(project(normed, w_value).astype(jnp.bfloat16), rows, VH)
    gate_pre = project(normed, w_gate)
    query_r = (
        rotate(query_pre.reshape(rows, -1, H, QK), positions)
        .astype(jnp.bfloat16)
        .transpose(0, 2, 1, 3)
    )
    key_r = (
        (rotate(key_pre.reshape(rows, -1, H, QK), positions) * QK ** (-0.5))
        .astype(jnp.bfloat16)
        .transpose(0, 2, 1, 3)
    )
    tables = decay_tables(flags, decay_rates())
    mask, enter, leave, carry = tables
    scores = jnp.einsum("rhcd,rhsd->rhcs", query_r, key_r, preferred_element_type=jnp.float32)
    mixing = (scores * mask).astype(jnp.bfloat16)
    inner = jnp.einsum("rhcs,rhse->rhce", mixing, value_r, preferred_element_type=jnp.float32)
    weighted_keys = (key_r.astype(jnp.float32) * leave[..., None]).astype(jnp.bfloat16)
    summary = jnp.einsum(
        "rhsd,rhse->rhde", weighted_keys, value_r, preferred_element_type=jnp.float32
    )
    state_low = pass_states(carry, summary, False)
    query_entered = (query_r.astype(jnp.float32) * enter[..., None]).astype(jnp.bfloat16)
    cross = jnp.einsum(
        "rhcd,rhde->rhce", query_entered, state_low, preferred_element_type=jnp.float32
    )
    retained = from_heads(inner + cross)
    mixed = norm_gate(retained, gate_pre, group_gain.astype(jnp.float32)).astype(jnp.bfloat16)
    hidden_in = flat + project(mixed, w_output)
    saved = (
        flat,
        normed,
        gate_pre,
        query_r,
        key_r,
        value_r,
        mixing,
        weighted_keys,
        query_entered,
        state_low,
        tables,
        retained,
        mixed,
    )
    return (hidden_in, saved)


def feed_forward(weights, hidden_in):
    second_gain, second_bias, w_up, w_down = weights
    normed = layer_norm(
        hidden_in, second_gain.astype(jnp.float32), second_bias.astype(jnp.float32)
    ).astype(jnp.bfloat16)
    upward = project(normed, w_up)
    activated = jax.nn.gelu(upward, approximate=True).astype(jnp.bfloat16)
    output = hidden_in + project(activated, w_down)
    return (output, (hidden_in, normed, upward, activated))


def feed_backward(weights, saved, grad_out):
    second_gain, second_bias, w_up, w_down = weights
    hidden_in, normed, upward, activated = saved
    grad_down = grad_out.astype(jnp.bfloat16)
    grad_w_down = collect(activated, grad_down)
    grad_activated = back_project(grad_down, w_down)
    _, pull_gelu = jax.vjp(lambda values: jax.nn.gelu(values, approximate=True), upward)
    grad_upward = pull_gelu(grad_activated)[0].astype(jnp.bfloat16)
    grad_w_up = collect(normed, grad_upward)
    grad_normed = back_project(grad_upward, w_up)
    _, pull_norm = jax.vjp(
        layer_norm, hidden_in, second_gain.astype(jnp.float32), second_bias.astype(jnp.float32)
    )
    grad_hidden, grad_gain, grad_bias = pull_norm(grad_normed)
    return (grad_out + grad_hidden, (grad_gain, grad_bias, grad_w_up, grad_w_down))


def attention_backward(weights, saved, grad_hidden, positions):
    first_gain, first_bias, w_query, w_key, w_value, w_gate, group_gain, w_output = weights
    (
        flat,
        normed,
        gate_pre,
        query_r,
        key_r,
        value_r,
        mixing,
        weighted_keys,
        query_entered,
        state_low,
        tables,
        retained,
        mixed,
    ) = saved
    mask, enter, leave, carry = tables
    rows = query_r.shape[0]
    grad_branch = grad_hidden.astype(jnp.bfloat16)
    grad_w_output = collect(mixed, grad_branch)
    grad_mixed = back_project(grad_branch, w_output)
    _, pull_gate = jax.vjp(norm_gate, retained, gate_pre, group_gain.astype(jnp.float32))
    grad_retained, grad_gate, grad_group = pull_gate(grad_mixed)
    grad_ret = to_heads(grad_retained.astype(jnp.bfloat16), rows, VH)
    grad_mixing = jnp.einsum(
        "rhce,rhse->rhcs", grad_ret, value_r, preferred_element_type=jnp.float32
    )
    grad_scores = (grad_mixing * mask).astype(jnp.bfloat16)
    grad_query = jnp.einsum(
        "rhcs,rhsd->rhcd", grad_scores, key_r, preferred_element_type=jnp.float32
    )
    grad_key = jnp.einsum(
        "rhcs,rhcd->rhsd", grad_scores, query_r, preferred_element_type=jnp.float32
    )
    grad_value = jnp.einsum("rhcs,rhce->rhse", mixing, grad_ret, preferred_element_type=jnp.float32)
    grad_query = (
        grad_query
        + jnp.einsum("rhce,rhde->rhcd", grad_ret, state_low, preferred_element_type=jnp.float32)
        * enter[..., None]
    )
    grad_state = jnp.einsum(
        "rhcd,rhce->rhde", query_entered, grad_ret, preferred_element_type=jnp.float32
    )
    summary_low = pass_states(carry, grad_state, True)
    grad_value = grad_value + jnp.einsum(
        "rhsd,rhde->rhse", weighted_keys, summary_low, preferred_element_type=jnp.float32
    )
    grad_key = (
        grad_key
        + jnp.einsum("rhse,rhde->rhsd", value_r, summary_low, preferred_element_type=jnp.float32)
        * leave[..., None]
    )
    grad_q = (
        unrotate(grad_query.transpose(0, 2, 1, 3), positions, 1.0)
        .reshape(-1, H * QK)
        .astype(jnp.bfloat16)
    )
    grad_k = (
        unrotate(grad_key.transpose(0, 2, 1, 3), positions, QK ** (-0.5))
        .reshape(-1, H * QK)
        .astype(jnp.bfloat16)
    )
    grad_v = from_heads(grad_value).astype(jnp.bfloat16)
    grad_g = grad_gate.astype(jnp.bfloat16)
    grad_normed = (
        back_project(grad_q, w_query)
        + back_project(grad_k, w_key)
        + back_project(grad_v, w_value)
        + back_project(grad_g, w_gate)
    )
    _, pull_norm = jax.vjp(
        layer_norm, flat, first_gain.astype(jnp.float32), first_bias.astype(jnp.float32)
    )
    grad_flat, grad_gain, grad_bias = pull_norm(grad_normed)
    grads = (
        grad_gain,
        grad_bias,
        collect(normed, grad_q),
        collect(normed, grad_k),
        collect(normed, grad_v),
        collect(normed, grad_g),
        grad_group,
        grad_w_output,
    )
    return (grad_hidden + grad_flat, grads)


def per_device(
    inputs,
    doc_flags,
    first_gain,
    first_bias,
    w_query,
    w_key,
    w_value,
    w_gate,
    group_gain,
    w_output,
    second_gain,
    second_bias,
    w_up,
    w_down,
    cotangent,
):
    batches, rows, length, width = inputs.shape
    positions = lax.axis_index("seq") * length + jnp.arange(length, dtype=jnp.int32)
    merged = inputs.reshape(batches * rows, length, width)
    flags = doc_flags.reshape(batches * rows, length)
    vectors = [first_gain, first_bias, group_gain, second_gain, second_bias]
    sizes = [vector.shape[0] for vector in vectors]
    edges = [sum(sizes[:k]) for k in range(len(sizes) + 1)]
    table = spread_vector(jnp.concatenate(vectors)[None])
    full = [table[:, a:b].reshape(-1) for a, b in zip(edges[:-1], edges[1:])]
    first_gain, first_bias, group_gain, second_gain, second_bias = full
    gathered = (
        first_gain,
        first_bias,
        spread(w_query),
        spread(w_key),
        spread(w_value),
        spread(w_gate),
        group_gain,
        spread(w_output),
    )
    hidden_in, attention_saved = attention_forward(gathered, merged, flags, positions)
    feeding = (second_gain, second_bias, spread(w_up), spread(w_down))
    train_output, feed_saved = feed_forward(feeding, hidden_in)
    grad_hidden, feed_parts = feed_backward(
        feeding, feed_saved, cotangent.reshape(-1, width).astype(jnp.float32)
    )
    grad_inputs, retention_parts = attention_backward(
        gathered, attention_saved, grad_hidden, positions
    )
    small = [retention_parts[0], retention_parts[1], retention_parts[6], feed_parts[0], feed_parts[1]]
    count = devices()
    summed = collect_vector(jnp.concatenate([part.reshape(count, -1) for part in small], axis=1))
    small = [summed[a:b] for a, b in zip(edges[:-1], edges[1:])]
    return (
        train_output.reshape(inputs.shape).astype(jnp.bfloat16),
        grad_inputs.reshape(inputs.shape),
        small[0],
        small[1],
        retention_parts[2],
        retention_parts[3],
        retention_parts[4],
        retention_parts[5],
        small[2],
        retention_parts[7],
        small[3],
        small[4],
        feed_parts[2],
        feed_parts[3],
    )


def solution(mesh):
    return jax.shard_map(
        per_device,
        mesh=mesh,
        in_specs=(
            P(None, "dp", "seq", None),
            P(None, "dp", "seq"),
            P(("dp", "seq")),
            P(("dp", "seq")),
            P(("dp", "seq"), None),
            P(("dp", "seq"), None),
            P(("dp", "seq"), None),
            P(("dp", "seq"), None),
            P(("dp", "seq")),
            P(("dp", "seq"), None),
            P(("dp", "seq")),
            P(("dp", "seq")),
            P(("dp", "seq"), None),
            P(("dp", "seq"), None),
            P(None, "dp", "seq", None),
        ),
        out_specs=(
            P(None, "dp", "seq", None),
            P(None, "dp", "seq", None),
            P(("dp", "seq")),
            P(("dp", "seq")),
            P(("dp", "seq"), None),
            P(("dp", "seq"), None),
            P(("dp", "seq"), None),
            P(("dp", "seq"), None),
            P(("dp", "seq")),
            P(("dp", "seq"), None),
            P(("dp", "seq")),
            P(("dp", "seq")),
            P(("dp", "seq"), None),
            P(("dp", "seq"), None),
        ),
        check_vma=False,
    )
```

```python
import functools

import jax
import jax.numpy as jnp
from jax import lax
from jax.experimental import pallas as pl
from jax.experimental.pallas import tpu as pltpu
from jax.sharding import PartitionSpec as P

H = 4
QK = 256
VH = 512
AXES = ("dp", "seq")
F32 = jnp.float32
BF16 = jnp.bfloat16
FAR = 4
VMEM = 56 * 1024 * 1024


def mm(left, right):
    return lax.dot_general(left, right, (((1,), (0,)), ((), ())), preferred_element_type=F32)


def nt(left, right):
    return lax.dot_general(left, right, (((1,), (1,)), ((), ())), preferred_element_type=F32)


def tn(left, right):
    return lax.dot_general(left, right, (((0,), (0,)), ((), ())), preferred_element_type=F32)


def devices():
    return lax.axis_size("dp") * lax.axis_size("seq")


def place():
    return lax.axis_index("dp") * lax.axis_size("seq") + lax.axis_index("seq")


def swap(values, bit):
    return lax.ppermute(values, AXES, [(i, i ^ bit) for i in range(devices())])


def upper_core():
    return lax.axis_index("seq") % 2 == 1


def orders():
    bits = [1 << k for k in range(1, devices().bit_length() - 1)]
    near = [bit for bit in bits if bit not in (2, FAR)] + [2]
    return [near[turn:] + near[:turn] for turn in range(3)]


def cut(width):
    tiles = width // 128
    third = tiles // 4
    first = (tiles - third + 1) // 2
    edges = [0, first * 128, (tiles - third) * 128, width]
    return list(zip(edges[:-1], edges[1:]))


def halves(values):
    half = values.shape[-1] // 2
    upper = upper_core()
    low, high = values[..., :half], values[..., half:]
    return jnp.where(upper, high, low), jnp.where(upper, low, high)


def ordered(mine, other, axis):
    upper = upper_core()
    return jnp.concatenate(
        [jnp.where(upper, other, mine), jnp.where(upper, mine, other)], axis=axis
    )


def settle(info, parts, cuts, held, width):
    chips = devices() // 2
    rows = parts[0].shape[1]

    def body(info_ref, *refs):
        sources, target = refs[:-1], refs[-1]
        me = info_ref[0]
        for turn, ((start, stop), bits) in enumerate(zip(cuts, held)):
            for far in range(chips):
                at = sum((1 << k) for k, bit in enumerate(bits[:-1]) if far & (bit >> 1))
                source = sources[2 * turn + (1 if far & (bits[-1] >> 1) else 0)]
                target[far ^ me, :, start:stop] = source[at]

    return pl.pallas_call(
        body,
        out_shape=jax.ShapeDtypeStruct((chips, rows, width), BF16),
        in_specs=[pl.BlockSpec(memory_space=pltpu.SMEM)]
        + [pl.BlockSpec(memory_space=pltpu.VMEM)] * len(parts),
        out_specs=pl.BlockSpec(memory_space=pltpu.VMEM),
        compiler_params=pltpu.CompilerParams(vmem_limit_bytes=20 * 1024 * 1024),
        cost_estimate=pl.CostEstimate(
            flops=0, bytes_accessed=4 * chips * rows * width, transcendentals=0
        ),
        name="settle",
    )(info, *parts)


def sync(*values):
    return lax.optimization_barrier(values)


def classes(piece, got):
    pair = jnp.stack([piece, got])
    return [pair[:, :, start:stop] for start, stop in cut(piece.shape[-1])]


def grow(parts, turn):
    return [swap(part, order[::-1][turn]) for part, order in zip(parts, orders())]


def join(parts, gots):
    return [jnp.concatenate([part, got], axis=0) for part, got in zip(parts, gots)]


def settled(info, parts, gots, width):
    held = [[FAR] + order[::-1] for order in orders()]
    both = [value for pair in zip(parts, gots) for value in pair]
    return settle(info, both, cut(width), held, width)


def total_of(mine, got):
    return mine.astype(F32) + got.astype(F32)


def split_first(own, got):
    chips, rows, width = own.shape
    levels = chips.bit_length() - 1
    dims = (2,) * levels + (rows, width)
    own, got = own.reshape(dims), got.reshape(dims)
    bits = [1 << k for k in range(levels, 0, -1)]
    return [
        (own[..., start:stop], got[..., start:stop], list(bits)) for start, stop in cut(width)
    ]


def shrink(parts, turn):
    after = []
    for (mine, theirs, bits), order in zip(parts, orders()):
        bit = order[turn]
        spot = bits.index(bit)

        def pick(values, side):
            return lax.index_in_dim(values, side, spot, False)

        send = total_of(pick(mine, 1), pick(theirs, 1)).astype(BF16)
        keep = total_of(pick(mine, 0), pick(theirs, 0)).astype(BF16)
        after.append((keep, swap(send, bit), [other for other in bits if other != bit]))
    return after


def shrink_far(parts):
    send = jnp.concatenate([total_of(m[1], t[1]).astype(BF16) for m, t, _ in parts], axis=1)
    mine = jnp.concatenate([total_of(m[0], t[0]) for m, t, _ in parts], axis=1)
    return mine, swap(send, FAR)


def hold(parts, *others):
    arrays = [(mine, theirs) for mine, theirs, _ in parts]
    arrays, others = lax.optimization_barrier((arrays, others))
    return ([(m, t, bits) for (m, t), (_, _, bits) in zip(arrays, parts)],) + tuple(others)


def finish_wide(values):
    rows = values.shape[0] // 2
    upper = upper_core()
    low, high = values[:rows], values[rows:]
    mine, give = jnp.where(upper, high, low), jnp.where(upper, low, high)
    return mine, swap(give, 1)


def finish_tall(values):
    half = values.shape[1] // 2
    upper = upper_core()
    low, high = values[:, :half], values[:, half:]
    mine, give = jnp.where(upper, high, low), jnp.where(upper, low, high)
    return ordered(mine, swap(give, 1), 1)


def begin_states(carry, near_carry, own, near, reverse):
    upper = upper_core()
    turned = jnp.logical_not(upper) if reverse else upper
    first_carry = jnp.where(turned, near_carry, carry)[:, :, None, None]
    last_carry = jnp.where(turned, carry, near_carry)[:, :, None, None]
    first = jnp.where(turned, near, own)
    last = jnp.where(turned, own, near)
    joined = last_carry * first + last
    both = first_carry * last_carry
    rows = own.shape[1]
    entering = [jnp.zeros_like(joined[:, 0]) for _ in range(rows)]
    return (turned, first_carry, first, joined, both, entering)


def hop(states, phase, reverse):
    turned, first_carry, first, joined, both, entering = states
    chips = lax.axis_size("seq") // 2
    arrived = []
    for row in range(len(entering)):
        step = phase - row
        if not 1 <= step < chips:
            arrived.append(None)
            continue
        message = (joined[:, row] + both[:, row] * entering[row]).astype(BF16)
        source, target = (step - 1, step) if not reverse else (chips - step, chips - step - 1)
        pairs = [(2 * source + core, 2 * target + core) for core in range(2)]
        arrived.append(lax.ppermute(message, "seq", pairs))
    return arrived


def land(states, arrived):
    turned, first_carry, first, joined, both, entering = states
    entering = [
        e if a is None else e + a.astype(F32)
        for e, a in zip(entering, arrived)
    ]
    return (turned, first_carry, first, joined, both, entering)


def end_states(states):
    turned, first_carry, first, joined, both, entering = states
    entering = jnp.stack(entering, axis=1)
    middle = (first_carry * entering + first).astype(BF16)
    entering = entering.astype(BF16)
    mine = jnp.where(turned, middle, entering)
    theirs = swap(jnp.where(turned, entering, middle), 1)
    return mine, theirs


def call(body, grid, info, ins, outs, scratch, flops, name):
    def spec(block, index):
        if block is None:
            return pl.BlockSpec(memory_space=pltpu.SMEM)
        return pl.BlockSpec(block, index)

    moved = sum(a.size * a.dtype.itemsize for a, _, _ in ins)
    for shape, dtype, _, _ in outs:
        size = jnp.dtype(dtype).itemsize
        for extent in shape:
            size *= extent
        moved += size
    return pl.pallas_call(
        body,
        grid_spec=pltpu.PrefetchScalarGridSpec(
            num_scalar_prefetch=1,
            grid=(grid,),
            in_specs=[spec(block, index) for _, block, index in ins],
            out_specs=[spec(block, index) for _, _, block, index in outs],
            scratch_shapes=scratch,
        ),
        out_shape=[jax.ShapeDtypeStruct(shape, dtype) for shape, dtype, _, _ in outs],
        compiler_params=pltpu.CompilerParams(
            vmem_limit_bytes=VMEM, dimension_semantics=("arbitrary",)
        ),
        cost_estimate=pl.CostEstimate(flops=int(flops), bytes_accessed=int(moved), transcendentals=0),
        name=name,
    )(info, *[a for a, _, _ in ins])


def whole(array):
    zeros = (0,) * array.ndim
    return (array, array.shape, lambda h, info: zeros)


def whole_out(shape, dtype):
    zeros = (0,) * len(shape)
    return (shape, dtype, shape, lambda h, info: zeros)


def head_in(array):
    rest = (0,) * (array.ndim - 1)
    return (array, (1,) + array.shape[1:], lambda h, info: (h,) + rest)


def head_out(shape, dtype):
    rest = (0,) * (len(shape) - 1)
    return (shape, dtype, (1,) + shape[1:], lambda h, info: (h,) + rest)


def own_in(array):
    rest = (0,) * (array.ndim - 1)
    return (array, (1,) + array.shape[1:], lambda h, info: (jnp.minimum(h, 1),) + rest)


def other_in(array):
    rest = (0,) * (array.ndim - 1)
    return (array, (1,) + array.shape[1:], lambda h, info: (jnp.maximum(h - 2, 0),) + rest)


def own_out(shape, dtype):
    rest = (0,) * (len(shape) - 1)
    return (shape, dtype, (1,) + shape[1:], lambda h, info: (jnp.minimum(h, 1),) + rest)


def other_out(shape, dtype):
    rest = (0,) * (len(shape) - 1)
    return (shape, dtype, (1,) + shape[1:], lambda h, info: (jnp.maximum(h - 2, 0),) + rest)


def real(h, info):
    return lax.rem(h + 2 * info[1], 4)


def real_in(array):
    rest = (0,) * (array.ndim - 1)
    return (array, (1,) + array.shape[1:], lambda h, info: (real(h, info),) + rest)


def columns(array, width, first, own):
    block = array.shape[:2] + (width,)
    if own:
        return (array, block, lambda h, info: (0, 0, first + jnp.minimum(h, 1)))
    return (array, block, lambda h, info: (0, 0, first + jnp.maximum(h - 2, 0)))


def tall(array):
    block = (array.shape[0] // 4, array.shape[1], 1024)
    return (array, block, lambda h, info: (real(h, info), 0, 1))


def tall_rows(ref):
    chips = ref.shape[0]
    pieces = []
    for chip in range(chips):
        pieces += [ref[chip, :, :512], ref[chip, :, 512:]]
    return jnp.concatenate(pieces, axis=0)


def flat(ref):
    chips, rows, width = ref.shape
    return ref[...].reshape(chips * rows, width)


def side(info, own):
    return pl.multiple_of(512 * (info[1] if own else 1 - info[1]), 512)


def put_wide(target, info, values, start):
    chips, rows, _ = target.shape
    width = values.shape[1]
    values = values.astype(BF16)
    for chip in range(chips):
        target[chip ^ info[0], :, start : start + width] = values[chip * rows : (chip + 1) * rows]


def put_tall(target, info, values, block, start):
    chips, rows, _ = target.shape
    values = values.astype(BF16)
    share = chips // 4
    for chip in range(share):
        at = (block * share + chip) ^ info[0]
        base = 2 * rows * chip
        target[at, :, start : start + 512] = values[base : base + rows]
        target[at, :, start + 512 : start + 1024] = values[base + rows : base + 2 * rows]


def rotated(values, cosine, sine):
    a, b = values[:, :128], values[:, 128:]
    return jnp.concatenate([a * cosine - b * sine, b * cosine + a * sine], axis=1)


def unrotated(values, cosine, sine):
    a, b = values[:, :128], values[:, 128:]
    return jnp.concatenate([a * cosine + b * sine, b * cosine - a * sine], axis=1)


def mask_of(rate, tall_count, wide_count):
    length = tall_count.shape[0]
    i = lax.broadcasted_iota(jnp.int32, (length, length), 0)
    s = lax.broadcasted_iota(jnp.int32, (length, length), 1)
    decay = jnp.exp((i - s).astype(F32) * rate)
    return jnp.where((tall_count == wide_count) & (i >= s), decay, 0.0)


def enter_of(rate, tall_count):
    i = lax.broadcasted_iota(jnp.int32, tall_count.shape, 0)
    return jnp.where(tall_count == 0, jnp.exp((i + 1).astype(F32) * rate), 0.0)


def leave_of(rate, tall_count):
    length = tall_count.shape[0]
    i = lax.broadcasted_iota(jnp.int32, tall_count.shape, 0)
    last = tall_count[length - 1 :, :]
    return jnp.where(tall_count == last, jnp.exp((length - 1 - i).astype(F32) * rate), 0.0)


def norm_parts(values, eps):
    average = jnp.mean(values, axis=-1, keepdims=True)
    centred = values - average
    spread_ = jnp.mean(centred * centred, axis=-1, keepdims=True)
    scale = lax.rsqrt(spread_ + eps)
    return centred * scale, scale


def norm_back(grad, normal, scale):
    first = jnp.mean(grad, axis=-1, keepdims=True)
    second = jnp.mean(grad * normal, axis=-1, keepdims=True)
    return scale * (grad - first - normal * second)


CHUNK = 64


def norm_kernel(info, x, gain, bias, normed, normed_t):
    @pl.loop(0, x.shape[0] // CHUNK)
    def _(k):
        at = pl.ds(pl.multiple_of(k * CHUNK, CHUNK), CHUNK)
        normal, _ = norm_parts(x[at, :].astype(F32), 1e-05)
        normed[at, :] = (normal * gain[...].astype(F32) + bias[...].astype(F32)).astype(BF16)

    normed_t[...] = normed[...].T


def project_kernel(
    info, rates, normed, cosine, sine, tall_count, wide_count,
    q_own, k_own, v_own, q_oth, k_oth, v_oth,
    q_out, k_out, v_out, mix_out, inner_out, sum_own, sum_oth, pre,
):
    h = pl.program_id(0)

    def fill(wq, wk, wv):
        left = normed[...]
        pre[:, :256] = mm(left, flat(wq))
        pre[:, 256:512] = mm(left, flat(wk))
        pre[:, 512:] = mm(left, flat(wv))

    @pl.when(h < 2)
    def _():
        fill(q_own, k_own, v_own)

    @pl.when(h >= 2)
    def _():
        fill(q_oth, k_oth, v_oth)

    rate = rates[h]
    length = cosine.shape[0]
    for row in range(tall_count.shape[0]):
        at = slice(row * length, (row + 1) * length)
        count = tall_count[row]
        query = rotated(pre[at, :256], cosine[...], sine[...]).astype(BF16)
        key = (rotated(pre[at, 256:512], cosine[...], sine[...]) * QK**-0.5).astype(BF16)
        value = pre[at, 512:].astype(BF16)
        q_out[0, at] = query
        k_out[0, at] = key
        v_out[0, at] = value
        mixing = (nt(query, key) * mask_of(rate, count, wide_count[row])).astype(BF16)
        mix_out[0, at] = mixing
        inner_out[0, at] = mm(mixing, value)
        weighted = (key.astype(F32) * leave_of(rate, count)).astype(BF16)
        summary = tn(weighted, value)

        @pl.when(h < 2)
        def _():
            sum_own[0, row] = summary

        @pl.when(h >= 2)
        def _():
            sum_oth[0, row] = summary


def gate_kernel(info, normed, own, oth, out):
    h = pl.program_id(0)

    @pl.when(h < 2)
    def _():
        out[0] = mm(normed[...], flat(own))

    @pl.when(h >= 2)
    def _():
        out[0] = mm(normed[...], flat(oth))


def mix_kernel(
    info, rates, x, gain, second_gain, second_bias, tall_count, query, inner, gate,
    state_own, state_oth, wo_own, wo_oth,
    retained, mixed_t, hidden, normed, normed_t,
):
    h = pl.program_id(0)
    rate = rates[h]
    length = tall_count.shape[1]

    @pl.when(h == 0)
    def _():
        hidden[...] = x[...].astype(F32)

    for row in range(tall_count.shape[0]):
        at = slice(row * length, (row + 1) * length)
        entered = (query[0, at].astype(F32) * enter_of(rate, tall_count[row])).astype(BF16)

        @pl.when(h < 2)
        def _():
            retained[0, at] = inner[0, at] + mm(entered, state_own[0, row])

        @pl.when(h >= 2)
        def _():
            retained[0, at] = inner[0, at] + mm(entered, state_oth[0, row])

    normal, _ = norm_parts(retained[0], 1.0)
    pre = gate[0]
    mixed = (pre / (1.0 + jnp.exp(-pre)) * (normal * gain[0].astype(F32))).astype(BF16)
    mixed_t[0] = mixed.T
    hidden[:, pl.ds(side(info, True), 512)] += mm(mixed, tall_rows(wo_own))
    hidden[:, pl.ds(side(info, False), 512)] += mm(mixed, tall_rows(wo_oth))

    @pl.when(h == 3)
    def _():
        @pl.loop(0, x.shape[0] // CHUNK)
        def _(k):
            at = pl.ds(pl.multiple_of(k * CHUNK, CHUNK), CHUNK)
            normal, _ = norm_parts(hidden[at, :], 1e-05)
            normed[at, :] = (
                normal * second_gain[...].astype(F32) + second_bias[...].astype(F32)
            ).astype(BF16)

        normed_t[...] = normed[...].T


def feed_kernel(
    info, hidden, normed, normed_t, cot, second_gain,
    up_own, up_oth, down_own, down_oth,
    output, grad_hidden, grad_low, grad_gain, grad_bias, g_own, g_oth,
    upward, out_sum, norm_sum,
):
    f = pl.program_id(0)
    own_at = pl.ds(side(info, True), 512)
    oth_at = pl.ds(side(info, False), 512)

    @pl.when(f == 0)
    def _():
        out_sum[...] = hidden[...]
        norm_sum[...] = jnp.zeros_like(norm_sum)

    @pl.when(f < 2)
    def _():
        upward[...] = mm(normed[...], flat(up_own))

    @pl.when(f >= 2)
    def _():
        upward[...] = mm(normed[...], flat(up_oth))

    up = upward[...]
    root = 0.7978845608028654
    squared = up * up
    bent = jnp.tanh(root * (up + 0.044715 * (squared * up)))
    activated = (0.5 * up * (1.0 + bent)).astype(BF16)
    slope = 0.5 * (1.0 + bent) + 0.5 * up * (1.0 - bent * bent) * (
        root * (1.0 + 3 * 0.044715 * squared)
    )
    own, oth = tall_rows(down_own), tall_rows(down_oth)
    out_sum[:, own_at] += mm(activated, own)
    out_sum[:, oth_at] += mm(activated, oth)
    grad_up = (slope * (nt(cot[:, own_at], own) + nt(cot[:, oth_at], oth))).astype(BF16)
    block = real(f, info)
    act_t = activated.T
    put_tall(g_own, info, mm(act_t, cot[:, own_at]), block, 1024)
    put_tall(g_oth, info, mm(act_t, cot[:, oth_at]), block, 1024)
    grad_w = mm(normed_t[...], grad_up)
    for step in range(4):

        @pl.when(f == step)
        def _():
            put_wide(g_own if step < 2 else g_oth, info, grad_w, 512 * (step % 2))

    @pl.when(f < 2)
    def _():
        norm_sum[...] += nt(grad_up, flat(up_own))

    @pl.when(f >= 2)
    def _():
        norm_sum[...] += nt(grad_up, flat(up_oth))

    @pl.when(f == 3)
    def _():
        grad_gain[...] = jnp.zeros_like(grad_gain)
        grad_bias[...] = jnp.zeros_like(grad_bias)

        @pl.loop(0, hidden.shape[0] // CHUNK)
        def _(k):
            at = pl.ds(pl.multiple_of(k * CHUNK, CHUNK), CHUNK)
            output[at, :] = out_sum[at, :].astype(BF16)
            normal, scale = norm_parts(hidden[at, :], 1e-05)
            grad = norm_sum[at, :]
            grad_gain[...] += jnp.sum(grad * normal, axis=0, keepdims=True)
            grad_bias[...] += jnp.sum(grad, axis=0, keepdims=True)
            total = cot[at, :].astype(F32) + norm_back(
                grad * second_gain[...].astype(F32), normal, scale
            )
            grad_hidden[at, :] = total
            grad_low[at, :] = total.astype(BF16)


def unmix_kernel(
    info, rates, grad_low, gain, tall_count, query, retained, gate, wo_own, wo_oth,
    grad_ret, grad_gate, grad_gain, state_own, state_oth,
):
    h = pl.program_id(0)
    rate = rates[h]
    length = tall_count.shape[1]
    grad = nt(grad_low[:, pl.ds(side(info, True), 512)], tall_rows(wo_own)) + nt(
        grad_low[:, pl.ds(side(info, False), 512)], tall_rows(wo_oth)
    )
    normal, scale = norm_parts(retained[0], 1.0)
    pre = gate[0]
    share = 1.0 / (1.0 + jnp.exp(-pre))
    curve = pre * share
    scaled = gain[0].astype(F32)
    grad_gate[0] = (grad * (normal * scaled) * (share * (1.0 + pre * (1.0 - share)))).astype(BF16)
    grad_normal = grad * curve
    grad_gain[0] = jnp.sum(grad_normal * normal, axis=0, keepdims=True)
    grad_ret[0] = norm_back(grad_normal * scaled, normal, scale).astype(BF16)
    for row in range(tall_count.shape[0]):
        at = slice(row * length, (row + 1) * length)
        entered = (query[0, at].astype(F32) * enter_of(rate, tall_count[row])).astype(BF16)
        state = tn(entered, grad_ret[0, at])

        @pl.when(h < 2)
        def _():
            state_own[0, row] = state

        @pl.when(h >= 2)
        def _():
            state_oth[0, row] = state


def outer_kernel(
    info, grad_low, normed_t, mixed_t, grad_gate, g_own, g_oth,
    norm_part, out_own, out_oth,
):
    h = pl.program_id(0)

    @pl.when(h == 0)
    def _():
        norm_part[...] = jnp.zeros_like(norm_part)

    block = real(h, info)
    left = mixed_t[0]
    put_tall(out_own, info, mm(left, grad_low[:, pl.ds(side(info, True), 512)]), block, 1024)
    put_tall(out_oth, info, mm(left, grad_low[:, pl.ds(side(info, False), 512)]), block, 1024)
    grad_wg = mm(normed_t[...], grad_gate[0])
    for step in range(4):

        @pl.when(h == step)
        def _():
            put_wide(out_own if step < 2 else out_oth, info, grad_wg, 512 * (step % 2))

    @pl.when(h < 2)
    def _():
        norm_part[...] += nt(grad_gate[0], flat(g_own))

    @pl.when(h >= 2)
    def _():
        norm_part[...] += nt(grad_gate[0], flat(g_oth))


def inside_kernel(
    info, rates, normed_t, grad_ret, query, key, value, mixing,
    cosine, sine, tall_count, wide_count, state_own, state_oth,
    q_own, q_oth, norm_before,
    key_part, value_part, norm_part, out_own, out_oth,
    grad_q,
):
    h = pl.program_id(0)
    rate = rates[h]
    length = cosine.shape[0]

    @pl.when(h == 0)
    def _():
        norm_part[...] = norm_before[...]

    for row in range(tall_count.shape[0]):
        at = slice(row * length, (row + 1) * length)
        grad = grad_ret[0, at]
        mask = mask_of(rate, tall_count[row], wide_count[row])
        scores = (nt(grad, value[0, at]) * mask).astype(BF16)
        enter = enter_of(rate, tall_count[row])

        def set_query(state):
            total = mm(scores, key[0, at]) + nt(grad, state[0, row]) * enter
            grad_q[at, :] = unrotated(total, cosine[...], sine[...]).astype(BF16)

        @pl.when(h < 2)
        def _():
            set_query(state_own)

        @pl.when(h >= 2)
        def _():
            set_query(state_oth)

        key_part[0, at] = tn(scores, query[0, at])
        value_part[0, at] = tn(mixing[0, at], grad)

    grad_wq = mm(normed_t[...], grad_q[...])
    for step in range(4):

        @pl.when(h == step)
        def _():
            put_wide(out_own if step < 2 else out_oth, info, grad_wq, 256 * (step % 2))

    @pl.when(h < 2)
    def _():
        norm_part[...] += nt(grad_q[...], flat(q_own))

    @pl.when(h >= 2)
    def _():
        norm_part[...] += nt(grad_q[...], flat(q_oth))


def last_kernel(
    info, rates, normed_t, key, value, key_part, value_part, cosine, sine, tall_count,
    state_own, state_oth,
    grad_k, grad_v, out_own, out_oth,
):
    h = pl.program_id(0)
    rate = rates[h]
    length = cosine.shape[0]
    for row in range(tall_count.shape[0]):
        at = slice(row * length, (row + 1) * length)
        leave = leave_of(rate, tall_count[row])
        weighted = (key[0, at].astype(F32) * leave).astype(BF16)

        def set_both(state):
            low = state[0, row]
            grad_v[0, at] = (value_part[0, at] + mm(weighted, low)).astype(BF16)
            total = key_part[0, at] + nt(value[0, at], low) * leave
            grad_k[0, at] = (unrotated(total, cosine[...], sine[...]) * QK**-0.5).astype(BF16)

        @pl.when(h < 2)
        def _():
            set_both(state_own)

        @pl.when(h >= 2)
        def _():
            set_both(state_oth)

    grad_wk = mm(normed_t[...], grad_k[0])
    grad_wv = mm(normed_t[...], grad_v[0])
    for step in range(4):

        @pl.when(h == step)
        def _():
            target = out_own if step < 2 else out_oth
            put_wide(target, info, grad_wk, 256 * (step % 2))
            put_wide(target, info, grad_wv, 512 + 512 * (step % 2))


def input_kernel(
    info, x, gain, grad_hidden, norm_part, grad_k, grad_v, k_own, k_oth, v_own, v_oth,
    input_grad, grad_gain, grad_bias, norm_sum,
):
    h = pl.program_id(0)

    @pl.when(h == 0)
    def _():
        norm_sum[...] = norm_part[...]

    @pl.when(h < 2)
    def _():
        norm_sum[...] += nt(grad_k[0], flat(k_own)) + nt(grad_v[0], flat(v_own))

    @pl.when(h >= 2)
    def _():
        norm_sum[...] += nt(grad_k[0], flat(k_oth)) + nt(grad_v[0], flat(v_oth))

    @pl.when(h == 3)
    def _():
        grad_gain[...] = jnp.zeros_like(grad_gain)
        grad_bias[...] = jnp.zeros_like(grad_bias)

        @pl.loop(0, x.shape[0] // CHUNK)
        def _(k):
            at = pl.ds(pl.multiple_of(k * CHUNK, CHUNK), CHUNK)
            normal, scale = norm_parts(x[at, :].astype(F32), 1e-05)
            grad = norm_sum[at, :]
            grad_gain[...] += jnp.sum(grad * normal, axis=0, keepdims=True)
            grad_bias[...] += jnp.sum(grad, axis=0, keepdims=True)
            input_grad[at, :] = grad_hidden[at, :] + norm_back(
                grad * gain[...].astype(F32), normal, scale
            )


def per_device(
    inputs,
    doc_flags,
    first_gain,
    first_bias,
    w_query,
    w_key,
    w_value,
    w_gate,
    group_gain,
    w_output,
    second_gain,
    second_bias,
    w_up,
    w_down,
    cotangent,
):
    batches, row_count, length, width = inputs.shape
    rows = batches * row_count
    tokens = rows * length
    count = devices()
    chips = count // 2
    core = lax.axis_index("seq") % 2
    info = jnp.stack([place() // 2, core]).astype(jnp.int32)
    x = inputs.reshape(tokens, width)
    cot = cotangent.reshape(tokens, width)

    share = w_query.shape[0]
    upper = upper_core()

    def rows_of(values):
        return values.reshape(1, -1)

    def both_cores(keep, got, axis):
        return jnp.concatenate(
            [jnp.where(upper, got, keep), jnp.where(upper, keep, got)], axis=axis
        )

    def top_piece(*weights):
        pairs = [halves(w) for w in weights]
        keep = jnp.concatenate([a for a, _ in pairs], axis=1)
        got = swap(jnp.concatenate([b for _, b in pairs], axis=1), 1)
        return both_cores(keep, got, 0)

    def side_piece(weight):
        keep, give = halves(weight)
        return both_cores(keep, swap(give, 1), 1)

    vectors = [first_gain, first_bias, second_gain, second_bias, group_gain]
    vector = jnp.concatenate(vectors)[None]
    sizes = [v.shape[0] for v in vectors]
    edges = [sum(sizes[:k]) for k in range(len(sizes) + 1)]
    vector = jnp.concatenate([vector, jnp.zeros((15, vector.shape[1]), BF16)], axis=0)

    qkv = top_piece(w_query, w_key, w_value)
    go = jnp.concatenate([top_piece(w_gate), side_piece(w_output)], axis=1)
    ff = jnp.concatenate([top_piece(w_up), side_piece(w_down)], axis=1)
    got_qkv = swap(qkv, FAR)
    table = vector[None]
    for bit in [1 << k for k in range(count.bit_length() - 1)]:
        table = both_cores(table, swap(table, bit), 0) if bit == 1 else jnp.concatenate(
            [
                jnp.where((place() // bit) % 2 == 1, swapped, table)
                if first
                else jnp.where((place() // bit) % 2 == 1, table, swapped)
                for swapped in [swap(table, bit)]
                for first in (True, False)
            ],
            axis=0,
        )
    table = table[:, 0]
    first_gain, first_bias, second_gain, second_bias, group_gain = [
        table[:, a:b].reshape(1, -1) for a, b in zip(edges[:-1], edges[1:])
    ]
    group_gain = group_gain.reshape(H, 1, VH)

    positions = lax.axis_index("seq") * length + jnp.arange(length, dtype=jnp.int32)
    frequency = 10000.0 ** (-jnp.arange(QK // 2, dtype=F32) / (QK // 2))
    angles = positions.astype(F32)[:, None] * frequency[None, :]
    cosine, sine = jnp.cos(angles), jnp.sin(angles)
    rates = jnp.log1p(-(2.0 ** (-5.0 - 3.0 * jnp.arange(H, dtype=F32))))
    rates = jnp.where(upper, jnp.roll(rates, 2), rates)
    counts = jnp.cumsum(doc_flags.reshape(rows, length), axis=-1, dtype=jnp.int32)
    tall_count, wide_count = counts[:, :, None], counts[:, None, :]
    open_row = (counts[:, -1] == 0).astype(F32)
    near_row = swap(open_row, 1)
    decay = jnp.exp(rates[:2] * float(length))
    carry, near_carry = decay[:, None] * open_row[None], decay[:, None] * near_row[None]

    per_head = (H, tokens)
    state_shape = (2, rows, QK, VH)
    grad_shape = (chips, 2 * share)
    rates_in = (rates, None, None)
    unit = 2.0 * tokens * width * 512

    got_qkv, go, ff, gains, tables = sync(
        got_qkv, go, ff, (first_gain, first_bias, second_gain, second_bias, group_gain),
        (cosine, sine, tall_count, wide_count, carry, near_carry),
    )
    first_gain, first_bias, second_gain, second_bias, group_gain = gains
    cosine, sine, tall_count, wide_count, carry, near_carry = tables
    qkv_parts = classes(qkv, got_qkv)
    qkv_gots = grow(qkv_parts, 0)
    qkv_parts, qkv_gots, go = sync(qkv_parts, qkv_gots, go)
    qkv_parts = join(qkv_parts, qkv_gots)
    qkv_gots = grow(qkv_parts, 1)
    got_go = swap(go, FAR)
    qkv_parts, qkv_gots, got_go, go, ff = sync(qkv_parts, qkv_gots, got_go, go, ff)
    levels = len(orders()[0])
    for turn in range(2, levels - 1):
        qkv_parts = join(qkv_parts, qkv_gots)
        qkv_gots = grow(qkv_parts, turn)
        qkv_parts, qkv_gots = sync(qkv_parts, qkv_gots)
    qkv_parts = join(qkv_parts, qkv_gots)
    qkv_gots = grow(qkv_parts, levels - 1)
    go_parts = classes(go, got_go)
    go_gots = grow(go_parts, 0)
    got_ff = swap(ff, FAR)
    normed, normed_t = call(
        norm_kernel,
        1,
        info,
        [whole(x), whole(first_gain), whole(first_bias)],
        [whole_out((tokens, width), BF16), whole_out((width, tokens), BF16)],
        [],
        unit / 100,
        "norm",
    )
    qkv_parts, qkv_gots, go_parts, go_gots, got_ff, ff, normed, normed_t = sync(
        qkv_parts, qkv_gots, go_parts, go_gots, got_ff, ff, normed, normed_t
    )

    qkv_own = settled(info, qkv_parts, qkv_gots, 2048)
    qkv_oth = swap(qkv_own, 1)
    for turn in range(1, levels - 2):
        go_parts = join(go_parts, go_gots)
        go_gots = grow(go_parts, turn)
        go_parts, go_gots = sync(go_parts, go_gots)
    go_parts = join(go_parts, go_gots)
    go_gots = grow(go_parts, levels - 2)
    ff_parts = classes(ff, got_ff)
    ff_gots = grow(ff_parts, 0)
    (query, key, value, mixing, inner, sum_own, sum_oth) = call(
        project_kernel,
        H,
        info,
        [
            rates_in, whole(normed), whole(cosine), whole(sine),
            whole(tall_count), whole(wide_count),
            columns(qkv_own, 256, 0, True), columns(qkv_own, 256, 2, True),
            columns(qkv_own, 512, 2, True),
            columns(qkv_oth, 256, 0, False), columns(qkv_oth, 256, 2, False),
            columns(qkv_oth, 512, 2, False),
        ],
        [
            head_out(per_head + (QK,), BF16), head_out(per_head + (QK,), BF16),
            head_out(per_head + (VH,), BF16), head_out(per_head + (length,), BF16),
            head_out(per_head + (VH,), F32),
            own_out(state_shape, F32), other_out(state_shape, F32),
        ],
        [pltpu.VMEM((tokens, 1024), F32)],
        10 * unit,
        "project",
    )
    sum_near = swap(sum_oth, 1)
    go_parts, go_gots, ff_parts, ff_gots, sum_own, sum_near = sync(
        go_parts, go_gots, ff_parts, ff_gots, sum_own, sum_near
    )

    states = begin_states(carry, near_carry, sum_own, sum_near, False)
    arrived = hop(states, 1, False)
    go_parts = join(go_parts, go_gots)
    go_gots = grow(go_parts, levels - 1)
    for turn in range(1, levels - 2):
        ff_parts = join(ff_parts, ff_gots)
        ff_gots = grow(ff_parts, turn)
        ff_parts, ff_gots = sync(ff_parts, ff_gots)
    states, arrived, go_parts, go_gots = sync(states, arrived, go_parts, go_gots)
    states = land(states, arrived)

    arrived = hop(states, 2, False)
    go_own = settled(info, go_parts, go_gots, 2048)
    go_oth = swap(go_own, 1)
    ff_parts = join(ff_parts, ff_gots)
    ff_gots = grow(ff_parts, levels - 2)
    states, arrived, go_own, go_oth, ff_parts, ff_gots = sync(
        states, arrived, go_own, go_oth, ff_parts, ff_gots
    )
    states = land(states, arrived)

    arrived = hop(states, 3, False)
    ff_parts = join(ff_parts, ff_gots)
    ff_gots = grow(ff_parts, levels - 1)
    (gate,) = call(
        gate_kernel,
        H,
        info,
        [whole(normed), columns(go_own, 512, 0, True), columns(go_oth, 512, 0, False)],
        [head_out(per_head + (VH,), F32)],
        [],
        4 * unit,
        "gate",
    )
    states, arrived, gate, ff_parts, ff_gots = sync(states, arrived, gate, ff_parts, ff_gots)
    states = land(states, arrived)

    phases = lax.axis_size("seq") // 2 - 1 + rows - 1
    ff_own = settled(info, ff_parts, ff_gots, 2048)
    ff_oth = swap(ff_own, 1)
    for phase in range(4, phases + 1):
        arrived = hop(states, phase, False)
        states, arrived = sync(states, arrived)
        states = land(states, arrived)
    state_own, state_oth = end_states(states)

    retained, mixed_t, hidden, normed_second, normed_second_t = call(
        mix_kernel,
        H,
        info,
        [
            rates_in, whole(x), real_in(group_gain), whole(second_gain), whole(second_bias),
            whole(tall_count), head_in(query), head_in(inner), head_in(gate),
            own_in(state_own), other_in(state_oth), tall(go_own), tall(go_oth),
        ],
        [
            head_out(per_head + (VH,), F32), head_out((H, VH, tokens), BF16),
            whole_out((tokens, width), F32), whole_out((tokens, width), BF16),
            whole_out((width, tokens), BF16),
        ],
        [],
        5 * unit,
        "mix",
    )
    output, grad_hidden, grad_low, grad_second_gain, grad_second_bias, ff_g_own, ff_g_oth = call(
        feed_kernel,
        4,
        info,
        [
            whole(hidden), whole(normed_second), whole(normed_second_t), whole(cot),
            whole(second_gain),
            columns(ff_own, 512, 0, True), columns(ff_oth, 512, 0, False),
            tall(ff_own), tall(ff_oth),
        ],
        [
            whole_out((tokens, width), BF16), whole_out((tokens, width), F32),
            whole_out((tokens, width), BF16), whole_out((1, width), F32),
            whole_out((1, width), F32),
            whole_out(grad_shape + (2048,), BF16), whole_out(grad_shape + (2048,), BF16),
        ],
        [
            pltpu.VMEM((tokens, 512), F32), pltpu.VMEM((tokens, width), F32),
            pltpu.VMEM((tokens, width), F32),
        ],
        24 * unit,
        "feed",
    )

    ff_g_got = swap(ff_g_oth, 1)
    grad_ret, grad_gate, grad_group_gain, gstate_own, gstate_oth = call(
        unmix_kernel,
        H,
        info,
        [
            rates_in, whole(grad_low), real_in(group_gain), whole(tall_count), head_in(query),
            head_in(retained), head_in(gate), tall(go_own), tall(go_oth),
        ],
        [
            head_out(per_head + (VH,), BF16), head_out(per_head + (VH,), BF16),
            (
                (H, 1, VH), F32, (1, 1, VH),
                lambda h, info: (real(h, info), 0, 0),
            ),
            own_out(state_shape, F32), other_out(state_shape, F32),
        ],
        [],
        5 * unit,
        "unmix",
    )
    gstate_near = swap(gstate_oth, 1)
    gstate_own, gstate_near, ff_g_own, ff_g_got, grad_gate, grad_ret = sync(
        gstate_own, gstate_near, ff_g_own, ff_g_got, grad_gate, grad_ret
    )

    states = begin_states(carry, near_carry, gstate_own, gstate_near, True)
    arrived = hop(states, 1, True)
    ff_sums = shrink(split_first(ff_g_own, ff_g_got), 0)
    norm_part, go_g_own, go_g_oth = call(
        outer_kernel,
        H,
        info,
        [
            whole(grad_low), whole(normed_t), head_in(mixed_t), head_in(grad_gate),
            columns(go_own, 512, 0, True), columns(go_oth, 512, 0, False),
        ],
        [
            whole_out((tokens, width), F32),
            whole_out(grad_shape + (2048,), BF16), whole_out(grad_shape + (2048,), BF16),
        ],
        [],
        12 * unit,
        "outer",
    )
    ff_sums, states, arrived, norm_part, go_g_own, go_g_oth = hold(
        ff_sums, states, arrived, norm_part, go_g_own, go_g_oth
    )
    states = land(states, arrived)

    arrived = hop(states, 2, True)
    ff_sums = shrink(ff_sums, 1)
    key_part, value_part, norm_part, q_g_own, q_g_oth = call(
        inside_kernel,
        H,
        info,
        [
            rates_in, whole(normed_t), head_in(grad_ret),
            head_in(query), head_in(key), head_in(value), head_in(mixing),
            whole(cosine), whole(sine), whole(tall_count), whole(wide_count),
            own_in(state_own), other_in(state_oth),
            columns(qkv_own, 256, 0, True), columns(qkv_oth, 256, 0, False), whole(norm_part),
        ],
        [
            head_out(per_head + (QK,), F32), head_out(per_head + (VH,), F32),
            whole_out((tokens, width), F32),
            whole_out(grad_shape + (512,), BF16), whole_out(grad_shape + (512,), BF16),
        ],
        [pltpu.VMEM((tokens, QK), BF16)],
        7 * unit,
        "inside",
    )
    go_g_own = jnp.concatenate([go_g_own, q_g_own], axis=2)
    go_g_oth = jnp.concatenate([go_g_oth, q_g_oth], axis=2)
    ff_sums, states, arrived, key_part, value_part, norm_part, go_g_own, go_g_oth = hold(
        ff_sums, states, arrived, key_part, value_part, norm_part, go_g_own, go_g_oth
    )
    states = land(states, arrived)

    arrived = hop(states, 3, True)
    go_g_got = swap(go_g_oth, 1)
    for turn in range(2, levels):
        ff_sums = shrink(ff_sums, turn)
    ff_sums, states, arrived, go_g_own, go_g_got = hold(
        ff_sums, states, arrived, go_g_own, go_g_got
    )
    states = land(states, arrived)

    ff_far = shrink_far(ff_sums)
    go_sums = shrink(split_first(go_g_own, go_g_got), 0)
    for phase in range(4, phases + 1):
        arrived = hop(states, phase, True)
        states, arrived = sync(states, arrived)
        states = land(states, arrived)
    after_own, after_oth = end_states(states)
    go_sums, ff_far, after_own, after_oth = hold(go_sums, ff_far, after_own, after_oth)

    go_sums = shrink(go_sums, 1)
    grad_k, grad_v, kv_g_own, kv_g_oth = call(
        last_kernel,
        H,
        info,
        [
            rates_in, whole(normed_t), head_in(key), head_in(value), head_in(key_part),
            head_in(value_part), whole(cosine), whole(sine), whole(tall_count),
            own_in(after_own), other_in(after_oth),
        ],
        [
            head_out(per_head + (QK,), BF16), head_out(per_head + (VH,), BF16),
            whole_out(grad_shape + (1536,), BF16), whole_out(grad_shape + (1536,), BF16),
        ],
        [],
        8 * unit,
        "last",
    )
    go_sums, kv_g_own, kv_g_oth, grad_k, grad_v = hold(
        go_sums, kv_g_own, kv_g_oth, grad_k, grad_v
    )
    kv_g_got = swap(kv_g_oth, 1)
    for turn in range(2, levels):
        go_sums = shrink(go_sums, turn)
    go_sums, kv_g_own, kv_g_got = hold(go_sums, kv_g_own, kv_g_got)
    kv_sums = shrink(split_first(kv_g_own, kv_g_got), 0)
    go_far = shrink_far(go_sums)
    input_grad, grad_first_gain, grad_first_bias = call(
        input_kernel,
        H,
        info,
        [
            whole(x), whole(first_gain), whole(grad_hidden), whole(norm_part),
            head_in(grad_k), head_in(grad_v),
            columns(qkv_own, 256, 2, True), columns(qkv_oth, 256, 2, False),
            columns(qkv_own, 512, 2, True), columns(qkv_oth, 512, 2, False),
        ],
        [
            whole_out((tokens, width), F32), whole_out((1, width), F32),
            whole_out((1, width), F32),
        ],
        [pltpu.VMEM((tokens, width), F32)],
        6 * unit,
        "input",
    )
    kv_sums, go_far, input_grad, grad_first_gain, grad_first_bias = hold(
        kv_sums, go_far, input_grad, grad_first_gain, grad_first_bias
    )
    small = [grad_first_gain, grad_first_bias, grad_second_gain, grad_second_bias, grad_group_gain]
    small = jnp.concatenate([part.reshape(count, -1) for part in small], axis=1)
    small = jnp.pad(small, ((0, 0), (0, 1024 - edges[-1]))).reshape(count, 8, 128)
    kv_sums = shrink(kv_sums, 1)
    spread_small = lax.all_to_all(small, AXES, 0, 0, tiled=True)
    kv_sums, spread_small = hold(kv_sums, spread_small)
    for turn in range(2, levels):
        kv_sums = shrink(kv_sums, turn)
    summed = jnp.sum(spread_small, axis=0).reshape(-1)
    small = [summed[a:b] for a, b in zip(edges[:-1], edges[1:])]
    kv_far = shrink_far(kv_sums)

    def whole_sum(far):
        return far[0] + far[1].astype(F32)

    ff_grad, go_grad, kv_grad = whole_sum(ff_far), whole_sum(go_far), whole_sum(kv_far)
    ff_mine, ff_got = finish_wide(ff_grad[:, :1024])
    go_mine, go_got = finish_wide(jnp.concatenate([go_grad[:, :1024], go_grad[:, 2048:]], axis=1))
    kv_mine, kv_got = finish_wide(kv_grad)

    def wide(mine, got, start, stop):
        return ordered(mine[:, start:stop], got[:, start:stop], 1)

    return (
        output.reshape(inputs.shape),
        input_grad.reshape(inputs.shape),
        small[0],
        small[1],
        wide(go_mine, go_got, 1024, 1536),
        wide(kv_mine, kv_got, 0, 512),
        wide(kv_mine, kv_got, 512, 1536),
        wide(go_mine, go_got, 0, 1024),
        small[4],
        finish_tall(go_grad[:, 1024:2048]),
        small[2],
        small[3],
        wide(ff_mine, ff_got, 0, 1024),
        finish_tall(ff_grad[:, 1024:2048]),
    )


def solution(mesh):
    return jax.shard_map(
        per_device,
        mesh=mesh,
        in_specs=(
            P(None, "dp", "seq", None),
            P(None, "dp", "seq"),
            P(("dp", "seq")),
            P(("dp", "seq")),
            P(("dp", "seq"), None),
            P(("dp", "seq"), None),
            P(("dp", "seq"), None),
            P(("dp", "seq"), None),
            P(("dp", "seq")),
            P(("dp", "seq"), None),
            P(("dp", "seq")),
            P(("dp", "seq")),
            P(("dp", "seq"), None),
            P(("dp", "seq"), None),
            P(None, "dp", "seq", None),
        ),
        out_specs=(
            P(None, "dp", "seq", None),
            P(None, "dp", "seq", None),
            P(("dp", "seq")),
            P(("dp", "seq")),
            P(("dp", "seq"), None),
            P(("dp", "seq"), None),
            P(("dp", "seq"), None),
            P(("dp", "seq"), None),
            P(("dp", "seq")),
            P(("dp", "seq"), None),
            P(("dp", "seq")),
            P(("dp", "seq")),
            P(("dp", "seq"), None),
            P(("dp", "seq"), None),
        ),
        check_vma=False,
    )
```

```python
import jax
import jax.numpy as jnp
from jax import lax
from jax.experimental import pallas as pl
from jax.experimental.pallas import tpu as pltpu
from jax.sharding import PartitionSpec as P

H = 4
QK = 256
VH = 512
AXES = ("dp", "seq")
F32 = jnp.float32
BF16 = jnp.bfloat16
FAR = 4
MIB = 1024 * 1024


def mm(left, right):
    return lax.dot_general(left, right, (((1,), (0,)), ((), ())), preferred_element_type=F32)


def nt(left, right):
    return lax.dot_general(left, right, (((1,), (1,)), ((), ())), preferred_element_type=F32)


def tn(left, right):
    return lax.dot_general(left, right, (((0,), (0,)), ((), ())), preferred_element_type=F32)


def devices():
    return lax.axis_size("dp") * lax.axis_size("seq")


def place():
    return lax.axis_index("dp") * lax.axis_size("seq") + lax.axis_index("seq")


def swap(values, bit):
    return lax.ppermute(values, AXES, [(i, i ^ bit) for i in range(devices())])


def upper_core():
    return lax.axis_index("seq") % 2 == 1


def sync(*values):
    return lax.optimization_barrier(values)


def orders():
    bits = [1 << k for k in range(1, devices().bit_length() - 1)]
    near = [bit for bit in bits if bit not in (2, FAR)]
    return (near[:1] + [2] + near[1:] + [FAR], near[1:] + near[:1] + [2, FAR])


def step(values, turn):
    pairs = [(i, i ^ orders()[i % 2][turn]) for i in range(devices())]
    return lax.ppermute(values, AXES, pairs)


def chip_tables():
    count = devices() // 2
    me, core = place() // 2, lax.axis_index("seq") % 2
    every = jnp.arange(count, dtype=jnp.int32)

    def spread_bits(values, sources, targets):
        return sum(((values >> s) & 1) << t for s, t in zip(sources, targets))

    spots, chips = [], []
    for order in orders():
        sources = [bit.bit_length() - 2 for bit in order]
        targets = list(range(len(order)))[::-1]
        spots.append(spread_bits(every ^ me, sources, targets))
        chips.append(spread_bits(every, targets, sources) ^ me)
    return jnp.concatenate(
        [
            jnp.stack([me, core]),
            jnp.where(core == 1, spots[1], spots[0]),
            jnp.where(core == 1, chips[1], chips[0]),
            jnp.where(core == 1, spots[0], spots[1]),
        ]
    ).astype(jnp.int32)


def local(body, outs, *arrays, name):
    size = sum(a.size * a.dtype.itemsize for a in arrays)
    for shape, dtype in outs:
        extent = jnp.dtype(dtype).itemsize
        for length in shape:
            extent *= length
        size += extent

    def spec(shape):
        zeros = (0,) * len(shape)
        return pl.BlockSpec(shape, lambda k: zeros)

    return pl.pallas_call(
        body,
        grid=(1,),
        out_shape=[jax.ShapeDtypeStruct(shape, dtype) for shape, dtype in outs],
        in_specs=[
            pl.BlockSpec(memory_space=pltpu.SMEM) if a.dtype == jnp.int32 else spec(a.shape)
            for a in arrays
        ],
        out_specs=[spec(shape) for shape, _ in outs],
        compiler_params=pltpu.CompilerParams(vmem_limit_bytes=2 * size + 4 * MIB),
        cost_estimate=pl.CostEstimate(flops=1, bytes_accessed=1, transcendentals=0),
        name=name,
    )(*arrays)


def pack(info, *weights):
    width = sum(w.shape[1] for w in weights) // 2
    shape = (weights[0].shape[0], width)

    def body(info_ref, *refs):
        keep, give = refs[-2:]
        at = 0
        for ref in refs[:-2]:
            half = ref.shape[1] // 2
            here = pl.multiple_of(info_ref[1] * half, 128)
            there = pl.multiple_of((1 - info_ref[1]) * half, 128)
            keep[:, at : at + half] = ref[:, pl.ds(here, half)]
            give[:, at : at + half] = ref[:, pl.ds(there, half)]
            at += half

    return local(body, [(shape, BF16)] * 2, info, *weights, name="pack")


def stack_rows(info, keep, got):
    rows, width = keep.shape

    def body(info_ref, keep_ref, got_ref, out):
        upper = info_ref[1] == 1
        out[:rows] = jnp.where(upper, got_ref[...], keep_ref[...])
        out[rows:] = jnp.where(upper, keep_ref[...], got_ref[...])

    return local(body, [((2 * rows, width), BF16)], info, keep, got, name="stack")[0]


def join(part, got):
    half = part.shape[0]

    def body(part_ref, got_ref, out):
        out[:half] = part_ref[...]
        out[half:] = got_ref[...]

    outs = [((2 * half,) + part.shape[1:], BF16)]
    return local(body, outs, part, got, name="join")[0]


def settle(info, *pieces):
    lengths = [piece.shape[0] for piece in pieces]
    chips = sum(lengths)

    def body(info_ref, *refs):
        at = 0
        for ref, length in zip(refs, lengths):
            for block in range(length):
                refs[-1][info_ref[2 + chips + at]] = ref[block]
                at += 1

    outs = [((chips,) + pieces[0].shape[1:], BF16)]
    return local(body, outs, info, *pieces, name="settle")[0]


@jax.tree_util.register_pytree_node_class
class Piece:
    def __init__(self, array, start=0):
        self.array, self.start = array, start

    def tree_flatten(self):
        return (self.array,), self.start

    @classmethod
    def tree_unflatten(cls, start, children):
        return cls(children[0], start)


def summed(pieces, start, stop):
    total = None
    for piece in pieces:
        first, last = start - piece.start, stop - piece.start
        if 0 <= first and last <= piece.array.shape[0]:
            value = piece.array[first:last].astype(F32)
            total = value if total is None else total + value
    return total


def span(turn):
    length = devices() // 2 >> turn
    return length // 2, length


def shrink(pieces, turn, part=None):
    start, stop = span(turn)
    shift = start
    if part is not None:
        middle = (start + stop) // 2
        start, stop = (middle, stop) if part else (start, middle)
    send = summed(pieces, start, stop).astype(BF16)
    return [Piece(step(send, turn), start - shift)]


def ordered(mine, other, axis):
    upper = upper_core()
    return jnp.concatenate(
        [jnp.where(upper, other, mine), jnp.where(upper, mine, other)], axis=axis
    )


def finish_wide(values):
    rows = values.shape[0] // 2
    upper = upper_core()
    low, high = values[:rows], values[rows:]
    mine, give = jnp.where(upper, high, low), jnp.where(upper, low, high)
    return mine, swap(give, 1)


def finish_tall(values):
    half = values.shape[1] // 2
    upper = upper_core()
    low, high = values[:, :half], values[:, half:]
    mine, give = jnp.where(upper, high, low), jnp.where(upper, low, high)
    return ordered(mine, swap(give, 1), 1)


def states_of(carry, near_carry, own, near, reverse):
    upper = upper_core()
    turned = jnp.logical_not(upper) if reverse else upper
    one, zero = jnp.ones_like(carry), jnp.zeros_like(carry)

    def either(yes, no):
        return jnp.where(turned, yes, no)[:, :, None, None]

    passed = (either(one, near_carry), either(carry, one), (carry * near_carry)[:, :, None, None])
    mine = (either(zero, zero), either(one, zero), either(near_carry, one))
    theirs = (either(zero, one), either(zero, zero), either(one, carry))
    return (passed, mine, theirs, own, near)


def entered(arrived, row):
    total = None
    for arrivals in arrived:
        if arrivals[row] is not None:
            value = arrivals[row].astype(F32)
            total = value if total is None else total + value
    return total


def hop(states, arrived, phase, reverse):
    (a, b, c), _, _, own, near = states
    chips = lax.axis_size("seq") // 2
    arrivals = []
    for row in range(own.shape[1]):
        step = phase - row
        if not 1 <= step < chips:
            arrivals.append(None)
            continue
        message = a[:, row] * own[:, row] + b[:, row] * near[:, row]
        before = entered(arrived, row)
        if before is not None:
            message = message + c[:, row] * before
        source, target = (step - 1, step) if not reverse else (chips - step, chips - step - 1)
        pairs = [(2 * source + core, 2 * target + core) for core in range(2)]
        arrivals.append(lax.ppermute(message.astype(BF16), "seq", pairs))
    return arrivals


def end_states(states, arrived):
    _, mine, theirs, own, near = states
    before = jnp.stack([entered(arrived, row) for row in range(own.shape[1])], axis=1)

    def taken(factors):
        a, b, c = factors
        return (a * own + b * near + c * before).astype(BF16)

    return taken(mine), swap(taken(theirs), 1)


def call(body, grid, info, ins, outs, scratch, flops, name, vmem):
    def spec(block, index):
        if block is None:
            return pl.BlockSpec(memory_space=pltpu.SMEM)
        return pl.BlockSpec(block, index)

    moved = sum(a.size * a.dtype.itemsize for a, _, _ in ins)
    for shape, dtype, _, _ in outs:
        size = jnp.dtype(dtype).itemsize
        for extent in shape:
            size *= extent
        moved += size
    return pl.pallas_call(
        body,
        grid_spec=pltpu.PrefetchScalarGridSpec(
            num_scalar_prefetch=1,
            grid=(grid,),
            in_specs=[spec(block, index) for _, block, index in ins],
            out_specs=[spec(block, index) for _, _, block, index in outs],
            scratch_shapes=scratch,
        ),
        out_shape=[jax.ShapeDtypeStruct(shape, dtype) for shape, dtype, _, _ in outs],
        compiler_params=pltpu.CompilerParams(
            vmem_limit_bytes=vmem * MIB, dimension_semantics=("arbitrary",)
        ),
        cost_estimate=pl.CostEstimate(flops=1, bytes_accessed=1, transcendentals=0),
        name=name,
    )(info, *[a for a, _, _ in ins])


def whole(array):
    zeros = (0,) * array.ndim
    return (array, array.shape, lambda h, info: zeros)


def whole_out(shape, dtype):
    zeros = (0,) * len(shape)
    return (shape, dtype, shape, lambda h, info: zeros)


def head_in(array):
    rest = (0,) * (array.ndim - 1)
    return (array, (1,) + array.shape[1:], lambda h, info: (h,) + rest)


def head_out(shape, dtype):
    rest = (0,) * (len(shape) - 1)
    return (shape, dtype, (1,) + shape[1:], lambda h, info: (h,) + rest)


def own_in(array):
    rest = (0,) * (array.ndim - 1)
    return (array, (1,) + array.shape[1:], lambda h, info: (jnp.minimum(h, 1),) + rest)


def other_in(array):
    rest = (0,) * (array.ndim - 1)
    return (array, (1,) + array.shape[1:], lambda h, info: (jnp.maximum(h - 2, 0),) + rest)


def own_out(shape, dtype):
    rest = (0,) * (len(shape) - 1)
    return (shape, dtype, (1,) + shape[1:], lambda h, info: (jnp.minimum(h, 1),) + rest)


def other_out(shape, dtype):
    rest = (0,) * (len(shape) - 1)
    return (shape, dtype, (1,) + shape[1:], lambda h, info: (jnp.maximum(h - 2, 0),) + rest)


def real(h, info):
    return lax.rem(h + 2 * info[1], 4)


def real_in(array):
    rest = (0,) * (array.ndim - 1)
    return (array, (1,) + array.shape[1:], lambda h, info: (real(h, info),) + rest)


def columns(array, width, first, own):
    block = array.shape[:2] + (width,)
    if own:
        return (array, block, lambda h, info: (0, 0, first + jnp.minimum(h, 1)))
    return (array, block, lambda h, info: (0, 0, first + jnp.maximum(h - 2, 0)))


def tall(array):
    block = (array.shape[0] // 4, array.shape[1], 1024)
    return (array, block, lambda h, info: (real(h, info), 0, 1))


def tall_rows(ref):
    chips = ref.shape[0]
    pieces = []
    for chip in range(chips):
        pieces += [ref[chip, :, :512], ref[chip, :, 512:]]
    return jnp.concatenate(pieces, axis=0)


def flat(ref):
    chips, rows, width = ref.shape
    return ref[...].reshape(chips * rows, width)


def side(info, own):
    return pl.multiple_of(512 * (info[1] if own else 1 - info[1]), 512)


def put_wide(target, info, values, start, own):
    chips, rows, _ = target.shape
    width = values.shape[1]
    values = values.astype(BF16)
    for chip in range(chips):
        target[info[(2 if own else 2 + 2 * chips) + chip], :, start : start + width] = values[chip * rows : (chip + 1) * rows]


def put_tall(target, info, values, block, start, own):
    chips, rows, _ = target.shape
    values = values.astype(BF16)
    share = chips // 4
    for chip in range(share):
        at = info[(2 if own else 2 + 2 * chips) + block * share + chip]
        base = 2 * rows * chip
        target[at, :, start : start + 512] = values[base : base + rows]
        target[at, :, start + 512 : start + 1024] = values[base + rows : base + 2 * rows]


def rotated(values, cosine, sine):
    a, b = values[:, :128], values[:, 128:]
    return jnp.concatenate([a * cosine - b * sine, b * cosine + a * sine], axis=1)


def unrotated(values, cosine, sine):
    a, b = values[:, :128], values[:, 128:]
    return jnp.concatenate([a * cosine + b * sine, b * cosine - a * sine], axis=1)


def mask_of(rate, tall_count, wide_count):
    length = tall_count.shape[0]
    i = lax.broadcasted_iota(jnp.int32, (length, length), 0)
    s = lax.broadcasted_iota(jnp.int32, (length, length), 1)
    decay = jnp.exp((i - s).astype(F32) * rate)
    return jnp.where((tall_count == wide_count) & (i >= s), decay, 0.0)


def enter_of(rate, tall_count):
    i = lax.broadcasted_iota(jnp.int32, tall_count.shape, 0)
    return jnp.where(tall_count == 0, jnp.exp((i + 1).astype(F32) * rate), 0.0)


def leave_of(rate, tall_count):
    length = tall_count.shape[0]
    i = lax.broadcasted_iota(jnp.int32, tall_count.shape, 0)
    last = tall_count[length - 1 :, :]
    return jnp.where(tall_count == last, jnp.exp((length - 1 - i).astype(F32) * rate), 0.0)


def norm_parts(values, eps):
    average = jnp.mean(values, axis=-1, keepdims=True)
    centred = values - average
    spread_ = jnp.mean(centred * centred, axis=-1, keepdims=True)
    scale = lax.rsqrt(spread_ + eps)
    return centred * scale, scale


def norm_back(grad, normal, scale):
    first = jnp.mean(grad, axis=-1, keepdims=True)
    second = jnp.mean(grad * normal, axis=-1, keepdims=True)
    return scale * (grad - first - normal * second)


CHUNK = 64


def norm_kernel(info, x, gain, bias, normed, normed_t):
    @pl.loop(0, x.shape[0] // CHUNK)
    def _(k):
        at = pl.ds(pl.multiple_of(k * CHUNK, CHUNK), CHUNK)
        normal, _ = norm_parts(x[at, :].astype(F32), 1e-05)
        normed[at, :] = (normal * gain[...].astype(F32) + bias[...].astype(F32)).astype(BF16)

    normed_t[...] = normed[...].T


def project_kernel(
    info, rates, normed, cosine, sine, tall_count, wide_count,
    q_own, k_own, v_own, q_oth, k_oth, v_oth,
    q_out, k_out, v_out, mix_out, inner_out, sum_own, sum_oth, pre,
):
    h = pl.program_id(0)

    def fill(wq, wk, wv):
        left = normed[...]
        pre[:, :256] = mm(left, flat(wq))
        pre[:, 256:512] = mm(left, flat(wk))
        pre[:, 512:] = mm(left, flat(wv))

    @pl.when(h < 2)
    def _():
        fill(q_own, k_own, v_own)

    @pl.when(h >= 2)
    def _():
        fill(q_oth, k_oth, v_oth)

    rate = rates[h]
    length = cosine.shape[0]
    for row in range(tall_count.shape[0]):
        at = slice(row * length, (row + 1) * length)
        count = tall_count[row]
        query = rotated(pre[at, :256], cosine[...], sine[...]).astype(BF16)
        key = (rotated(pre[at, 256:512], cosine[...], sine[...]) * QK**-0.5).astype(BF16)
        value = pre[at, 512:].astype(BF16)
        q_out[0, at] = query
        k_out[0, at] = key
        v_out[0, at] = value
        mixing = (nt(query, key) * mask_of(rate, count, wide_count[row])).astype(BF16)
        mix_out[0, at] = mixing
        inner_out[0, at] = mm(mixing, value)
        weighted = (key.astype(F32) * leave_of(rate, count)).astype(BF16)
        summary = tn(weighted, value)

        @pl.when(h < 2)
        def _():
            sum_own[0, row] = summary

        @pl.when(h >= 2)
        def _():
            sum_oth[0, row] = summary


def gate_kernel(info, normed, own, oth, out):
    h = pl.program_id(0)

    @pl.when(h < 2)
    def _():
        out[0] = mm(normed[...], flat(own))

    @pl.when(h >= 2)
    def _():
        out[0] = mm(normed[...], flat(oth))


def mix_kernel(
    info, rates, x, gain, second_gain, second_bias, tall_count, query, inner, gate,
    state_own, state_oth, wo_own, wo_oth,
    retained, mixed_t, hidden, normed, normed_t,
):
    h = pl.program_id(0)
    rate = rates[h]
    length = tall_count.shape[1]

    @pl.when(h == 0)
    def _():
        hidden[...] = x[...].astype(F32)

    for row in range(tall_count.shape[0]):
        at = slice(row * length, (row + 1) * length)
        entered = (query[0, at].astype(F32) * enter_of(rate, tall_count[row])).astype(BF16)

        @pl.when(h < 2)
        def _():
            retained[0, at] = inner[0, at] + mm(entered, state_own[0, row])

        @pl.when(h >= 2)
        def _():
            retained[0, at] = inner[0, at] + mm(entered, state_oth[0, row])

    normal, _ = norm_parts(retained[0], 1.0)
    pre = gate[0]
    mixed = (pre / (1.0 + jnp.exp(-pre)) * (normal * gain[0].astype(F32))).astype(BF16)
    mixed_t[0] = mixed.T
    hidden[:, pl.ds(side(info, True), 512)] += mm(mixed, tall_rows(wo_own))
    hidden[:, pl.ds(side(info, False), 512)] += mm(mixed, tall_rows(wo_oth))

    @pl.when(h == 3)
    def _():
        @pl.loop(0, x.shape[0] // CHUNK)
        def _(k):
            at = pl.ds(pl.multiple_of(k * CHUNK, CHUNK), CHUNK)
            normal, _ = norm_parts(hidden[at, :], 1e-05)
            normed[at, :] = (
                normal * second_gain[...].astype(F32) + second_bias[...].astype(F32)
            ).astype(BF16)

        normed_t[...] = normed[...].T


def feed_kernel(
    info, hidden, normed, normed_t, cot, second_gain,
    up_own, up_oth, down_own, down_oth,
    output, grad_hidden, grad_low, grad_gain, grad_bias, g_own, g_oth,
    upward, out_sum, norm_sum,
):
    f = pl.program_id(0)
    own_at = pl.ds(side(info, True), 512)
    oth_at = pl.ds(side(info, False), 512)

    @pl.when(f == 0)
    def _():
        out_sum[...] = hidden[...]
        norm_sum[...] = jnp.zeros_like(norm_sum)

    @pl.when(f < 2)
    def _():
        upward[...] = mm(normed[...], flat(up_own))

    @pl.when(f >= 2)
    def _():
        upward[...] = mm(normed[...], flat(up_oth))

    up = upward[...]
    root = 0.7978845608028654
    squared = up * up
    bent = jnp.tanh(root * (up + 0.044715 * (squared * up)))
    activated = (0.5 * up * (1.0 + bent)).astype(BF16)
    slope = 0.5 * (1.0 + bent) + 0.5 * up * (1.0 - bent * bent) * (
        root * (1.0 + 3 * 0.044715 * squared)
    )
    own, oth = tall_rows(down_own), tall_rows(down_oth)
    out_sum[:, own_at] += mm(activated, own)
    out_sum[:, oth_at] += mm(activated, oth)
    grad_up = (slope * (nt(cot[:, own_at], own) + nt(cot[:, oth_at], oth))).astype(BF16)
    block = real(f, info)
    act_t = activated.T
    put_tall(g_own, info, mm(act_t, cot[:, own_at]), block, 1024, True)
    put_tall(g_oth, info, mm(act_t, cot[:, oth_at]), block, 1024, False)
    grad_w = mm(normed_t[...], grad_up)
    for step in range(4):

        @pl.when(f == step)
        def _():
            put_wide(g_own if step < 2 else g_oth, info, grad_w, 512 * (step % 2), step < 2)

    @pl.when(f < 2)
    def _():
        norm_sum[...] += nt(grad_up, flat(up_own))

    @pl.when(f >= 2)
    def _():
        norm_sum[...] += nt(grad_up, flat(up_oth))

    @pl.when(f == 3)
    def _():
        grad_gain[...] = jnp.zeros_like(grad_gain)
        grad_bias[...] = jnp.zeros_like(grad_bias)

        @pl.loop(0, hidden.shape[0] // CHUNK)
        def _(k):
            at = pl.ds(pl.multiple_of(k * CHUNK, CHUNK), CHUNK)
            output[at, :] = out_sum[at, :].astype(BF16)
            normal, scale = norm_parts(hidden[at, :], 1e-05)
            grad = norm_sum[at, :]
            grad_gain[...] += jnp.sum(grad * normal, axis=0, keepdims=True)
            grad_bias[...] += jnp.sum(grad, axis=0, keepdims=True)
            total = cot[at, :].astype(F32) + norm_back(
                grad * second_gain[...].astype(F32), normal, scale
            )
            grad_hidden[at, :] = total
            grad_low[at, :] = total.astype(BF16)


def unmix_kernel(
    info, rates, grad_low, gain, tall_count, query, retained, gate, wo_own, wo_oth,
    grad_ret, grad_gate, grad_gain, state_own, state_oth,
):
    h = pl.program_id(0)
    rate = rates[h]
    length = tall_count.shape[1]
    grad = nt(grad_low[:, pl.ds(side(info, True), 512)], tall_rows(wo_own)) + nt(
        grad_low[:, pl.ds(side(info, False), 512)], tall_rows(wo_oth)
    )
    normal, scale = norm_parts(retained[0], 1.0)
    pre = gate[0]
    share = 1.0 / (1.0 + jnp.exp(-pre))
    curve = pre * share
    scaled = gain[0].astype(F32)
    grad_gate[0] = (grad * (normal * scaled) * (share * (1.0 + pre * (1.0 - share)))).astype(BF16)
    grad_normal = grad * curve
    grad_gain[0] = jnp.sum(grad_normal * normal, axis=0, keepdims=True)
    grad_ret[0] = norm_back(grad_normal * scaled, normal, scale).astype(BF16)
    for row in range(tall_count.shape[0]):
        at = slice(row * length, (row + 1) * length)
        entered = (query[0, at].astype(F32) * enter_of(rate, tall_count[row])).astype(BF16)
        state = tn(entered, grad_ret[0, at])

        @pl.when(h < 2)
        def _():
            state_own[0, row] = state

        @pl.when(h >= 2)
        def _():
            state_oth[0, row] = state


def inside_kernel(
    info, rates, grad_ret, query, key, value, mixing,
    cosine, sine, tall_count, wide_count, state_own, state_oth,
    grad_q, key_part, value_part,
):
    h = pl.program_id(0)
    rate = rates[h]
    length = cosine.shape[0]
    for row in range(tall_count.shape[0]):
        at = slice(row * length, (row + 1) * length)
        grad = grad_ret[0, at]
        mask = mask_of(rate, tall_count[row], wide_count[row])
        scores = (nt(grad, value[0, at]) * mask).astype(BF16)
        enter = enter_of(rate, tall_count[row])

        def set_query(state):
            total = mm(scores, key[0, at]) + nt(grad, state[0, row]) * enter
            grad_q[0, at] = unrotated(total, cosine[...], sine[...]).astype(BF16)

        @pl.when(h < 2)
        def _():
            set_query(state_own)

        @pl.when(h >= 2)
        def _():
            set_query(state_oth)

        key_part[0, at] = tn(scores, query[0, at])
        value_part[0, at] = tn(mixing[0, at], grad)


def outer_kernel(
    info, grad_low, normed_t, mixed_t, grad_gate, grad_q, g_own, g_oth, q_own, q_oth,
    norm_part, out_own, out_oth,
):
    h = pl.program_id(0)

    @pl.when(h == 0)
    def _():
        norm_part[...] = jnp.zeros_like(norm_part)

    block = real(h, info)
    left = mixed_t[0]
    put_tall(out_own, info, mm(left, grad_low[:, pl.ds(side(info, True), 512)]), block, 1024, True)
    put_tall(out_oth, info, mm(left, grad_low[:, pl.ds(side(info, False), 512)]), block, 1024, False)
    grad_wg = mm(normed_t[...], grad_gate[0])
    grad_wq = mm(normed_t[...], grad_q[0])
    for step in range(4):

        @pl.when(h == step)
        def _():
            target = out_own if step < 2 else out_oth
            put_wide(target, info, grad_wg, 512 * (step % 2), step < 2)
            put_wide(target, info, grad_wq, 2048 + 256 * (step % 2), step < 2)

    @pl.when(h < 2)
    def _():
        norm_part[...] += nt(grad_gate[0], flat(g_own)) + nt(grad_q[0], flat(q_own))

    @pl.when(h >= 2)
    def _():
        norm_part[...] += nt(grad_gate[0], flat(g_oth)) + nt(grad_q[0], flat(q_oth))


def last_kernel(
    info, rates, normed_t, key, value, key_part, value_part, cosine, sine, tall_count,
    state_own, state_oth,
    grad_k, grad_v, out_own, out_oth,
):
    h = pl.program_id(0)
    rate = rates[h]
    length = cosine.shape[0]
    for row in range(tall_count.shape[0]):
        at = slice(row * length, (row + 1) * length)
        leave = leave_of(rate, tall_count[row])
        weighted = (key[0, at].astype(F32) * leave).astype(BF16)

        def set_both(state):
            low = state[0, row]
            grad_v[0, at] = (value_part[0, at] + mm(weighted, low)).astype(BF16)
            total = key_part[0, at] + nt(value[0, at], low) * leave
            grad_k[0, at] = (unrotated(total, cosine[...], sine[...]) * QK**-0.5).astype(BF16)

        @pl.when(h < 2)
        def _():
            set_both(state_own)

        @pl.when(h >= 2)
        def _():
            set_both(state_oth)

    grad_wk = mm(normed_t[...], grad_k[0])
    grad_wv = mm(normed_t[...], grad_v[0])
    for step in range(4):

        @pl.when(h == step)
        def _():
            target = out_own if step < 2 else out_oth
            put_wide(target, info, grad_wk, 256 * (step % 2), step < 2)
            put_wide(target, info, grad_wv, 512 + 512 * (step % 2), step < 2)


def input_kernel(
    info, x, gain, grad_hidden, norm_part, grad_k, grad_v, k_own, k_oth, v_own, v_oth,
    input_grad, grad_gain, grad_bias, norm_sum,
):
    h = pl.program_id(0)

    @pl.when(h == 0)
    def _():
        norm_sum[...] = norm_part[...]

    @pl.when(h < 2)
    def _():
        norm_sum[...] += nt(grad_k[0], flat(k_own)) + nt(grad_v[0], flat(v_own))

    @pl.when(h >= 2)
    def _():
        norm_sum[...] += nt(grad_k[0], flat(k_oth)) + nt(grad_v[0], flat(v_oth))

    @pl.when(h == 3)
    def _():
        grad_gain[...] = jnp.zeros_like(grad_gain)
        grad_bias[...] = jnp.zeros_like(grad_bias)

        @pl.loop(0, x.shape[0] // CHUNK)
        def _(k):
            at = pl.ds(pl.multiple_of(k * CHUNK, CHUNK), CHUNK)
            normal, scale = norm_parts(x[at, :].astype(F32), 1e-05)
            grad = norm_sum[at, :]
            grad_gain[...] += jnp.sum(grad * normal, axis=0, keepdims=True)
            grad_bias[...] += jnp.sum(grad, axis=0, keepdims=True)
            input_grad[at, :] = grad_hidden[at, :] + norm_back(
                grad * gain[...].astype(F32), normal, scale
            )


def per_device(
    inputs,
    doc_flags,
    first_gain,
    first_bias,
    w_query,
    w_key,
    w_value,
    w_gate,
    group_gain,
    w_output,
    second_gain,
    second_bias,
    w_up,
    w_down,
    cotangent,
):
    batches, row_count, length, width = inputs.shape
    rows = batches * row_count
    tokens = rows * length
    count = devices()
    chips = count // 2
    info = chip_tables()
    x = inputs.reshape(tokens, width)
    cot = cotangent.reshape(tokens, width)

    upper = upper_core()
    share = w_query.shape[0]
    last = len(orders()[0]) - 1

    keep, give = pack(info, w_query, w_key, w_value)
    qkv = stack_rows(info, keep, swap(give, 1))
    vectors = [first_gain, first_bias, second_gain, second_bias, group_gain]
    qkv, vectors = sync(qkv, vectors)
    got_qkv = step(qkv[None], last)

    sizes = [v.shape[0] for v in vectors]
    edges = [sum(sizes[:k]) for k in range(len(sizes) + 1)]
    lanes = -(-edges[-1] // 128) * 128
    table = jnp.concatenate([v.reshape(1, -1) for v in vectors], axis=1)
    table = jnp.pad(table, ((0, 15), (0, lanes - edges[-1])))

    def table_step(table, done, bit):
        got = swap(table, bit)
        turned = (place() // bit) % 2 == 1
        spot = sum(1 for other in done if other > bit)
        done.append(bit)
        return jnp.stack(
            [jnp.where(turned, got, table), jnp.where(turned, table, got)], axis=spot
        )

    bits = [1 << k for k in range(count.bit_length() - 1)]
    done = []
    for bit in bits[:1] + bits[3:]:
        table = table_step(table, done, bit)
    got_qkv, table = sync(got_qkv, table)
    part, got = qkv[None], got_qkv
    for turn in range(last - 1, 1, -1):
        part = join(part, got)
        got = step(part, turn)
        if turn == last - 1:
            table = table_step(table, done, 2)
        part, got, table, w_gate, w_up, w_output, w_down, doc_flags = sync(
            part, got, table, w_gate, w_up, w_output, w_down, doc_flags
        )

    part = join(part, got)
    got = step(part, 1)
    table = table_step(table, done, FAR)

    top_keep, top_give = pack(info, w_gate, w_up)
    tall_keep, tall_give = pack(info, w_output, w_down)
    top = stack_rows(info, top_keep, swap(top_give, 1))
    tall_got = swap(tall_give, 1)
    low, high = jnp.where(upper, tall_got, tall_keep), jnp.where(upper, tall_keep, tall_got)
    go = jnp.concatenate([top[:, :1024], low[:, :512], high[:, :512]], axis=1)
    ff = jnp.concatenate([top[:, 1024:], low[:, 512:], high[:, 512:]], axis=1)
    go_part, ff_part = go[None], ff[None]
    part, got, go_part, ff_part, table, doc_flags = sync(
        part, got, go_part, ff_part, table, doc_flags
    )

    pieces = [part, got, step(part, 0), step(got, 0)]
    go_got = step(go_part, last)
    vector = table.reshape(count, -1, lanes)[:, 0]
    first_gain, first_bias, second_gain, second_bias, group_gain = [
        vector[:, a:b].reshape(1, -1) for a, b in zip(edges[:-1], edges[1:])
    ]
    group_gain = group_gain.reshape(H, 1, VH)

    positions = lax.axis_index("seq") * length + jnp.arange(length, dtype=jnp.int32)
    frequency = 10000.0 ** (-jnp.arange(QK // 2, dtype=F32) / (QK // 2))
    angles = positions.astype(F32)[:, None] * frequency[None, :]
    cosine, sine = jnp.cos(angles), jnp.sin(angles)
    rates = jnp.log1p(-(2.0 ** (-5.0 - 3.0 * jnp.arange(H, dtype=F32))))
    rates = jnp.where(upper, jnp.roll(rates, 2), rates)
    counts = jnp.cumsum(doc_flags.reshape(rows, length), axis=-1, dtype=jnp.int32)
    tall_count, wide_count = counts[:, :, None], counts[:, None, :]
    open_row = (counts[:, -1] == 0).astype(F32)
    near_row = swap(open_row, 1)
    decay = jnp.exp(rates[:2] * float(length))
    carry, near_carry = decay[:, None] * open_row[None], decay[:, None] * near_row[None]

    per_head = (H, tokens)
    state_shape = (2, rows, QK, VH)
    grad_shape = (chips, 2 * share)
    rates_in = (rates, None, None)
    unit = 2.0 * tokens * width * 512

    normed, normed_t = call(
        norm_kernel,
        1,
        info,
        [whole(x), whole(first_gain), whole(first_bias)],
        [whole_out((tokens, width), BF16), whole_out((width, tokens), BF16)],
        [],
        unit / 100,
        "norm",
        16,
    )
    pieces, go_part, go_got, normed, normed_t, tables, gains = sync(
        pieces, go_part, go_got, normed, normed_t,
        (cosine, sine, tall_count, wide_count, carry, near_carry, rates),
        (second_gain, second_bias, group_gain),
    )
    cosine, sine, tall_count, wide_count, carry, near_carry, rates = tables
    second_gain, second_bias, group_gain = gains
    rates_in = (rates, None, None)

    qkv_own = settle(info, *pieces)
    qkv_oth = swap(qkv_own, 1)
    go_part = join(go_part, go_got)
    go_got = step(go_part, last - 1)
    qkv_own, qkv_oth, go_part, go_got, ff_part = sync(qkv_own, qkv_oth, go_part, go_got, ff_part)

    go_part = join(go_part, go_got)
    go_got = step(go_part, last - 2)
    ff_got = step(ff_part, last)
    (query, key, value, mixing, inner, sum_own, sum_oth) = call(
        project_kernel,
        H,
        info,
        [
            rates_in, whole(normed), whole(cosine), whole(sine),
            whole(tall_count), whole(wide_count),
            columns(qkv_own, 256, 0, True), columns(qkv_own, 256, 2, True),
            columns(qkv_own, 512, 2, True),
            columns(qkv_oth, 256, 0, False), columns(qkv_oth, 256, 2, False),
            columns(qkv_oth, 512, 2, False),
        ],
        [
            head_out(per_head + (QK,), BF16), head_out(per_head + (QK,), BF16),
            head_out(per_head + (VH,), BF16), head_out(per_head + (length,), BF16),
            head_out(per_head + (VH,), F32),
            own_out(state_shape, F32), other_out(state_shape, F32),
        ],
        [pltpu.VMEM((tokens, 1024), F32)],
        10 * unit,
        "project",
        56,
    )
    go_part, go_got, ff_part, ff_got, sum_own, sum_oth = sync(
        go_part, go_got, ff_part, ff_got, sum_own, sum_oth
    )
    for turn in range(last - 3, 0, -1):
        go_part = join(go_part, go_got)
        go_got = step(go_part, turn)
        ff_part = join(ff_part, ff_got)
        ff_got = step(ff_part, turn + 2)
        go_part, go_got, ff_part, ff_got = sync(go_part, go_got, ff_part, ff_got)
    sum_near = swap(sum_oth, 1)
    ff_part = join(ff_part, ff_got)
    ff_got = step(ff_part, 2)
    sum_own, sum_near, go_part, go_got, ff_part, ff_got = sync(
        sum_own, sum_near, go_part, go_got, ff_part, ff_got
    )

    states = states_of(carry, near_carry, sum_own, sum_near, False)
    phases = lax.axis_size("seq") // 2 - 1 + rows - 1
    arrivals = hop(states, [], 1, False)
    go_first = step(go_part, 0)
    states, arrivals, go_part, go_got, go_first = sync(
        states, arrivals, go_part, go_got, go_first
    )
    arrived = [arrivals]

    arrivals = hop(states, arrived, 2, False)
    go_second = step(go_got, 0)
    states, arrived, arrivals, pieces, ff_part, ff_got = sync(
        states, arrived, arrivals, [go_part, go_got, go_first, go_second], ff_part, ff_got
    )
    arrived = arrived + [arrivals]

    arrivals = hop(states, arrived, 3, False)
    go_own = settle(info, *pieces)
    go_oth = swap(go_own, 1)
    ff_part = join(ff_part, ff_got)
    ff_got = step(ff_part, 1)
    states, arrived, arrivals, go_own, go_oth, normed, ff_part, ff_got = sync(
        states, arrived, arrivals, go_own, go_oth, normed, ff_part, ff_got
    )
    arrived = arrived + [arrivals]

    for phase in range(4, phases + 1):
        arrivals = hop(states, arrived, phase, False)
        if phase == 4:
            ff_first = step(ff_part, 0)
            (gate,) = call(
                gate_kernel,
                H,
                info,
                [whole(normed), columns(go_own, 512, 0, True), columns(go_oth, 512, 0, False)],
                [head_out(per_head + (VH,), F32)],
                [],
                4 * unit,
                "gate",
                20,
            )
        states, arrived, arrivals, gate, ff_part, ff_got, ff_first = sync(
            states, arrived, arrivals, gate, ff_part, ff_got, ff_first
        )
        arrived = arrived + [arrivals]
    state_own, state_oth = end_states(states, arrived)
    state_own, state_oth, ff_got = sync(state_own, state_oth, ff_got)
    ff_second = step(ff_got, 0)

    retained, mixed_t, hidden, normed_second, normed_second_t = call(
        mix_kernel,
        H,
        info,
        [
            rates_in, whole(x), real_in(group_gain), whole(second_gain), whole(second_bias),
            whole(tall_count), head_in(query), head_in(inner), head_in(gate),
            own_in(state_own), other_in(state_oth), tall(go_own), tall(go_oth),
        ],
        [
            head_out(per_head + (VH,), F32), head_out((H, VH, tokens), BF16),
            whole_out((tokens, width), F32), whole_out((tokens, width), BF16),
            whole_out((width, tokens), BF16),
        ],
        [],
        5 * unit,
        "mix",
        32,
    )
    ff_second, hidden = sync(ff_second, hidden)
    ff_own = settle(info, ff_part, ff_got, ff_first, ff_second)
    ff_oth = swap(ff_own, 1)
    output, grad_hidden, grad_low, grad_second_gain, grad_second_bias, ff_g_own, ff_g_oth = call(
        feed_kernel,
        4,
        info,
        [
            whole(hidden), whole(normed_second), whole(normed_second_t), whole(cot),
            whole(second_gain),
            columns(ff_own, 512, 0, True), columns(ff_oth, 512, 0, False),
            tall(ff_own), tall(ff_oth),
        ],
        [
            whole_out((tokens, width), BF16), whole_out((tokens, width), F32),
            whole_out((tokens, width), BF16), whole_out((1, width), F32),
            whole_out((1, width), F32),
            whole_out(grad_shape + (2048,), BF16), whole_out(grad_shape + (2048,), BF16),
        ],
        [
            pltpu.VMEM((tokens, 512), F32), pltpu.VMEM((tokens, width), F32),
            pltpu.VMEM((tokens, width), F32),
        ],
        24 * unit,
        "feed",
        48,
    )

    ff_g_got = swap(ff_g_oth, 1)
    grad_ret, grad_gate, grad_group_gain, gstate_own, gstate_oth = call(
        unmix_kernel,
        H,
        info,
        [
            rates_in, whole(grad_low), real_in(group_gain), whole(tall_count), head_in(query),
            head_in(retained), head_in(gate), tall(go_own), tall(go_oth),
        ],
        [
            head_out(per_head + (VH,), BF16), head_out(per_head + (VH,), BF16),
            (
                (H, 1, VH), F32, (1, 1, VH),
                lambda h, info: (real(h, info), 0, 0),
            ),
            own_out(state_shape, F32), other_out(state_shape, F32),
        ],
        [],
        5 * unit,
        "unmix",
        32,
    )
    ff_g_own, ff_g_got, gstate_own, gstate_oth, grad_gate, grad_ret = sync(
        ff_g_own, ff_g_got, gstate_own, gstate_oth, grad_gate, grad_ret
    )
    gstate_near = swap(gstate_oth, 1)
    ff_sum = [Piece(ff_g_own), Piece(ff_g_got)]
    gstate_own, gstate_near, grad_gate, grad_ret = sync(
        gstate_own, gstate_near, grad_gate, grad_ret
    )

    states = states_of(carry, near_carry, gstate_own, gstate_near, True)
    arrived = []
    arrivals = hop(states, arrived, 1, True)
    ff_first = shrink(ff_sum, 0, 1)
    grad_q, key_part, value_part = call(
        inside_kernel,
        H,
        info,
        [
            rates_in, head_in(grad_ret),
            head_in(query), head_in(key), head_in(value), head_in(mixing),
            whole(cosine), whole(sine), whole(tall_count), whole(wide_count),
            own_in(state_own), other_in(state_oth),
        ],
        [
            head_out(per_head + (QK,), BF16),
            head_out(per_head + (QK,), F32), head_out(per_head + (VH,), F32),
        ],
        [],
        3 * unit,
        "inside",
        24,
    )
    states, arrivals, ff_sum, ff_first, grad_q, key_part, value_part = sync(
        states, arrivals, ff_sum, ff_first, grad_q, key_part, value_part
    )
    arrived = arrived + [arrivals]

    arrivals = hop(states, arrived, 2, True)
    ff_sum = ff_sum + ff_first + shrink(ff_sum, 0, 0)
    norm_part, go_g_own, go_g_oth = call(
        outer_kernel,
        H,
        info,
        [
            whole(grad_low), whole(normed_t), head_in(mixed_t), head_in(grad_gate),
            head_in(grad_q),
            columns(go_own, 512, 0, True), columns(go_oth, 512, 0, False),
            columns(qkv_own, 256, 0, True), columns(qkv_oth, 256, 0, False),
        ],
        [
            whole_out((tokens, width), F32),
            whole_out(grad_shape + (2560,), BF16), whole_out(grad_shape + (2560,), BF16),
        ],
        [],
        16 * unit,
        "outer",
        44,
    )
    states, arrived, arrivals, ff_sum, norm_part, go_g_own, go_g_oth = sync(
        states, arrived, arrivals, ff_sum, norm_part, go_g_own, go_g_oth
    )
    arrived = arrived + [arrivals]

    arrivals = hop(states, arrived, 3, True)
    go_g_got = swap(go_g_oth, 1)
    ff_sum = ff_sum + shrink(ff_sum, 1)
    states, arrived, arrivals, go_g_own, go_g_got, ff_sum = sync(
        states, arrived, arrivals, go_g_own, go_g_got, ff_sum
    )
    arrived = arrived + [arrivals]

    go_sum = [Piece(go_g_own), Piece(go_g_got)]
    for phase in range(4, phases + 1):
        arrivals = hop(states, arrived, phase, True)
        if phase == 4:
            go_first = shrink(go_sum, 0, 1)
            ff_sum = ff_sum + shrink(ff_sum, 2)
        states, arrived, arrivals, go_sum, go_first, ff_sum = sync(
            states, arrived, arrivals, go_sum, go_first, ff_sum
        )
        arrived = arrived + [arrivals]
    after_own, after_oth = end_states(states, arrived)
    after_own, after_oth, go_sum, ff_sum = sync(after_own, after_oth, go_sum, ff_sum)
    go_sum = go_sum + go_first + shrink(go_sum, 0, 0)
    for turn in range(3, last + 1):
        ff_sum = ff_sum + shrink(ff_sum, turn)

    grad_k, grad_v, kv_g_own, kv_g_oth = call(
        last_kernel,
        H,
        info,
        [
            rates_in, whole(normed_t), head_in(key), head_in(value), head_in(key_part),
            head_in(value_part), whole(cosine), whole(sine), whole(tall_count),
            own_in(after_own), other_in(after_oth),
        ],
        [
            head_out(per_head + (QK,), BF16), head_out(per_head + (VH,), BF16),
            whole_out(grad_shape + (1536,), BF16), whole_out(grad_shape + (1536,), BF16),
        ],
        [],
        8 * unit,
        "last",
        32,
    )
    ff_sum, go_sum, kv_g_own, kv_g_oth, grad_k, grad_v = sync(
        ff_sum, go_sum, kv_g_own, kv_g_oth, grad_k, grad_v
    )
    kv_g_got = swap(kv_g_oth, 1)
    kv_g_own, kv_g_got, go_sum = sync(kv_g_own, kv_g_got, go_sum)
    kv_sum = [Piece(kv_g_own), Piece(kv_g_got)]
    kv_first = shrink(kv_sum, 0, 1)
    go_next = shrink(go_sum, 1)
    input_grad, grad_first_gain, grad_first_bias = call(
        input_kernel,
        H,
        info,
        [
            whole(x), whole(first_gain), whole(grad_hidden), whole(norm_part),
            head_in(grad_k), head_in(grad_v),
            columns(qkv_own, 256, 2, True), columns(qkv_oth, 256, 2, False),
            columns(qkv_own, 512, 2, True), columns(qkv_oth, 512, 2, False),
        ],
        [
            whole_out((tokens, width), F32), whole_out((1, width), F32),
            whole_out((1, width), F32),
        ],
        [pltpu.VMEM((tokens, width), F32)],
        6 * unit,
        "input",
        56,
    )
    kv_sum, kv_first, go_sum, go_next, ff_sum, input_grad, grad_first_gain, grad_first_bias = sync(
        kv_sum, kv_first, go_sum, go_next, ff_sum, input_grad, grad_first_gain, grad_first_bias
    )
    small = [grad_first_gain, grad_first_bias, grad_second_gain, grad_second_bias, grad_group_gain]
    small = jnp.concatenate([part.reshape(count, -1) for part in small], axis=1)
    small = jnp.pad(small, ((0, 0), (0, lanes - edges[-1])))
    small = small.reshape((2,) * len(bits) + (1, lanes))

    def small_step(small, bit):
        turned = (place() // bit) % 2 == 1
        got = swap(jnp.where(turned, small[0], small[1]), bit)
        return jnp.where(turned, small[1], small[0]) + got

    kv_sum = kv_sum + kv_first
    go_sum = go_sum + go_next
    kv_second, kv_next = shrink(kv_sum, 0, 0), shrink(kv_sum, 1)
    go_next = shrink(go_sum, 2)
    for bit in bits[:1:-1]:
        small = small_step(small, bit)
    kv_sum, kv_second, kv_next, go_sum, go_next, small = sync(
        kv_sum, kv_second, kv_next, go_sum, go_next, small
    )
    kv_sum = kv_sum + kv_second + kv_next
    go_sum = go_sum + go_next
    kv_next = shrink(kv_sum, 2)
    for turn in range(3, last + 1):
        go_sum = go_sum + shrink(go_sum, turn)
    for bit in bits[1::-1]:
        small = small_step(small, bit)
    ff_grad = summed(ff_sum, 0, 1)[0]
    kv_sum, kv_next, small, ff_grad = sync(kv_sum, kv_next, small, ff_grad)
    kv_sum = kv_sum + kv_next
    for turn in range(3, last + 1):
        kv_sum = kv_sum + shrink(kv_sum, turn)
    small = [small[0, a:b] for a, b in zip(edges[:-1], edges[1:])]

    go_grad, kv_grad = summed(go_sum, 0, 1)[0], summed(kv_sum, 0, 1)[0]
    ff_mine, ff_got = finish_wide(ff_grad[:, :1024])
    go_mine, go_got = finish_wide(jnp.concatenate([go_grad[:, :1024], go_grad[:, 2048:]], axis=1))
    kv_mine, kv_got = finish_wide(kv_grad)

    def wide(mine, got, start, stop):
        return ordered(mine[:, start:stop], got[:, start:stop], 1)

    return (
        output.reshape(inputs.shape),
        input_grad.reshape(inputs.shape),
        small[0],
        small[1],
        wide(go_mine, go_got, 1024, 1536),
        wide(kv_mine, kv_got, 0, 512),
        wide(kv_mine, kv_got, 512, 1536),
        wide(go_mine, go_got, 0, 1024),
        small[4],
        finish_tall(go_grad[:, 1024:2048]),
        small[2],
        small[3],
        wide(ff_mine, ff_got, 0, 1024),
        finish_tall(ff_grad[:, 1024:2048]),
    )


def solution(mesh):
    return jax.shard_map(
        per_device,
        mesh=mesh,
        in_specs=(
            P(None, "dp", "seq", None),
            P(None, "dp", "seq"),
            P(("dp", "seq")),
            P(("dp", "seq")),
            P(("dp", "seq"), None),
            P(("dp", "seq"), None),
            P(("dp", "seq"), None),
            P(("dp", "seq"), None),
            P(("dp", "seq")),
            P(("dp", "seq"), None),
            P(("dp", "seq")),
            P(("dp", "seq")),
            P(("dp", "seq"), None),
            P(("dp", "seq"), None),
            P(None, "dp", "seq", None),
        ),
        out_specs=(
            P(None, "dp", "seq", None),
            P(None, "dp", "seq", None),
            P(("dp", "seq")),
            P(("dp", "seq")),
            P(("dp", "seq"), None),
            P(("dp", "seq"), None),
            P(("dp", "seq"), None),
            P(("dp", "seq"), None),
            P(("dp", "seq")),
            P(("dp", "seq"), None),
            P(("dp", "seq")),
            P(("dp", "seq")),
            P(("dp", "seq"), None),
            P(("dp", "seq"), None),
        ),
        check_vma=False,
    )
```

```python
import jax
import jax.numpy as jnp
from jax import lax
from jax.experimental import pallas as pl
from jax.experimental.pallas import tpu as pltpu
from jax.sharding import PartitionSpec as P

H = 4
QK = 256
VH = 512
AXES = ("dp", "seq")
F32 = jnp.float32
BF16 = jnp.bfloat16
FAR = 4
LONE, EDGE, EVEN = range(3)
MIB = 1024 * 1024


def mm(left, right):
    return lax.dot_general(left, right, (((1,), (0,)), ((), ())), preferred_element_type=F32)


def nt(left, right):
    return lax.dot_general(left, right, (((1,), (1,)), ((), ())), preferred_element_type=F32)


def tn(left, right):
    return lax.dot_general(left, right, (((0,), (0,)), ((), ())), preferred_element_type=F32)


def devices():
    return lax.axis_size("dp") * lax.axis_size("seq")


def place():
    return lax.axis_index("dp") * lax.axis_size("seq") + lax.axis_index("seq")


def swap(values, bit):
    return lax.ppermute(values, AXES, [(i, i ^ bit) for i in range(devices())])


def upper_core():
    return lax.axis_index("seq") % 2 == 1


def sync(*values):
    return lax.optimization_barrier(values)


def orders(kind):
    bits = [1 << k for k in range(1, devices().bit_length() - 1)]
    near = [bit for bit in bits if bit not in (2, FAR)]
    turned = near[1:] + near[:1]
    return {
        LONE: (near[:1] + [2] + near[1:] + [FAR], turned + [2, FAR]),
        EDGE: (near + [2, FAR], turned + [2, FAR]),
        EVEN: (near[:1] + [2] + near[1:] + [FAR], turned[:1] + [2] + turned[1:] + [FAR]),
    }[kind]


def step(values, turn, kind):
    pairs = [(i, i ^ orders(kind)[i % 2][turn]) for i in range(devices())]
    return lax.ppermute(values, AXES, pairs)


def chip_tables(kind):
    count = devices() // 2
    me, core = place() // 2, lax.axis_index("seq") % 2
    every = jnp.arange(count, dtype=jnp.int32)

    def spread_bits(values, sources, targets):
        return sum(((values >> s) & 1) << t for s, t in zip(sources, targets))

    spots, chips = [], []
    for order in orders(kind):
        sources = [bit.bit_length() - 2 for bit in order]
        targets = list(range(len(order)))[::-1]
        spots.append(spread_bits(every ^ me, sources, targets))
        chips.append(spread_bits(every, targets, sources) ^ me)
    swapped = core == 1
    return jnp.concatenate(
        [
            jnp.stack([me, core]),
            jnp.where(swapped, spots[1], spots[0]),
            jnp.where(swapped, spots[0], spots[1]),
            jnp.where(swapped, chips[1], chips[0]),
            jnp.where(swapped, chips[0], chips[1]),
        ]
    ).astype(jnp.int32)


def local(body, outs, *arrays, name):
    size = sum(a.size * a.dtype.itemsize for a in arrays)
    for shape, dtype in outs:
        extent = jnp.dtype(dtype).itemsize
        for length in shape:
            extent *= length
        size += extent

    def spec(shape):
        zeros = (0,) * len(shape)
        return pl.BlockSpec(shape, lambda k: zeros)

    return pl.pallas_call(
        body,
        grid=(1,),
        out_shape=[jax.ShapeDtypeStruct(shape, dtype) for shape, dtype in outs],
        in_specs=[
            pl.BlockSpec(memory_space=pltpu.SMEM) if a.dtype == jnp.int32 else spec(a.shape)
            for a in arrays
        ],
        out_specs=[spec(shape) for shape, _ in outs],
        compiler_params=pltpu.CompilerParams(vmem_limit_bytes=2 * size + 4 * MIB),
        cost_estimate=pl.CostEstimate(flops=1, bytes_accessed=1, transcendentals=0),
        name=name,
    )(*arrays)


def pack(info, *weights):
    width = sum(w.shape[1] for w in weights) // 2
    shape = (weights[0].shape[0], width)

    def body(info_ref, *refs):
        keep, give = refs[-2:]
        at = 0
        for ref in refs[:-2]:
            half = ref.shape[1] // 2
            here = pl.multiple_of(info_ref[1] * half, 128)
            there = pl.multiple_of((1 - info_ref[1]) * half, 128)
            keep[:, at : at + half] = ref[:, pl.ds(here, half)]
            give[:, at : at + half] = ref[:, pl.ds(there, half)]
            at += half

    return local(body, [(shape, BF16)] * 2, info, *weights, name="pack")


def stack_rows(info, keep, got):
    rows, width = keep.shape

    def body(info_ref, keep_ref, got_ref, out):
        upper = info_ref[1] == 1
        out[:rows] = jnp.where(upper, got_ref[...], keep_ref[...])
        out[rows:] = jnp.where(upper, keep_ref[...], got_ref[...])

    return local(body, [((2 * rows, width), BF16)], info, keep, got, name="stack")[0]


def join(part, got):
    half = part.shape[0]

    def body(part_ref, got_ref, out):
        out[:half] = part_ref[...]
        out[half:] = got_ref[...]

    outs = [((2 * half,) + part.shape[1:], BF16)]
    return local(body, outs, part, got, name="join")[0]


def settle(info, pieces, own):
    lengths = [piece.shape[0] for piece in pieces]
    chips = sum(lengths)

    def body(info_ref, *refs):
        at = 0
        for ref, length in zip(refs, lengths):
            for block in range(length):
                refs[-1][info_ref[2 + (2 if own else 3) * chips + at]] = ref[block]
                at += 1

    outs = [((chips,) + pieces[0].shape[1:], BF16)]
    return local(body, outs, info, *pieces, name="settle")[0]


@jax.tree_util.register_pytree_node_class
class Piece:
    def __init__(self, array, start=0):
        self.array, self.start = array, start

    def tree_flatten(self):
        return (self.array,), self.start

    @classmethod
    def tree_unflatten(cls, start, children):
        return cls(children[0], start)


def summed(pieces, start, stop):
    total = None
    for piece in pieces:
        first, last = start - piece.start, stop - piece.start
        if 0 <= first and last <= piece.array.shape[0]:
            value = piece.array[first:last].astype(F32)
            total = value if total is None else total + value
    return total


def span(turn):
    length = devices() // 2 >> turn
    return length // 2, length


def upper_part(pieces, turn, part=None):
    start, stop = span(turn)
    shift = start
    if part is not None:
        middle = (start + stop) // 2
        start, stop = (middle, stop) if part else (start, middle)
    return Piece(summed(pieces, start, stop).astype(BF16), start - shift)


def send(piece, turn, kind):
    return [Piece(step(piece.array, turn, kind), piece.start)]


def shrink(pieces, turn, kind, part=None):
    return send(upper_part(pieces, turn, part), turn, kind)


def ordered(mine, other, axis):
    upper = upper_core()
    return jnp.concatenate(
        [jnp.where(upper, other, mine), jnp.where(upper, mine, other)], axis=axis
    )


def finish_wide(values):
    rows = values.shape[0] // 2
    upper = upper_core()
    low, high = values[:rows], values[rows:]
    mine, give = jnp.where(upper, high, low), jnp.where(upper, low, high)
    return mine, swap(give, 1)


def finish_tall(values):
    half = values.shape[1] // 2
    upper = upper_core()
    low, high = values[:, :half], values[:, half:]
    mine, give = jnp.where(upper, high, low), jnp.where(upper, low, high)
    return ordered(mine, swap(give, 1), 1)


def phase_count(rows):
    return lax.axis_size("seq") // 2 - 1 + rows - 1


def chip_place(reverse):
    chips = lax.axis_size("seq") // 2
    at = lax.axis_index("seq") // 2
    return chips - 1 - at if reverse else at


def row_at(phase, rows, reverse):
    return jnp.clip(phase - 1 - chip_place(reverse), 0, rows - 1)


def factors_of(carry, near_carry, reverse):
    rows = carry.shape[0]
    upper = upper_core()
    turned = jnp.logical_not(upper) if reverse else upper
    one, zero = jnp.ones_like(carry), jnp.zeros_like(carry)

    def either(yes, no):
        return jnp.where(turned, yes, no)

    table = (either(one, near_carry), either(carry, one), carry * near_carry)
    passed = []
    for phase in range(1, phase_count(rows) + 1):
        row = row_at(phase, rows, reverse)
        passed.append([
            sum(jnp.where(row == k, factor[k], 0.0) for k in range(rows))[:, None, None]
            for factor in table
        ])
    mine = (either(zero, zero), either(one, zero), either(near_carry, one))
    theirs = (either(zero, one), either(zero, zero), either(one, carry))
    return passed, [[f[:, :, None, None] for f in side] for side in (mine, theirs)]


def hop(states, arrived, phase, reverse):
    passed, _, own, near = states
    rows = own.shape[0]
    row = row_at(phase, rows, reverse)
    a, b, c = passed[phase - 1]
    message = a * lax.dynamic_index_in_dim(own, row, 0, False)
    message = message + b * lax.dynamic_index_in_dim(near, row, 0, False)
    if arrived:
        message = message + c * arrived[-1].astype(F32)
    chips = lax.axis_size("seq") // 2
    pairs = []
    for at in range(chips - 1):
        if 0 <= phase - 1 - at < rows:
            source, target = (chips - 1 - at, chips - 2 - at) if reverse else (at, at + 1)
            pairs += [(2 * source + core, 2 * target + core) for core in range(2)]
    return lax.ppermute(message.astype(BF16), "seq", pairs)


def end_states(states, arrived, reverse):
    _, (mine, theirs), own, near = states
    at = chip_place(reverse)
    chips = lax.axis_size("seq") // 2
    before = []
    for row in range(own.shape[0]):
        value = jnp.zeros_like(arrived[0])
        for other in range(1, chips):
            value = jnp.where(at == other, arrived[row + other - 1], value)
        before.append(value.astype(F32))
    before = jnp.stack(before)

    def taken(factors):
        a, b, c = factors
        return (a * own + b * near + c * before).astype(BF16)

    return taken(mine), swap(taken(theirs), 1)


def call(body, grid, info, ins, outs, scratch, flops, name, vmem):
    def spec(shape, block, index, once):
        if block is None:
            return pl.BlockSpec(memory_space=pltpu.SMEM)
        if once and block == shape and name == "feed":
            return pl.BlockSpec(block, index, pipeline_mode=pl.Buffered(1))
        return pl.BlockSpec(block, index)

    moved = sum(a.size * a.dtype.itemsize for a, _, _ in ins)
    for shape, dtype, _, _ in outs:
        size = jnp.dtype(dtype).itemsize
        for extent in shape:
            size *= extent
        moved += size
    return pl.pallas_call(
        body,
        grid_spec=pltpu.PrefetchScalarGridSpec(
            num_scalar_prefetch=1,
            grid=(grid,),
            in_specs=[spec(a.shape, block, index, True) for a, block, index in ins],
            out_specs=[spec(shape, block, index, False) for shape, _, block, index in outs],
            scratch_shapes=scratch,
        ),
        out_shape=[jax.ShapeDtypeStruct(shape, dtype) for shape, dtype, _, _ in outs],
        compiler_params=pltpu.CompilerParams(
            vmem_limit_bytes=vmem * MIB, dimension_semantics=("arbitrary",)
        ),
        cost_estimate=pl.CostEstimate(flops=1, bytes_accessed=1, transcendentals=0),
        name=name,
    )(info, *[a for a, _, _ in ins])


def whole(array):
    zeros = (0,) * array.ndim
    return (array, array.shape, lambda h, info: zeros)


def whole_out(shape, dtype):
    zeros = (0,) * len(shape)
    return (shape, dtype, shape, lambda h, info: zeros)


def head_in(array):
    rest = (0,) * (array.ndim - 1)
    return (array, (1,) + array.shape[1:], lambda h, info: (h,) + rest)


def head_out(shape, dtype):
    rest = (0,) * (len(shape) - 1)
    return (shape, dtype, (1,) + shape[1:], lambda h, info: (h,) + rest)


def state_block(shape, own):
    block = (shape[0], 1) + shape[2:]
    if own:
        return block, lambda h, info: (0, jnp.minimum(h, 1), 0, 0)
    return block, lambda h, info: (0, jnp.maximum(h - 2, 0), 0, 0)


def own_in(array):
    return (array,) + state_block(array.shape, True)


def other_in(array):
    return (array,) + state_block(array.shape, False)


def own_out(shape, dtype):
    return (shape, dtype) + state_block(shape, True)


def other_out(shape, dtype):
    return (shape, dtype) + state_block(shape, False)


def real(h, info):
    return lax.rem(h + 2 * info[1], 4)


def real_in(array):
    rest = (0,) * (array.ndim - 1)
    return (array, (1,) + array.shape[1:], lambda h, info: (real(h, info),) + rest)


def columns(array, width, first, own):
    block = array.shape[:2] + (width,)
    if own:
        return (array, block, lambda h, info: (0, 0, first + jnp.minimum(h, 1)))
    return (array, block, lambda h, info: (0, 0, first + jnp.maximum(h - 2, 0)))


def tall(array):
    block = (array.shape[0] // 4, array.shape[1], 1024)
    return (array, block, lambda h, info: (real(h, info), 0, 1))


def tall_rows(ref):
    chips = ref.shape[0]
    pieces = []
    for chip in range(chips):
        pieces += [ref[chip, :, :512], ref[chip, :, 512:]]
    return jnp.concatenate(pieces, axis=0)


def flat(ref):
    chips, rows, width = ref.shape
    return ref[...].reshape(chips * rows, width)


def side(info, own):
    return pl.multiple_of(512 * (info[1] if own else 1 - info[1]), 512)


def put_wide(target, info, values, start, own):
    chips, rows, _ = target.shape
    width = values.shape[1]
    values = values.astype(BF16)
    for chip in range(chips):
        target[info[(2 if own else 2 + chips) + chip], :, start : start + width] = values[chip * rows : (chip + 1) * rows]


def put_tall(target, info, values, block, start, own):
    chips, rows, _ = target.shape
    values = values.astype(BF16)
    share = chips // 4
    for chip in range(share):
        at = info[(2 if own else 2 + chips) + block * share + chip]
        base = 2 * rows * chip
        target[at, :, start : start + 512] = values[base : base + rows]
        target[at, :, start + 512 : start + 1024] = values[base + rows : base + 2 * rows]


def rotated(values, cosine, sine):
    a, b = values[:, :128], values[:, 128:]
    return jnp.concatenate([a * cosine - b * sine, b * cosine + a * sine], axis=1)


def unrotated(values, cosine, sine):
    a, b = values[:, :128], values[:, 128:]
    return jnp.concatenate([a * cosine + b * sine, b * cosine - a * sine], axis=1)


def mask_of(rate, tall_count, wide_count):
    length = tall_count.shape[0]
    i = lax.broadcasted_iota(jnp.int32, (length, length), 0)
    s = lax.broadcasted_iota(jnp.int32, (length, length), 1)
    decay = jnp.exp((i - s).astype(F32) * rate)
    return jnp.where((tall_count == wide_count) & (i >= s), decay, 0.0)


def enter_of(rate, tall_count):
    i = lax.broadcasted_iota(jnp.int32, tall_count.shape, 0)
    return jnp.where(tall_count == 0, jnp.exp((i + 1).astype(F32) * rate), 0.0)


def leave_of(rate, tall_count):
    length = tall_count.shape[0]
    i = lax.broadcasted_iota(jnp.int32, tall_count.shape, 0)
    last = tall_count[length - 1 :, :]
    return jnp.where(tall_count == last, jnp.exp((length - 1 - i).astype(F32) * rate), 0.0)


def norm_parts(values, eps):
    average = jnp.mean(values, axis=-1, keepdims=True)
    centred = values - average
    spread_ = jnp.mean(centred * centred, axis=-1, keepdims=True)
    scale = lax.rsqrt(spread_ + eps)
    return centred * scale, scale


def norm_back(grad, normal, scale):
    first = jnp.mean(grad, axis=-1, keepdims=True)
    second = jnp.mean(grad * normal, axis=-1, keepdims=True)
    return scale * (grad - first - normal * second)


CHUNK = 64


def norm_kernel(info, x, gain, bias, normed, normed_t):
    @pl.loop(0, x.shape[0] // CHUNK)
    def _(k):
        at = pl.ds(pl.multiple_of(k * CHUNK, CHUNK), CHUNK)
        normal, _ = norm_parts(x[at, :].astype(F32), 1e-05)
        normed[at, :] = (normal * gain[...].astype(F32) + bias[...].astype(F32)).astype(BF16)

    normed_t[...] = normed[...].T


def project_kernel(
    info, rates, normed, cosine, sine, tall_count, wide_count,
    q_own, k_own, v_own, q_oth, k_oth, v_oth,
    q_out, k_out, v_out, mix_out, inner_out, sum_own, sum_oth, pre,
):
    h = pl.program_id(0)

    def fill(wq, wk, wv):
        left = normed[...]
        pre[:, :256] = mm(left, flat(wq))
        pre[:, 256:512] = mm(left, flat(wk))
        pre[:, 512:] = mm(left, flat(wv))

    @pl.when(h < 2)
    def _():
        fill(q_own, k_own, v_own)

    @pl.when(h >= 2)
    def _():
        fill(q_oth, k_oth, v_oth)

    rate = rates[h]
    length = cosine.shape[0]
    for row in range(tall_count.shape[0]):
        at = slice(row * length, (row + 1) * length)
        count = tall_count[row]
        query = rotated(pre[at, :256], cosine[...], sine[...]).astype(BF16)
        key = (rotated(pre[at, 256:512], cosine[...], sine[...]) * QK**-0.5).astype(BF16)
        value = pre[at, 512:].astype(BF16)
        q_out[0, at] = query
        k_out[0, at] = key
        v_out[0, at] = value
        mixing = (nt(query, key) * mask_of(rate, count, wide_count[row])).astype(BF16)
        mix_out[0, at] = mixing
        inner_out[0, at] = mm(mixing, value)
        weighted = (key.astype(F32) * leave_of(rate, count)).astype(BF16)
        summary = tn(weighted, value)

        @pl.when(h < 2)
        def _():
            sum_own[row, 0] = summary

        @pl.when(h >= 2)
        def _():
            sum_oth[row, 0] = summary


def gate_kernel(info, normed, own, oth, out):
    h = pl.program_id(0)

    @pl.when(h < 2)
    def _():
        out[0] = mm(normed[...], flat(own))

    @pl.when(h >= 2)
    def _():
        out[0] = mm(normed[...], flat(oth))


def mix_kernel(
    info, rates, x, gain, second_gain, second_bias, tall_count, query, inner, gate,
    state_own, state_oth, wo_own, wo_oth,
    retained, mixed_t, hidden, normed, normed_t,
):
    h = pl.program_id(0)
    rate = rates[h]
    length = tall_count.shape[1]

    @pl.when(h == 0)
    def _():
        hidden[...] = x[...].astype(F32)

    for row in range(tall_count.shape[0]):
        at = slice(row * length, (row + 1) * length)
        entered = (query[0, at].astype(F32) * enter_of(rate, tall_count[row])).astype(BF16)

        @pl.when(h < 2)
        def _():
            retained[0, at] = inner[0, at] + mm(entered, state_own[row, 0])

        @pl.when(h >= 2)
        def _():
            retained[0, at] = inner[0, at] + mm(entered, state_oth[row, 0])

    normal, _ = norm_parts(retained[0], 1.0)
    pre = gate[0]
    mixed = (pre / (1.0 + jnp.exp(-pre)) * (normal * gain[0].astype(F32))).astype(BF16)
    mixed_t[0] = mixed.T
    hidden[:, pl.ds(side(info, True), 512)] += mm(mixed, tall_rows(wo_own))
    hidden[:, pl.ds(side(info, False), 512)] += mm(mixed, tall_rows(wo_oth))

    @pl.when(h == 3)
    def _():
        @pl.loop(0, x.shape[0] // CHUNK)
        def _(k):
            at = pl.ds(pl.multiple_of(k * CHUNK, CHUNK), CHUNK)
            normal, _ = norm_parts(hidden[at, :], 1e-05)
            normed[at, :] = (
                normal * second_gain[...].astype(F32) + second_bias[...].astype(F32)
            ).astype(BF16)

        normed_t[...] = normed[...].T


def feed_kernel(
    info, hidden, normed, normed_t, cot, second_gain,
    up_own, up_oth, down_own, down_oth,
    output, grad_hidden, grad_low, grad_gain, grad_bias, g_own, g_oth,
    upward, out_sum, norm_sum,
):
    f = pl.program_id(0)
    own_at = pl.ds(side(info, True), 512)
    oth_at = pl.ds(side(info, False), 512)

    @pl.when(f == 0)
    def _():
        out_sum[...] = hidden[...]
        norm_sum[...] = jnp.zeros_like(norm_sum)

    @pl.when(f < 2)
    def _():
        upward[...] = mm(normed[...], flat(up_own))

    @pl.when(f >= 2)
    def _():
        upward[...] = mm(normed[...], flat(up_oth))

    up = upward[...]
    root = 0.7978845608028654
    squared = up * up
    bent = jnp.tanh(root * (up + 0.044715 * (squared * up)))
    activated = (0.5 * up * (1.0 + bent)).astype(BF16)
    slope = 0.5 * (1.0 + bent) + 0.5 * up * (1.0 - bent * bent) * (
        root * (1.0 + 3 * 0.044715 * squared)
    )
    own, oth = tall_rows(down_own), tall_rows(down_oth)
    out_sum[:, own_at] += mm(activated, own)
    out_sum[:, oth_at] += mm(activated, oth)
    grad_up = (slope * (nt(cot[:, own_at], own) + nt(cot[:, oth_at], oth))).astype(BF16)
    block = real(f, info)
    act_t = activated.T
    put_tall(g_own, info, mm(act_t, cot[:, own_at]), block, 1024, True)
    put_tall(g_oth, info, mm(act_t, cot[:, oth_at]), block, 1024, False)
    grad_w = mm(normed_t[...], grad_up)
    for step in range(4):

        @pl.when(f == step)
        def _():
            put_wide(g_own if step < 2 else g_oth, info, grad_w, 512 * (step % 2), step < 2)

    @pl.when(f < 2)
    def _():
        norm_sum[...] += nt(grad_up, flat(up_own))

    @pl.when(f >= 2)
    def _():
        norm_sum[...] += nt(grad_up, flat(up_oth))

    @pl.when(f == 3)
    def _():
        grad_gain[...] = jnp.zeros_like(grad_gain)
        grad_bias[...] = jnp.zeros_like(grad_bias)

        @pl.loop(0, hidden.shape[0] // CHUNK)
        def _(k):
            at = pl.ds(pl.multiple_of(k * CHUNK, CHUNK), CHUNK)
            output[at, :] = out_sum[at, :].astype(BF16)
            normal, scale = norm_parts(hidden[at, :], 1e-05)
            grad = norm_sum[at, :]
            grad_gain[...] += jnp.sum(grad * normal, axis=0, keepdims=True)
            grad_bias[...] += jnp.sum(grad, axis=0, keepdims=True)
            total = cot[at, :].astype(F32) + norm_back(
                grad * second_gain[...].astype(F32), normal, scale
            )
            grad_hidden[at, :] = total
            grad_low[at, :] = total.astype(BF16)


def unmix_kernel(
    info, rates, grad_low, gain, tall_count, query, retained, gate, wo_own, wo_oth,
    grad_ret, grad_gate, grad_gain, state_own, state_oth,
):
    h = pl.program_id(0)
    rate = rates[h]
    length = tall_count.shape[1]
    grad = nt(grad_low[:, pl.ds(side(info, True), 512)], tall_rows(wo_own)) + nt(
        grad_low[:, pl.ds(side(info, False), 512)], tall_rows(wo_oth)
    )
    normal, scale = norm_parts(retained[0], 1.0)
    pre = gate[0]
    share = 1.0 / (1.0 + jnp.exp(-pre))
    curve = pre * share
    scaled = gain[0].astype(F32)
    grad_gate[0] = (grad * (normal * scaled) * (share * (1.0 + pre * (1.0 - share)))).astype(BF16)
    grad_normal = grad * curve
    grad_gain[0] = jnp.sum(grad_normal * normal, axis=0, keepdims=True)
    grad_ret[0] = norm_back(grad_normal * scaled, normal, scale).astype(BF16)
    for row in range(tall_count.shape[0]):
        at = slice(row * length, (row + 1) * length)
        entered = (query[0, at].astype(F32) * enter_of(rate, tall_count[row])).astype(BF16)
        state = tn(entered, grad_ret[0, at])

        @pl.when(h < 2)
        def _():
            state_own[row, 0] = state

        @pl.when(h >= 2)
        def _():
            state_oth[row, 0] = state


def inside_kernel(
    info, rates, grad_ret, query, key, value, mixing,
    cosine, sine, tall_count, wide_count, state_own, state_oth,
    grad_q, key_part, value_part,
):
    h = pl.program_id(0)
    rate = rates[h]
    length = cosine.shape[0]
    for row in range(tall_count.shape[0]):
        at = slice(row * length, (row + 1) * length)
        grad = grad_ret[0, at]
        mask = mask_of(rate, tall_count[row], wide_count[row])
        scores = (nt(grad, value[0, at]) * mask).astype(BF16)
        enter = enter_of(rate, tall_count[row])

        def set_query(state):
            total = mm(scores, key[0, at]) + nt(grad, state[row, 0]) * enter
            grad_q[0, at] = unrotated(total, cosine[...], sine[...]).astype(BF16)

        @pl.when(h < 2)
        def _():
            set_query(state_own)

        @pl.when(h >= 2)
        def _():
            set_query(state_oth)

        key_part[0, at] = tn(scores, query[0, at])
        value_part[0, at] = tn(mixing[0, at], grad)


def outer_kernel(
    info, grad_low, normed_t, mixed_t, grad_gate, grad_q, out_own, out_oth,
):
    h = pl.program_id(0)
    block = real(h, info)
    left = mixed_t[0]
    put_tall(out_own, info, mm(left, grad_low[:, pl.ds(side(info, True), 512)]), block, 1024, True)
    put_tall(out_oth, info, mm(left, grad_low[:, pl.ds(side(info, False), 512)]), block, 1024, False)
    grad_wg = mm(normed_t[...], grad_gate[0])
    grad_wq = mm(normed_t[...], grad_q[0])
    for step in range(4):

        @pl.when(h == step)
        def _():
            target = out_own if step < 2 else out_oth
            put_wide(target, info, grad_wg, 512 * (step % 2), step < 2)
            put_wide(target, info, grad_wq, 2048 + 256 * (step % 2), step < 2)


def last_kernel(
    info, rates, normed_t, key, value, key_part, value_part, cosine, sine, tall_count,
    state_own, state_oth,
    grad_k, grad_v, out_own, out_oth,
):
    h = pl.program_id(0)
    rate = rates[h]
    length = cosine.shape[0]
    for row in range(tall_count.shape[0]):
        at = slice(row * length, (row + 1) * length)
        leave = leave_of(rate, tall_count[row])
        weighted = (key[0, at].astype(F32) * leave).astype(BF16)

        def set_both(state):
            low = state[row, 0]
            grad_v[0, at] = (value_part[0, at] + mm(weighted, low)).astype(BF16)
            total = key_part[0, at] + nt(value[0, at], low) * leave
            grad_k[0, at] = (unrotated(total, cosine[...], sine[...]) * QK**-0.5).astype(BF16)

        @pl.when(h < 2)
        def _():
            set_both(state_own)

        @pl.when(h >= 2)
        def _():
            set_both(state_oth)

    grad_wk = mm(normed_t[...], grad_k[0])
    grad_wv = mm(normed_t[...], grad_v[0])
    for step in range(4):

        @pl.when(h == step)
        def _():
            target = out_own if step < 2 else out_oth
            put_wide(target, info, grad_wk, 256 * (step % 2), step < 2)
            put_wide(target, info, grad_wv, 512 + 512 * (step % 2), step < 2)


def input_kernel(
    info, x, gain, grad_hidden, grad_q, grad_k, grad_v, grad_gate,
    q_own, q_oth, k_own, k_oth, v_own, v_oth, g_own, g_oth,
    input_grad, grad_gain, grad_bias, norm_sum,
):
    h = pl.program_id(0)

    @pl.when(h == 0)
    def _():
        norm_sum[...] = jnp.zeros_like(norm_sum)

    def add(wq, wk, wv, wg):
        norm_sum[...] += (
            nt(grad_q[0], flat(wq)) + nt(grad_k[0], flat(wk))
            + nt(grad_v[0], flat(wv)) + nt(grad_gate[0], flat(wg))
        )

    @pl.when(h < 2)
    def _():
        add(q_own, k_own, v_own, g_own)

    @pl.when(h >= 2)
    def _():
        add(q_oth, k_oth, v_oth, g_oth)

    @pl.when(h == 3)
    def _():
        grad_gain[...] = jnp.zeros_like(grad_gain)
        grad_bias[...] = jnp.zeros_like(grad_bias)

        @pl.loop(0, x.shape[0] // CHUNK)
        def _(k):
            at = pl.ds(pl.multiple_of(k * CHUNK, CHUNK), CHUNK)
            normal, scale = norm_parts(x[at, :].astype(F32), 1e-05)
            grad = norm_sum[at, :]
            grad_gain[...] += jnp.sum(grad * normal, axis=0, keepdims=True)
            grad_bias[...] += jnp.sum(grad, axis=0, keepdims=True)
            input_grad[at, :] = grad_hidden[at, :] + norm_back(
                grad * gain[...].astype(F32), normal, scale
            )


def per_device(
    inputs,
    doc_flags,
    first_gain,
    first_bias,
    w_query,
    w_key,
    w_value,
    w_gate,
    group_gain,
    w_output,
    second_gain,
    second_bias,
    w_up,
    w_down,
    cotangent,
):
    batches, row_count, length, width = inputs.shape
    rows = batches * row_count
    tokens = rows * length
    count = devices()
    chips = count // 2
    info, info_edge = chip_tables(LONE), chip_tables(EDGE)
    x = inputs.reshape(tokens, width)
    cot = cotangent.reshape(tokens, width)

    upper = upper_core()
    share = w_query.shape[0]
    last = len(orders(LONE)[0]) - 1

    keep, give = pack(info, w_query, w_key, w_value)
    qkv = stack_rows(info, keep, swap(give, 1))
    vectors = [first_gain, first_bias, second_gain, second_bias, group_gain]
    qkv, vectors = sync(qkv, vectors)
    got_qkv = step(qkv[None], last, LONE)

    sizes = [v.shape[0] for v in vectors]
    edges = [sum(sizes[:k]) for k in range(len(sizes) + 1)]
    lanes = -(-edges[-1] // 128) * 128
    table = jnp.concatenate([v.reshape(1, -1) for v in vectors], axis=1)
    table = jnp.pad(table, ((0, 15), (0, lanes - edges[-1])))

    def table_step(table, done, bit):
        got = swap(table, bit)
        turned = (place() // bit) % 2 == 1
        spot = sum(1 for other in done if other > bit)
        done.append(bit)
        return jnp.stack(
            [jnp.where(turned, got, table), jnp.where(turned, table, got)], axis=spot
        )

    bits = [1 << k for k in range(count.bit_length() - 1)]
    done = []
    for bit in (1, FAR):
        table = table_step(table, done, bit)
    got_qkv, table = sync(got_qkv, table)
    part, got = qkv[None], got_qkv
    for turn in range(last - 1, 1, -1):
        part = join(part, got)
        got = step(part, turn, LONE)
        if turn == last - 1:
            table = table_step(table, done, 2)
        part, got, table, w_gate, w_up, w_output, w_down, doc_flags = sync(
            part, got, table, w_gate, w_up, w_output, w_down, doc_flags
        )

    part = join(part, got)
    got = step(part, 1, LONE)
    for bit in bits[:2:-1]:
        table = table_step(table, done, bit)

    top_keep, top_give = pack(info, w_gate, w_up)
    tall_keep, tall_give = pack(info, w_output, w_down)
    top = stack_rows(info, top_keep, swap(top_give, 1))
    tall_got = swap(tall_give, 1)
    low, high = jnp.where(upper, tall_got, tall_keep), jnp.where(upper, tall_keep, tall_got)
    go = jnp.concatenate([top[:, :1024], low[:, :512], high[:, :512]], axis=1)
    ff = jnp.concatenate([top[:, 1024:], low[:, 512:], high[:, 512:]], axis=1)
    go_part, ff_part = go[None], ff[None]
    part, got, go_part, ff_part, table, doc_flags = sync(
        part, got, go_part, ff_part, table, doc_flags
    )

    pieces = [part, got, step(part, 0, LONE), step(got, 0, LONE)]
    go_got = step(go_part, last, EDGE)
    ff_got = step(ff_part, last, EDGE)
    vector = table.reshape(count, -1, lanes)[:, 0]
    first_gain, first_bias, second_gain, second_bias, group_gain = [
        vector[:, a:b].reshape(1, -1) for a, b in zip(edges[:-1], edges[1:])
    ]
    group_gain = group_gain.reshape(H, 1, VH)

    positions = lax.axis_index("seq") * length + jnp.arange(length, dtype=jnp.int32)
    frequency = 10000.0 ** (-jnp.arange(QK // 2, dtype=F32) / (QK // 2))
    angles = positions.astype(F32)[:, None] * frequency[None, :]
    cosine, sine = jnp.cos(angles), jnp.sin(angles)
    rates = jnp.log1p(-(2.0 ** (-5.0 - 3.0 * jnp.arange(H, dtype=F32))))
    rates = jnp.where(upper, jnp.roll(rates, 2), rates)
    counts = jnp.cumsum(doc_flags.reshape(rows, length), axis=-1, dtype=jnp.int32)
    tall_count, wide_count = counts[:, :, None], counts[:, None, :]
    open_row = (counts[:, -1] == 0).astype(F32)
    near_row = swap(open_row, 1)
    decay = jnp.exp(rates[:2] * float(length))
    carry, near_carry = decay[None] * open_row[:, None], decay[None] * near_row[:, None]
    ahead = factors_of(carry, near_carry, False)
    behind = factors_of(carry, near_carry, True)

    per_head = (H, tokens)
    state_shape = (rows, 2, QK, VH)
    grad_shape = (chips, 2 * share)
    rates_in = (rates, None, None)
    unit = 2.0 * tokens * width * 512

    normed, normed_t = call(
        norm_kernel,
        1,
        info,
        [whole(x), whole(first_gain), whole(first_bias)],
        [whole_out((tokens, width), BF16), whole_out((width, tokens), BF16)],
        [],
        unit / 100,
        "norm",
        16,
    )
    pieces, go_part, go_got, ff_part, ff_got, normed, normed_t, tables, gains = sync(
        pieces, go_part, go_got, ff_part, ff_got, normed, normed_t,
        (cosine, sine, tall_count, wide_count, ahead, behind, rates),
        (second_gain, second_bias, group_gain),
    )
    cosine, sine, tall_count, wide_count, ahead, behind, rates = tables
    second_gain, second_bias, group_gain = gains
    rates_in = (rates, None, None)

    qkv_own = settle(info, pieces, True)
    qkv_oth = swap(qkv_own, 1)
    go_part = join(go_part, go_got)
    go_got = step(go_part, last - 1, EDGE)
    qkv_own, qkv_oth, go_part, go_got, ff_part, ff_got = sync(
        qkv_own, qkv_oth, go_part, go_got, ff_part, ff_got
    )

    go_part = join(go_part, go_got)
    go_got = step(go_part, last - 2, EDGE)
    ff_part = join(ff_part, ff_got)
    ff_got = step(ff_part, last - 1, EDGE)
    (query, key, value, mixing, inner, sum_own, sum_oth) = call(
        project_kernel,
        H,
        info,
        [
            rates_in, whole(normed), whole(cosine), whole(sine),
            whole(tall_count), whole(wide_count),
            columns(qkv_own, 256, 0, True), columns(qkv_own, 256, 2, True),
            columns(qkv_own, 512, 2, True),
            columns(qkv_oth, 256, 0, False), columns(qkv_oth, 256, 2, False),
            columns(qkv_oth, 512, 2, False),
        ],
        [
            head_out(per_head + (QK,), BF16), head_out(per_head + (QK,), BF16),
            head_out(per_head + (VH,), BF16), head_out(per_head + (length,), BF16),
            head_out(per_head + (VH,), F32),
            own_out(state_shape, F32), other_out(state_shape, F32),
        ],
        [pltpu.VMEM((tokens, 1024), F32)],
        10 * unit,
        "project",
        56,
    )
    go_part, go_got, ff_part, ff_got, sum_own, sum_oth = sync(
        go_part, go_got, ff_part, ff_got, sum_own, sum_oth
    )
    for turn in range(last - 3, 0, -1):
        go_part = join(go_part, go_got)
        go_got = step(go_part, turn, EDGE)
        ff_part = join(ff_part, ff_got)
        ff_got = step(ff_part, turn + 1, EDGE)
        go_part, go_got, ff_part, ff_got = sync(go_part, go_got, ff_part, ff_got)
    sum_near = swap(sum_oth, 1)
    sum_own, sum_near, go_part, go_got, ff_part, ff_got = sync(
        sum_own, sum_near, go_part, go_got, ff_part, ff_got
    )

    states = tuple(ahead) + (sum_own, sum_near)
    phases = phase_count(rows)
    arrivals = hop(states, [], 1, False)
    go_first = step(go_part, 0, EDGE)
    states, arrivals, go_part, go_got, go_first = sync(
        states, arrivals, go_part, go_got, go_first
    )
    arrived = [arrivals]

    arrivals = hop(states, arrived, 2, False)
    go_second = step(go_got, 0, EDGE)
    states, arrived, arrivals, pieces, ff_part, ff_got = sync(
        states, arrived, arrivals, [go_part, go_got, go_first, go_second], ff_part, ff_got
    )
    arrived = arrived + [arrivals]

    arrivals = hop(states, arrived, 3, False)
    ff_part = join(ff_part, ff_got)
    ff_got = step(ff_part, 1, EDGE)
    states, arrived, arrivals, pieces, ff_part, ff_got = sync(
        states, arrived, arrivals, pieces, ff_part, ff_got
    )
    arrived = arrived + [arrivals]

    for phase in range(4, phases + 1):
        arrivals = hop(states, arrived, phase, False)
        if phase == 4:
            ff_first = step(ff_part, 0, EDGE)
            ff_others = [swap(ff_part, 1), swap(ff_got, 1)]
            go_own = settle(info_edge, pieces, True)
            go_oth = swap(go_own, 1)
        states, arrived, arrivals, go_own, go_oth, normed, ff_part, ff_got, ff_first, ff_others = (
            sync(
                states, arrived, arrivals, go_own, go_oth, normed, ff_part, ff_got, ff_first,
                ff_others,
            )
        )
        arrived = arrived + [arrivals]
    state_own, state_oth = end_states(states, arrived, False)
    (gate,) = call(
        gate_kernel,
        H,
        info,
        [whole(normed), columns(go_own, 512, 0, True), columns(go_oth, 512, 0, False)],
        [head_out(per_head + (VH,), F32)],
        [],
        4 * unit,
        "gate",
        20,
    )
    state_own, state_oth, gate, ff_got, ff_first = sync(
        state_own, state_oth, gate, ff_got, ff_first
    )
    ff_second = step(ff_got, 0, EDGE)
    ff_others = ff_others + [swap(ff_first, 1)]

    retained, mixed_t, hidden, normed_second, normed_second_t = call(
        mix_kernel,
        H,
        info,
        [
            rates_in, whole(x), real_in(group_gain), whole(second_gain), whole(second_bias),
            whole(tall_count), head_in(query), head_in(inner), head_in(gate),
            own_in(state_own), other_in(state_oth), tall(go_own), tall(go_oth),
        ],
        [
            head_out(per_head + (VH,), F32), head_out((H, VH, tokens), BF16),
            whole_out((tokens, width), F32), whole_out((tokens, width), BF16),
            whole_out((width, tokens), BF16),
        ],
        [],
        5 * unit,
        "mix",
        32,
    )
    ff_second, ff_others, hidden = sync(ff_second, ff_others, hidden)
    ff_others = ff_others + [swap(ff_second, 1)]
    ff_own = settle(info_edge, [ff_part, ff_got, ff_first, ff_second], True)
    ff_oth = settle(info_edge, ff_others, False)
    output, grad_hidden, grad_low, grad_second_gain, grad_second_bias, ff_g_own, ff_g_oth = call(
        feed_kernel,
        4,
        info_edge,
        [
            whole(hidden), whole(normed_second), whole(normed_second_t), whole(cot),
            whole(second_gain),
            columns(ff_own, 512, 0, True), columns(ff_oth, 512, 0, False),
            tall(ff_own), tall(ff_oth),
        ],
        [
            whole_out((tokens, width), BF16), whole_out((tokens, width), F32),
            whole_out((tokens, width), BF16), whole_out((1, width), F32),
            whole_out((1, width), F32),
            whole_out(grad_shape + (2048,), BF16), whole_out(grad_shape + (2048,), BF16),
        ],
        [
            pltpu.VMEM((tokens, 512), F32), pltpu.VMEM((tokens, width), F32),
            pltpu.VMEM((tokens, width), F32),
        ],
        24 * unit,
        "feed",
        48,
    )

    ff_g_got = swap(ff_g_oth, 1)
    grad_ret, grad_gate, grad_group_gain, gstate_own, gstate_oth = call(
        unmix_kernel,
        H,
        info,
        [
            rates_in, whole(grad_low), real_in(group_gain), whole(tall_count), head_in(query),
            head_in(retained), head_in(gate), tall(go_own), tall(go_oth),
        ],
        [
            head_out(per_head + (VH,), BF16), head_out(per_head + (VH,), BF16),
            (
                (H, 1, VH), F32, (1, 1, VH),
                lambda h, info: (real(h, info), 0, 0),
            ),
            own_out(state_shape, F32), other_out(state_shape, F32),
        ],
        [],
        5 * unit,
        "unmix",
        32,
    )
    ff_g_own, ff_g_got, gstate_own, gstate_oth, grad_gate, grad_ret = sync(
        ff_g_own, ff_g_got, gstate_own, gstate_oth, grad_gate, grad_ret
    )
    gstate_near = swap(gstate_oth, 1)
    ff_sum = [Piece(ff_g_own), Piece(ff_g_got)]
    ff_first = upper_part(ff_sum, 0, 1)
    gstate_own, gstate_near, grad_gate, grad_ret, ff_sum, ff_first = sync(
        gstate_own, gstate_near, grad_gate, grad_ret, ff_sum, ff_first
    )

    states = tuple(behind) + (gstate_own, gstate_near)
    arrived = []
    arrivals = hop(states, arrived, 1, True)
    ff_first = send(ff_first, 0, EDGE)
    ff_second = upper_part(ff_sum, 0, 0)
    grad_q, key_part, value_part = call(
        inside_kernel,
        H,
        info,
        [
            rates_in, head_in(grad_ret),
            head_in(query), head_in(key), head_in(value), head_in(mixing),
            whole(cosine), whole(sine), whole(tall_count), whole(wide_count),
            own_in(state_own), other_in(state_oth),
        ],
        [
            head_out(per_head + (QK,), BF16),
            head_out(per_head + (QK,), F32), head_out(per_head + (VH,), F32),
        ],
        [],
        3 * unit,
        "inside",
        24,
    )
    states, arrivals, ff_sum, ff_first, ff_second, grad_q, key_part, value_part = sync(
        states, arrivals, ff_sum, ff_first, ff_second, grad_q, key_part, value_part
    )
    arrived = arrived + [arrivals]

    arrivals = hop(states, arrived, 2, True)
    ff_sum = ff_sum + ff_first
    ff_second = send(ff_second, 0, EDGE)
    ff_next = upper_part(ff_sum, 1)
    go_g_own, go_g_oth = call(
        outer_kernel,
        H,
        info,
        [
            whole(grad_low), whole(normed_t), head_in(mixed_t), head_in(grad_gate),
            head_in(grad_q),
        ],
        [whole_out(grad_shape + (2560,), BF16), whole_out(grad_shape + (2560,), BF16)],
        [],
        11 * unit,
        "outer",
        44,
    )
    states, arrived, arrivals, ff_sum, ff_second, ff_next, go_g_own, go_g_oth = sync(
        states, arrived, arrivals, ff_sum, ff_second, ff_next, go_g_own, go_g_oth
    )
    ff_sum = ff_sum + ff_second
    arrived = arrived + [arrivals]

    arrivals = hop(states, arrived, 3, True)
    go_g_got = swap(go_g_oth, 1)
    ff_sum = ff_sum + send(ff_next, 1, EDGE)
    states, arrived, arrivals, go_g_own, go_g_got, ff_sum = sync(
        states, arrived, arrivals, go_g_own, go_g_got, ff_sum
    )
    arrived = arrived + [arrivals]

    go_sum = [Piece(go_g_own), Piece(go_g_got)]
    for phase in range(4, phases + 1):
        arrivals = hop(states, arrived, phase, True)
        if phase == 4:
            go_first = shrink(go_sum, 0, LONE, 1)
            go_second = upper_part(go_sum, 0, 0)
            ff_next = upper_part(ff_sum, 2)
        states, arrived, arrivals, go_sum, go_first, go_second, ff_sum, ff_next = sync(
            states, arrived, arrivals, go_sum, go_first, go_second, ff_sum, ff_next
        )
        arrived = arrived + [arrivals]
    after_own, after_oth = end_states(states, arrived, True)
    after_own, after_oth, go_sum, go_first, go_second, ff_sum, ff_next = sync(
        after_own, after_oth, go_sum, go_first, go_second, ff_sum, ff_next
    )
    go_sum = go_sum + go_first
    go_next = upper_part(go_sum, 1)
    go_second = send(go_second, 0, LONE)
    ff_sum = ff_sum + send(ff_next, 2, EDGE)

    grad_k, grad_v, kv_g_own, kv_g_oth = call(
        last_kernel,
        H,
        info,
        [
            rates_in, whole(normed_t), head_in(key), head_in(value), head_in(key_part),
            head_in(value_part), whole(cosine), whole(sine), whole(tall_count),
            own_in(after_own), other_in(after_oth),
        ],
        [
            head_out(per_head + (QK,), BF16), head_out(per_head + (VH,), BF16),
            whole_out(grad_shape + (1536,), BF16), whole_out(grad_shape + (1536,), BF16),
        ],
        [],
        8 * unit,
        "last",
        32,
    )
    ff_sum, go_sum, go_second, go_next, kv_g_own, kv_g_oth, grad_k, grad_v = sync(
        ff_sum, go_sum, go_second, go_next, kv_g_own, kv_g_oth, grad_k, grad_v
    )
    go_sum = go_sum + go_second
    kv_g_got = swap(kv_g_oth, 1)
    ff_next = upper_part(ff_sum, 3)
    kv_g_own, kv_g_got, go_sum, ff_sum, ff_next = sync(
        kv_g_own, kv_g_got, go_sum, ff_sum, ff_next
    )
    kv_sum = [Piece(kv_g_own), Piece(kv_g_got)]
    kv_first, kv_second = shrink(kv_sum, 0, LONE, 1), shrink(kv_sum, 0, LONE, 0)
    go_next = send(go_next, 1, LONE)
    ff_sum = ff_sum + send(ff_next, 3, EDGE)
    for turn in range(4, last + 1):
        ff_sum = ff_sum + shrink(ff_sum, turn, EDGE)
    input_grad, grad_first_gain, grad_first_bias = call(
        input_kernel,
        H,
        info,
        [
            whole(x), whole(first_gain), whole(grad_hidden), head_in(grad_q),
            head_in(grad_k), head_in(grad_v), head_in(grad_gate),
            columns(qkv_own, 256, 0, True), columns(qkv_oth, 256, 0, False),
            columns(qkv_own, 256, 2, True), columns(qkv_oth, 256, 2, False),
            columns(qkv_own, 512, 2, True), columns(qkv_oth, 512, 2, False),
            columns(go_own, 512, 0, True), columns(go_oth, 512, 0, False),
        ],
        [
            whole_out((tokens, width), F32), whole_out((1, width), F32),
            whole_out((1, width), F32),
        ],
        [pltpu.VMEM((tokens, width), F32)],
        6 * unit,
        "input",
        56,
    )
    kv_sum, kv_first, kv_second, go_sum, go_next, ff_sum, input_grad, sums = sync(
        kv_sum, kv_first, kv_second, go_sum, go_next, ff_sum, input_grad,
        (grad_first_gain, grad_first_bias),
    )
    grad_first_gain, grad_first_bias = sums
    small = jnp.concatenate(
        [
            grad_first_gain, grad_first_bias, grad_second_gain, grad_second_bias,
            grad_group_gain.reshape(-1, width), jnp.zeros((2, width), F32),
        ],
        axis=0,
    )

    kv_sum = kv_sum + kv_first + kv_second
    go_sum = go_sum + go_next
    kv_next = shrink(kv_sum, 1, LONE)
    go_next = shrink(go_sum, 2, LONE)
    for bit in bits[:2:-1]:
        small = small + swap(small, bit)
    kv_sum, kv_next, go_sum, go_next, small = sync(kv_sum, kv_next, go_sum, go_next, small)
    kv_sum = kv_sum + kv_next
    go_sum = go_sum + go_next
    kv_next = shrink(kv_sum, 2, LONE)
    for turn in range(3, last + 1):
        go_sum = go_sum + shrink(go_sum, turn, LONE)
    small = small + swap(small, bits[2])
    ff_grad = summed(ff_sum, 0, 1)[0]
    kv_sum, kv_next, small, ff_grad = sync(kv_sum, kv_next, small, ff_grad)
    kv_sum = kv_sum + kv_next
    for turn in range(3, last + 1):
        kv_sum = kv_sum + shrink(kv_sum, turn, LONE)
    for bit in bits[1::-1]:
        small = small + swap(small, bit)
    group = small[4:6].reshape(-1)
    small = lax.dynamic_slice_in_dim(small, place() * sizes[0], sizes[0], 1)
    group = lax.dynamic_slice_in_dim(group, place() * sizes[4], sizes[4], 0)

    go_grad, kv_grad = summed(go_sum, 0, 1)[0], summed(kv_sum, 0, 1)[0]
    ff_mine, ff_got = finish_wide(ff_grad[:, :1024])
    go_mine, go_got = finish_wide(jnp.concatenate([go_grad[:, :1024], go_grad[:, 2048:]], axis=1))
    kv_mine, kv_got = finish_wide(kv_grad)

    def wide(mine, got, start, stop):
        return ordered(mine[:, start:stop], got[:, start:stop], 1)

    return (
        output.reshape(inputs.shape),
        input_grad.reshape(inputs.shape),
        small[0],
        small[1],
        wide(go_mine, go_got, 1024, 1536),
        wide(kv_mine, kv_got, 0, 512),
        wide(kv_mine, kv_got, 512, 1536),
        wide(go_mine, go_got, 0, 1024),
        group,
        finish_tall(go_grad[:, 1024:2048]),
        small[2],
        small[3],
        wide(ff_mine, ff_got, 0, 1024),
        finish_tall(ff_grad[:, 1024:2048]),
    )


def solution(mesh):
    return jax.shard_map(
        per_device,
        mesh=mesh,
        in_specs=(
            P(None, "dp", "seq", None),
            P(None, "dp", "seq"),
            P(("dp", "seq")),
            P(("dp", "seq")),
            P(("dp", "seq"), None),
            P(("dp", "seq"), None),
            P(("dp", "seq"), None),
            P(("dp", "seq"), None),
            P(("dp", "seq")),
            P(("dp", "seq"), None),
            P(("dp", "seq")),
            P(("dp", "seq")),
            P(("dp", "seq"), None),
            P(("dp", "seq"), None),
            P(None, "dp", "seq", None),
        ),
        out_specs=(
            P(None, "dp", "seq", None),
            P(None, "dp", "seq", None),
            P(("dp", "seq")),
            P(("dp", "seq")),
            P(("dp", "seq"), None),
            P(("dp", "seq"), None),
            P(("dp", "seq"), None),
            P(("dp", "seq"), None),
            P(("dp", "seq")),
            P(("dp", "seq"), None),
            P(("dp", "seq")),
            P(("dp", "seq")),
            P(("dp", "seq"), None),
            P(("dp", "seq"), None),
        ),
        check_vma=False,
    )
```

```python
import jax
import jax.numpy as jnp
from jax import lax
from jax.experimental import pallas as pl
from jax.experimental.pallas import tpu as pltpu
from jax.sharding import PartitionSpec as P

H = 4
QK = 256
VH = 512
AXES = ("dp", "seq")
F32 = jnp.float32
BF16 = jnp.bfloat16
FAR = 4
LONE, EDGE, EVEN = range(3)
MIB = 1024 * 1024


def mm(left, right):
    return lax.dot_general(left, right, (((1,), (0,)), ((), ())), preferred_element_type=F32)


def nt(left, right):
    return lax.dot_general(left, right, (((1,), (1,)), ((), ())), preferred_element_type=F32)


def tn(left, right):
    return lax.dot_general(left, right, (((0,), (0,)), ((), ())), preferred_element_type=F32)


def devices():
    return lax.axis_size("dp") * lax.axis_size("seq")


def place():
    return lax.axis_index("dp") * lax.axis_size("seq") + lax.axis_index("seq")


def swap(values, bit):
    return lax.ppermute(values, AXES, [(i, i ^ bit) for i in range(devices())])


def upper_core():
    return lax.axis_index("seq") % 2 == 1


def sync(*values):
    return lax.optimization_barrier(values)


def orders(kind):
    bits = [1 << k for k in range(1, devices().bit_length() - 1)]
    near = [bit for bit in bits if bit not in (2, FAR)]
    turned = near[1:] + near[:1]
    return {
        LONE: (near[:1] + [2] + near[1:] + [FAR], turned + [2, FAR]),
        EDGE: (near + [2, FAR], turned + [2, FAR]),
        EVEN: (near[:1] + [2] + near[1:] + [FAR], turned[:1] + [2] + turned[1:] + [FAR]),
    }[kind]


def step(values, turn, kind):
    pairs = [(i, i ^ orders(kind)[i % 2][turn]) for i in range(devices())]
    return lax.ppermute(values, AXES, pairs)


def chip_tables(kind):
    count = devices() // 2
    me, core = place() // 2, lax.axis_index("seq") % 2
    every = jnp.arange(count, dtype=jnp.int32)

    def spread_bits(values, sources, targets):
        return sum(((values >> s) & 1) << t for s, t in zip(sources, targets))

    spots, chips = [], []
    for order in orders(kind):
        sources = [bit.bit_length() - 2 for bit in order]
        targets = list(range(len(order)))[::-1]
        spots.append(spread_bits(every ^ me, sources, targets))
        chips.append(spread_bits(every, targets, sources) ^ me)
    swapped = core == 1
    return jnp.concatenate(
        [
            jnp.stack([me, core]),
            jnp.where(swapped, spots[1], spots[0]),
            jnp.where(swapped, spots[0], spots[1]),
            jnp.where(swapped, chips[1], chips[0]),
            jnp.where(swapped, chips[0], chips[1]),
        ]
    ).astype(jnp.int32)


def local(body, outs, *arrays, name):
    size = sum(a.size * a.dtype.itemsize for a in arrays)
    for shape, dtype in outs:
        extent = jnp.dtype(dtype).itemsize
        for length in shape:
            extent *= length
        size += extent

    def spec(shape):
        zeros = (0,) * len(shape)
        return pl.BlockSpec(shape, lambda k: zeros)

    return pl.pallas_call(
        body,
        grid=(1,),
        out_shape=[jax.ShapeDtypeStruct(shape, dtype) for shape, dtype in outs],
        in_specs=[
            pl.BlockSpec(memory_space=pltpu.SMEM) if a.dtype == jnp.int32 else spec(a.shape)
            for a in arrays
        ],
        out_specs=[spec(shape) for shape, _ in outs],
        compiler_params=pltpu.CompilerParams(vmem_limit_bytes=2 * size + 4 * MIB),
        cost_estimate=pl.CostEstimate(flops=1, bytes_accessed=1, transcendentals=0),
        name=name,
    )(*arrays)


def pack(info, *weights):
    width = sum(w.shape[1] for w in weights) // 2
    shape = (weights[0].shape[0], width)

    def body(info_ref, *refs):
        keep, give = refs[-2:]
        at = 0
        for ref in refs[:-2]:
            half = ref.shape[1] // 2
            here = pl.multiple_of(info_ref[1] * half, 128)
            there = pl.multiple_of((1 - info_ref[1]) * half, 128)
            keep[:, at : at + half] = ref[:, pl.ds(here, half)]
            give[:, at : at + half] = ref[:, pl.ds(there, half)]
            at += half

    return local(body, [(shape, BF16)] * 2, info, *weights, name="pack")


def stack_rows(info, keep, got):
    rows, width = keep.shape

    def body(info_ref, keep_ref, got_ref, out):
        upper = info_ref[1] == 1
        out[:rows] = jnp.where(upper, got_ref[...], keep_ref[...])
        out[rows:] = jnp.where(upper, keep_ref[...], got_ref[...])

    return local(body, [((2 * rows, width), BF16)], info, keep, got, name="stack")[0]


def join(part, got):
    half = part.shape[0]

    def body(part_ref, got_ref, out):
        out[:half] = part_ref[...]
        out[half:] = got_ref[...]

    outs = [((2 * half,) + part.shape[1:], BF16)]
    return local(body, outs, part, got, name="join")[0]


def settle(info, pieces, own):
    lengths = [piece.shape[0] for piece in pieces]
    chips = sum(lengths)

    def body(info_ref, *refs):
        at = 0
        for ref, length in zip(refs, lengths):
            for block in range(length):
                refs[-1][info_ref[2 + (2 if own else 3) * chips + at]] = ref[block]
                at += 1

    outs = [((chips,) + pieces[0].shape[1:], BF16)]
    return local(body, outs, info, *pieces, name="settle")[0]


@jax.tree_util.register_pytree_node_class
class Piece:
    def __init__(self, array, start=0):
        self.array, self.start = array, start

    def tree_flatten(self):
        return (self.array,), self.start

    @classmethod
    def tree_unflatten(cls, start, children):
        return cls(children[0], start)


def summed(pieces, start, stop):
    total = None
    for piece in pieces:
        first, last = start - piece.start, stop - piece.start
        if 0 <= first and last <= piece.array.shape[0]:
            value = piece.array[first:last].astype(F32)
            total = value if total is None else total + value
    return total


def span(turn):
    length = devices() // 2 >> turn
    return length // 2, length


def upper_part(pieces, turn, part=None):
    start, stop = span(turn)
    shift = start
    if part is not None:
        middle = (start + stop) // 2
        start, stop = (middle, stop) if part else (start, middle)
    return Piece(summed(pieces, start, stop).astype(BF16), start - shift)


def send(piece, turn, kind):
    return [Piece(step(piece.array, turn, kind), piece.start)]


def shrink(pieces, turn, kind, part=None):
    return send(upper_part(pieces, turn, part), turn, kind)


def ordered(mine, other, axis):
    upper = upper_core()
    return jnp.concatenate(
        [jnp.where(upper, other, mine), jnp.where(upper, mine, other)], axis=axis
    )


def finish_wide(values):
    rows = values.shape[0] // 2
    upper = upper_core()
    low, high = values[:rows], values[rows:]
    mine, give = jnp.where(upper, high, low), jnp.where(upper, low, high)
    return mine, swap(give, 1)


def finish_tall(values):
    half = values.shape[1] // 2
    upper = upper_core()
    low, high = values[:, :half], values[:, half:]
    mine, give = jnp.where(upper, high, low), jnp.where(upper, low, high)
    return ordered(mine, swap(give, 1), 1)


def phase_count(rows):
    return lax.axis_size("seq") // 2 - 1 + rows - 1


def chip_place(reverse):
    chips = lax.axis_size("seq") // 2
    at = lax.axis_index("seq") // 2
    return chips - 1 - at if reverse else at


def row_at(phase, rows, reverse):
    return jnp.clip(phase - 1 - chip_place(reverse), 0, rows - 1)


def factors_of(carry, near_carry, reverse):
    rows = carry.shape[0]
    upper = upper_core()
    turned = jnp.logical_not(upper) if reverse else upper
    one, zero = jnp.ones_like(carry), jnp.zeros_like(carry)

    def either(yes, no):
        return jnp.where(turned, yes, no)

    table = (either(one, near_carry), either(carry, one), carry * near_carry)
    passed = []
    for phase in range(1, phase_count(rows) + 1):
        row = row_at(phase, rows, reverse)
        passed.append([
            sum(jnp.where(row == k, factor[k], 0.0) for k in range(rows))[:, None, None]
            for factor in table
        ])
    mine = (either(zero, zero), either(one, zero), either(near_carry, one))
    theirs = (either(zero, one), either(zero, zero), either(one, carry))
    return passed, [[f[:, :, None, None] for f in side] for side in (mine, theirs)]


def hop(states, arrived, phase, reverse):
    passed, _, own, near = states
    rows = own.shape[0]
    row = row_at(phase, rows, reverse)
    a, b, c = passed[phase - 1]
    message = a * lax.dynamic_index_in_dim(own, row, 0, False)
    message = message + b * lax.dynamic_index_in_dim(near, row, 0, False)
    if arrived:
        message = message + c * arrived[-1].astype(F32)
    chips = lax.axis_size("seq") // 2
    pairs = []
    for at in range(chips - 1):
        if 0 <= phase - 1 - at < rows:
            source, target = (chips - 1 - at, chips - 2 - at) if reverse else (at, at + 1)
            pairs += [(2 * source + core, 2 * target + core) for core in range(2)]
    return lax.ppermute(message.astype(BF16), "seq", pairs)


def end_states(states, arrived, reverse):
    _, (mine, theirs), own, near = states
    at = chip_place(reverse)
    chips = lax.axis_size("seq") // 2
    before = []
    for row in range(own.shape[0]):
        value = jnp.zeros_like(arrived[0])
        for other in range(1, chips):
            value = jnp.where(at == other, arrived[row + other - 1], value)
        before.append(value.astype(F32))
    before = jnp.stack(before)

    def taken(factors):
        a, b, c = factors
        return (a * own + b * near + c * before).astype(BF16)

    return taken(mine), swap(taken(theirs), 1)


def call(body, grid, info, ins, outs, scratch, flops, name, vmem):
    def spec(shape, block, index, once):
        if block is None:
            return pl.BlockSpec(memory_space=pltpu.SMEM)
        if once and block == shape and name == "feed":
            return pl.BlockSpec(block, index, pipeline_mode=pl.Buffered(1))
        return pl.BlockSpec(block, index)

    moved = sum(a.size * a.dtype.itemsize for a, _, _ in ins)
    for shape, dtype, _, _ in outs:
        size = jnp.dtype(dtype).itemsize
        for extent in shape:
            size *= extent
        moved += size
    return pl.pallas_call(
        body,
        grid_spec=pltpu.PrefetchScalarGridSpec(
            num_scalar_prefetch=1,
            grid=(grid,),
            in_specs=[spec(a.shape, block, index, True) for a, block, index in ins],
            out_specs=[spec(shape, block, index, False) for shape, _, block, index in outs],
            scratch_shapes=scratch,
        ),
        out_shape=[jax.ShapeDtypeStruct(shape, dtype) for shape, dtype, _, _ in outs],
        compiler_params=pltpu.CompilerParams(
            vmem_limit_bytes=vmem * MIB, dimension_semantics=("arbitrary",)
        ),
        cost_estimate=pl.CostEstimate(flops=1, bytes_accessed=1, transcendentals=0),
        name=name,
    )(info, *[a for a, _, _ in ins])


def whole(array):
    zeros = (0,) * array.ndim
    return (array, array.shape, lambda h, info: zeros)


def whole_out(shape, dtype):
    zeros = (0,) * len(shape)
    return (shape, dtype, shape, lambda h, info: zeros)


def head_in(array):
    rest = (0,) * (array.ndim - 1)
    return (array, (1,) + array.shape[1:], lambda h, info: (h,) + rest)


def head_out(shape, dtype):
    rest = (0,) * (len(shape) - 1)
    return (shape, dtype, (1,) + shape[1:], lambda h, info: (h,) + rest)


def state_block(shape, own):
    block = (shape[0], 1) + shape[2:]
    if own:
        return block, lambda h, info: (0, jnp.minimum(h, 1), 0, 0)
    return block, lambda h, info: (0, jnp.maximum(h - 2, 0), 0, 0)


def own_in(array):
    return (array,) + state_block(array.shape, True)


def other_in(array):
    return (array,) + state_block(array.shape, False)


def own_out(shape, dtype):
    return (shape, dtype) + state_block(shape, True)


def other_out(shape, dtype):
    return (shape, dtype) + state_block(shape, False)


def real(h, info):
    return lax.rem(h + 2 * info[1], 4)


def real_in(array):
    rest = (0,) * (array.ndim - 1)
    return (array, (1,) + array.shape[1:], lambda h, info: (real(h, info),) + rest)


def columns(array, width, first, own):
    block = array.shape[:2] + (width,)
    if own:
        return (array, block, lambda h, info: (0, 0, first + jnp.minimum(h, 1)))
    return (array, block, lambda h, info: (0, 0, first + jnp.maximum(h - 2, 0)))


def tall(array):
    block = (array.shape[0] // 4, array.shape[1], 1024)
    return (array, block, lambda h, info: (real(h, info), 0, 1))


def tall_rows(ref):
    chips = ref.shape[0]
    pieces = []
    for chip in range(chips):
        pieces += [ref[chip, :, :512], ref[chip, :, 512:]]
    return jnp.concatenate(pieces, axis=0)


def flat(ref):
    chips, rows, width = ref.shape
    return ref[...].reshape(chips * rows, width)


def side(info, own):
    return pl.multiple_of(512 * (info[1] if own else 1 - info[1]), 512)


def put_wide(target, info, values, start, own):
    chips, rows, _ = target.shape
    width = values.shape[1]
    values = values.astype(BF16)
    for chip in range(chips):
        target[info[(2 if own else 2 + chips) + chip], :, start : start + width] = values[chip * rows : (chip + 1) * rows]


def put_tall(target, info, values, block, start, own):
    chips, rows, _ = target.shape
    values = values.astype(BF16)
    share = chips // 4
    for chip in range(share):
        at = info[(2 if own else 2 + chips) + block * share + chip]
        base = 2 * rows * chip
        target[at, :, start : start + 512] = values[base : base + rows]
        target[at, :, start + 512 : start + 1024] = values[base + rows : base + 2 * rows]


def rotated(values, cosine, sine):
    a, b = values[:, :128], values[:, 128:]
    return jnp.concatenate([a * cosine - b * sine, b * cosine + a * sine], axis=1)


def unrotated(values, cosine, sine):
    a, b = values[:, :128], values[:, 128:]
    return jnp.concatenate([a * cosine + b * sine, b * cosine - a * sine], axis=1)


def mask_of(rate, tall_count, wide_count):
    length = tall_count.shape[0]
    i = lax.broadcasted_iota(jnp.int32, (length, length), 0)
    s = lax.broadcasted_iota(jnp.int32, (length, length), 1)
    decay = jnp.exp((i - s).astype(F32) * rate)
    return jnp.where((tall_count == wide_count) & (i >= s), decay, 0.0)


def enter_of(rate, tall_count):
    i = lax.broadcasted_iota(jnp.int32, tall_count.shape, 0)
    return jnp.where(tall_count == 0, jnp.exp((i + 1).astype(F32) * rate), 0.0)


def leave_of(rate, tall_count):
    length = tall_count.shape[0]
    i = lax.broadcasted_iota(jnp.int32, tall_count.shape, 0)
    last = tall_count[length - 1 :, :]
    return jnp.where(tall_count == last, jnp.exp((length - 1 - i).astype(F32) * rate), 0.0)


def norm_parts(values, eps):
    average = jnp.mean(values, axis=-1, keepdims=True)
    centred = values - average
    spread_ = jnp.mean(centred * centred, axis=-1, keepdims=True)
    scale = lax.rsqrt(spread_ + eps)
    return centred * scale, scale


def norm_back(grad, normal, scale):
    first = jnp.mean(grad, axis=-1, keepdims=True)
    second = jnp.mean(grad * normal, axis=-1, keepdims=True)
    return scale * (grad - first - normal * second)


CHUNK = 64


def norm_kernel(info, x, gain, bias, normed, normed_t):
    @pl.loop(0, x.shape[0] // CHUNK)
    def _(k):
        at = pl.ds(pl.multiple_of(k * CHUNK, CHUNK), CHUNK)
        normal, _ = norm_parts(x[at, :].astype(F32), 1e-05)
        normed[at, :] = (normal * gain[...].astype(F32) + bias[...].astype(F32)).astype(BF16)

    normed_t[...] = normed[...].T


def project_kernel(
    info, rates, normed, cosine, sine, tall_count, wide_count,
    q_own, k_own, v_own, q_oth, k_oth, v_oth,
    q_out, k_out, v_out, mix_out, inner_out, sum_own, sum_oth, pre,
):
    h = pl.program_id(0)

    def fill(wq, wk, wv):
        left = normed[...]
        pre[:, :256] = mm(left, flat(wq))
        pre[:, 256:512] = mm(left, flat(wk))
        pre[:, 512:] = mm(left, flat(wv))

    @pl.when(h < 2)
    def _():
        fill(q_own, k_own, v_own)

    @pl.when(h >= 2)
    def _():
        fill(q_oth, k_oth, v_oth)

    rate = rates[h]
    length = cosine.shape[0]
    for row in range(tall_count.shape[0]):
        at = slice(row * length, (row + 1) * length)
        count = tall_count[row]
        query = rotated(pre[at, :256], cosine[...], sine[...]).astype(BF16)
        key = (rotated(pre[at, 256:512], cosine[...], sine[...]) * QK**-0.5).astype(BF16)
        value = pre[at, 512:].astype(BF16)
        q_out[0, at] = query
        k_out[0, at] = key
        v_out[0, at] = value
        mixing = (nt(query, key) * mask_of(rate, count, wide_count[row])).astype(BF16)
        mix_out[0, at] = mixing
        inner_out[0, at] = mm(mixing, value)
        weighted = (key.astype(F32) * leave_of(rate, count)).astype(BF16)
        summary = tn(weighted, value)

        @pl.when(h < 2)
        def _():
            sum_own[row, 0] = summary

        @pl.when(h >= 2)
        def _():
            sum_oth[row, 0] = summary


def gate_kernel(info, normed, own, oth, out):
    h = pl.program_id(0)

    @pl.when(h < 2)
    def _():
        out[0] = mm(normed[...], flat(own))

    @pl.when(h >= 2)
    def _():
        out[0] = mm(normed[...], flat(oth))


def mix_kernel(
    info, rates, x, gain, second_gain, second_bias, tall_count, query, inner, gate,
    state_own, state_oth, wo_own, wo_oth,
    retained, mixed_t, hidden, normed, normed_t,
):
    h = pl.program_id(0)
    rate = rates[h]
    length = tall_count.shape[1]

    @pl.when(h == 0)
    def _():
        hidden[...] = x[...].astype(F32)

    for row in range(tall_count.shape[0]):
        at = slice(row * length, (row + 1) * length)
        entered = (query[0, at].astype(F32) * enter_of(rate, tall_count[row])).astype(BF16)

        @pl.when(h < 2)
        def _():
            retained[0, at] = inner[0, at] + mm(entered, state_own[row, 0])

        @pl.when(h >= 2)
        def _():
            retained[0, at] = inner[0, at] + mm(entered, state_oth[row, 0])

    normal, _ = norm_parts(retained[0], 1.0)
    pre = gate[0]
    mixed = (pre / (1.0 + jnp.exp(-pre)) * (normal * gain[0].astype(F32))).astype(BF16)
    mixed_t[0] = mixed.T
    hidden[:, pl.ds(side(info, True), 512)] += mm(mixed, tall_rows(wo_own))
    hidden[:, pl.ds(side(info, False), 512)] += mm(mixed, tall_rows(wo_oth))

    @pl.when(h == 3)
    def _():
        @pl.loop(0, x.shape[0] // CHUNK)
        def _(k):
            at = pl.ds(pl.multiple_of(k * CHUNK, CHUNK), CHUNK)
            normal, _ = norm_parts(hidden[at, :], 1e-05)
            normed[at, :] = (
                normal * second_gain[...].astype(F32) + second_bias[...].astype(F32)
            ).astype(BF16)

        normed_t[...] = normed[...].T


def feed_kernel(
    info, hidden, normed, normed_t, cot, second_gain,
    up_own, up_oth, down_own, down_oth,
    output, grad_hidden, grad_low, grad_gain, grad_bias, g_own, g_oth,
    upward, out_sum, norm_sum,
):
    f = pl.program_id(0)
    own_at = pl.ds(side(info, True), 512)
    oth_at = pl.ds(side(info, False), 512)

    @pl.when(f == 0)
    def _():
        out_sum[...] = hidden[...]
        norm_sum[...] = jnp.zeros_like(norm_sum)

    @pl.when(f < 2)
    def _():
        upward[...] = mm(normed[...], flat(up_own))

    @pl.when(f >= 2)
    def _():
        upward[...] = mm(normed[...], flat(up_oth))

    up = upward[...]
    root = 0.7978845608028654
    squared = up * up
    bent = jnp.tanh(root * (up + 0.044715 * (squared * up)))
    activated = (0.5 * up * (1.0 + bent)).astype(BF16)
    slope = 0.5 * (1.0 + bent) + 0.5 * up * (1.0 - bent * bent) * (
        root * (1.0 + 3 * 0.044715 * squared)
    )
    own, oth = tall_rows(down_own), tall_rows(down_oth)
    out_sum[:, own_at] += mm(activated, own)
    out_sum[:, oth_at] += mm(activated, oth)
    grad_up = (slope * (nt(cot[:, own_at], own) + nt(cot[:, oth_at], oth))).astype(BF16)
    block = real(f, info)
    act_t = activated.T
    put_tall(g_own, info, mm(act_t, cot[:, own_at]), block, 1024, True)
    put_tall(g_oth, info, mm(act_t, cot[:, oth_at]), block, 1024, False)
    grad_w = mm(normed_t[...], grad_up)
    for step in range(4):

        @pl.when(f == step)
        def _():
            put_wide(g_own if step < 2 else g_oth, info, grad_w, 512 * (step % 2), step < 2)

    @pl.when(f < 2)
    def _():
        norm_sum[...] += nt(grad_up, flat(up_own))

    @pl.when(f >= 2)
    def _():
        norm_sum[...] += nt(grad_up, flat(up_oth))

    @pl.when(f == 3)
    def _():
        grad_gain[...] = jnp.zeros_like(grad_gain)
        grad_bias[...] = jnp.zeros_like(grad_bias)

        @pl.loop(0, hidden.shape[0] // CHUNK)
        def _(k):
            at = pl.ds(pl.multiple_of(k * CHUNK, CHUNK), CHUNK)
            output[at, :] = out_sum[at, :].astype(BF16)
            normal, scale = norm_parts(hidden[at, :], 1e-05)
            grad = norm_sum[at, :]
            grad_gain[...] += jnp.sum(grad * normal, axis=0, keepdims=True)
            grad_bias[...] += jnp.sum(grad, axis=0, keepdims=True)
            total = cot[at, :].astype(F32) + norm_back(
                grad * second_gain[...].astype(F32), normal, scale
            )
            grad_hidden[at, :] = total
            grad_low[at, :] = total.astype(BF16)


def unmix_kernel(
    info, rates, grad_low, gain, tall_count, query, retained, gate, wo_own, wo_oth,
    grad_ret, grad_gate, grad_gain, state_own, state_oth,
):
    h = pl.program_id(0)
    rate = rates[h]
    length = tall_count.shape[1]
    grad = nt(grad_low[:, pl.ds(side(info, True), 512)], tall_rows(wo_own)) + nt(
        grad_low[:, pl.ds(side(info, False), 512)], tall_rows(wo_oth)
    )
    normal, scale = norm_parts(retained[0], 1.0)
    pre = gate[0]
    share = 1.0 / (1.0 + jnp.exp(-pre))
    curve = pre * share
    scaled = gain[0].astype(F32)
    grad_gate[0] = (grad * (normal * scaled) * (share * (1.0 + pre * (1.0 - share)))).astype(BF16)
    grad_normal = grad * curve
    grad_gain[0] = jnp.sum(grad_normal * normal, axis=0, keepdims=True)
    grad_ret[0] = norm_back(grad_normal * scaled, normal, scale).astype(BF16)
    for row in range(tall_count.shape[0]):
        at = slice(row * length, (row + 1) * length)
        entered = (query[0, at].astype(F32) * enter_of(rate, tall_count[row])).astype(BF16)
        state = tn(entered, grad_ret[0, at])

        @pl.when(h < 2)
        def _():
            state_own[row, 0] = state

        @pl.when(h >= 2)
        def _():
            state_oth[row, 0] = state


def inside_kernel(
    info, rates, grad_ret, query, key, value, mixing,
    cosine, sine, tall_count, wide_count, state_own, state_oth,
    grad_q, key_part, value_part,
):
    h = pl.program_id(0)
    rate = rates[h]
    length = cosine.shape[0]
    for row in range(tall_count.shape[0]):
        at = slice(row * length, (row + 1) * length)
        grad = grad_ret[0, at]
        mask = mask_of(rate, tall_count[row], wide_count[row])
        scores = (nt(grad, value[0, at]) * mask).astype(BF16)
        enter = enter_of(rate, tall_count[row])

        def set_query(state):
            total = mm(scores, key[0, at]) + nt(grad, state[row, 0]) * enter
            grad_q[0, at] = unrotated(total, cosine[...], sine[...]).astype(BF16)

        @pl.when(h < 2)
        def _():
            set_query(state_own)

        @pl.when(h >= 2)
        def _():
            set_query(state_oth)

        key_part[0, at] = tn(scores, query[0, at])
        value_part[0, at] = tn(mixing[0, at], grad)


def outer_kernel(
    info, grad_low, normed_t, mixed_t, grad_gate, grad_q, out_own, out_oth,
):
    h = pl.program_id(0)
    block = real(h, info)
    left = mixed_t[0]
    put_tall(out_own, info, mm(left, grad_low[:, pl.ds(side(info, True), 512)]), block, 1024, True)
    put_tall(out_oth, info, mm(left, grad_low[:, pl.ds(side(info, False), 512)]), block, 1024, False)
    grad_wg = mm(normed_t[...], grad_gate[0])
    grad_wq = mm(normed_t[...], grad_q[0])
    for step in range(4):

        @pl.when(h == step)
        def _():
            target = out_own if step < 2 else out_oth
            put_wide(target, info, grad_wg, 512 * (step % 2), step < 2)
            put_wide(target, info, grad_wq, 2048 + 256 * (step % 2), step < 2)


def last_kernel(
    info, rates, normed_t, key, value, key_part, value_part, cosine, sine, tall_count,
    state_own, state_oth,
    grad_k, grad_v, out_own, out_oth,
):
    h = pl.program_id(0)
    rate = rates[h]
    length = cosine.shape[0]
    for row in range(tall_count.shape[0]):
        at = slice(row * length, (row + 1) * length)
        leave = leave_of(rate, tall_count[row])
        weighted = (key[0, at].astype(F32) * leave).astype(BF16)

        def set_both(state):
            low = state[row, 0]
            grad_v[0, at] = (value_part[0, at] + mm(weighted, low)).astype(BF16)
            total = key_part[0, at] + nt(value[0, at], low) * leave
            grad_k[0, at] = (unrotated(total, cosine[...], sine[...]) * QK**-0.5).astype(BF16)

        @pl.when(h < 2)
        def _():
            set_both(state_own)

        @pl.when(h >= 2)
        def _():
            set_both(state_oth)

    grad_wk = mm(normed_t[...], grad_k[0])
    grad_wv = mm(normed_t[...], grad_v[0])
    for step in range(4):

        @pl.when(h == step)
        def _():
            target = out_own if step < 2 else out_oth
            put_wide(target, info, grad_wk, 256 * (step % 2), step < 2)
            put_wide(target, info, grad_wv, 512 + 512 * (step % 2), step < 2)


def input_kernel(
    info, x, gain, grad_hidden, grad_q, grad_k, grad_v, grad_gate,
    q_own, q_oth, k_own, k_oth, v_own, v_oth, g_own, g_oth,
    input_grad, grad_gain, grad_bias, norm_sum,
):
    h = pl.program_id(0)

    @pl.when(h == 0)
    def _():
        norm_sum[...] = jnp.zeros_like(norm_sum)

    def add(wq, wk, wv, wg):
        norm_sum[...] += (
            nt(grad_q[0], flat(wq)) + nt(grad_k[0], flat(wk))
            + nt(grad_v[0], flat(wv)) + nt(grad_gate[0], flat(wg))
        )

    @pl.when(h < 2)
    def _():
        add(q_own, k_own, v_own, g_own)

    @pl.when(h >= 2)
    def _():
        add(q_oth, k_oth, v_oth, g_oth)

    @pl.when(h == 3)
    def _():
        grad_gain[...] = jnp.zeros_like(grad_gain)
        grad_bias[...] = jnp.zeros_like(grad_bias)

        @pl.loop(0, x.shape[0] // CHUNK)
        def _(k):
            at = pl.ds(pl.multiple_of(k * CHUNK, CHUNK), CHUNK)
            normal, scale = norm_parts(x[at, :].astype(F32), 1e-05)
            grad = norm_sum[at, :]
            grad_gain[...] += jnp.sum(grad * normal, axis=0, keepdims=True)
            grad_bias[...] += jnp.sum(grad, axis=0, keepdims=True)
            input_grad[at, :] = grad_hidden[at, :] + norm_back(
                grad * gain[...].astype(F32), normal, scale
            )


def per_device(
    inputs,
    doc_flags,
    first_gain,
    first_bias,
    w_query,
    w_key,
    w_value,
    w_gate,
    group_gain,
    w_output,
    second_gain,
    second_bias,
    w_up,
    w_down,
    cotangent,
):
    batches, row_count, length, width = inputs.shape
    rows = batches * row_count
    tokens = rows * length
    count = devices()
    chips = count // 2
    info, info_edge = chip_tables(LONE), chip_tables(EDGE)
    x = inputs.reshape(tokens, width)
    cot = cotangent.reshape(tokens, width)

    upper = upper_core()
    share = w_query.shape[0]
    last = len(orders(LONE)[0]) - 1

    keep, give = pack(info, w_query, w_key, w_value)
    qkv = stack_rows(info, keep, swap(give, 1))
    vectors = [first_gain, first_bias, second_gain, second_bias, group_gain]
    qkv, vectors = sync(qkv, vectors)
    got_qkv = step(qkv[None], last, LONE)

    sizes = [v.shape[0] for v in vectors]
    edges = [sum(sizes[:k]) for k in range(len(sizes) + 1)]
    lanes = -(-edges[-1] // 128) * 128
    table = jnp.concatenate([v.reshape(1, -1) for v in vectors], axis=1)
    table = jnp.pad(table, ((0, 15), (0, lanes - edges[-1])))

    def table_step(table, done, bit):
        got = swap(table, bit)
        turned = (place() // bit) % 2 == 1
        spot = sum(1 for other in done if other > bit)
        done.append(bit)
        return jnp.stack(
            [jnp.where(turned, got, table), jnp.where(turned, table, got)], axis=spot
        )

    bits = [1 << k for k in range(count.bit_length() - 1)]
    done = []
    for bit in (1, FAR):
        table = table_step(table, done, bit)
    got_qkv, table = sync(got_qkv, table)
    part, got = qkv[None], got_qkv
    start = lax.axis_index("seq") * length
    for turn in range(last - 1, 1, -1):
        part = join(part, got)
        got = step(part, turn, LONE)
        if turn == last - 1:
            table = table_step(table, done, 2)
        part, got, table, w_gate, w_up, w_output, w_down, doc_flags, start = sync(
            part, got, table, w_gate, w_up, w_output, w_down, doc_flags, start
        )

    part = join(part, got)
    got = step(part, 1, LONE)
    for bit in bits[:2:-1]:
        table = table_step(table, done, bit)

    top_keep, top_give = pack(info, w_gate, w_up)
    tall_keep, tall_give = pack(info, w_output, w_down)
    top = stack_rows(info, top_keep, swap(top_give, 1))
    tall_got = swap(tall_give, 1)
    low, high = jnp.where(upper, tall_got, tall_keep), jnp.where(upper, tall_keep, tall_got)
    go = jnp.concatenate([top[:, :1024], low[:, :512], high[:, :512]], axis=1)
    ff = jnp.concatenate([top[:, 1024:], low[:, 512:], high[:, 512:]], axis=1)
    go_part, ff_part = go[None], ff[None]
    part, got, go_part, ff_part, table, doc_flags = sync(
        part, got, go_part, ff_part, table, doc_flags
    )

    pieces = [part, got, step(part, 0, LONE), step(got, 0, LONE)]
    go_got = step(go_part, last, EDGE)
    ff_got = step(ff_part, last, EDGE)
    vector = table.reshape(count, -1, lanes)[:, 0]
    first_gain, first_bias, second_gain, second_bias, group_gain = [
        vector[:, a:b].reshape(1, -1) for a, b in zip(edges[:-1], edges[1:])
    ]
    group_gain = group_gain.reshape(H, 1, VH)

    positions = start + jnp.arange(length, dtype=jnp.int32)
    frequency = 10000.0 ** (-jnp.arange(QK // 2, dtype=F32) / (QK // 2))
    angles = positions.astype(F32)[:, None] * frequency[None, :]
    cosine, sine = jnp.cos(angles), jnp.sin(angles)
    rates = jnp.log1p(-(2.0 ** (-5.0 - 3.0 * jnp.arange(H, dtype=F32))))
    rates = jnp.where(upper, jnp.roll(rates, 2), rates)
    counts = jnp.cumsum(doc_flags.reshape(rows, length), axis=-1, dtype=jnp.int32)
    tall_count, wide_count = counts[:, :, None], counts[:, None, :]
    open_row = (counts[:, -1] == 0).astype(F32)
    near_row = swap(open_row, 1)
    decay = jnp.exp(rates[:2] * float(length))
    carry, near_carry = decay[None] * open_row[:, None], decay[None] * near_row[:, None]
    ahead = factors_of(carry, near_carry, False)
    behind = factors_of(carry, near_carry, True)

    per_head = (H, tokens)
    state_shape = (rows, 2, QK, VH)
    grad_shape = (chips, 2 * share)
    rates_in = (rates, None, None)
    unit = 2.0 * tokens * width * 512

    normed, normed_t = call(
        norm_kernel,
        1,
        info,
        [whole(x), whole(first_gain), whole(first_bias)],
        [whole_out((tokens, width), BF16), whole_out((width, tokens), BF16)],
        [],
        unit / 100,
        "norm",
        16,
    )
    pieces, go_part, go_got, ff_part, ff_got, normed, normed_t, tables, gains = sync(
        pieces, go_part, go_got, ff_part, ff_got, normed, normed_t,
        (cosine, sine, tall_count, wide_count, ahead, behind, rates),
        (second_gain, second_bias, group_gain),
    )
    cosine, sine, tall_count, wide_count, ahead, behind, rates = tables
    second_gain, second_bias, group_gain = gains
    rates_in = (rates, None, None)

    qkv_own = settle(info, pieces, True)
    qkv_oth = swap(qkv_own, 1)
    go_part = join(go_part, go_got)
    go_got = step(go_part, last - 1, EDGE)
    qkv_own, qkv_oth, go_part, go_got, ff_part, ff_got = sync(
        qkv_own, qkv_oth, go_part, go_got, ff_part, ff_got
    )

    go_part = join(go_part, go_got)
    go_got = step(go_part, last - 2, EDGE)
    ff_part = join(ff_part, ff_got)
    ff_got = step(ff_part, last - 1, EDGE)
    (query, key, value, mixing, inner, sum_own, sum_oth) = call(
        project_kernel,
        H,
        info,
        [
            rates_in, whole(normed), whole(cosine), whole(sine),
            whole(tall_count), whole(wide_count),
            columns(qkv_own, 256, 0, True), columns(qkv_own, 256, 2, True),
            columns(qkv_own, 512, 2, True),
            columns(qkv_oth, 256, 0, False), columns(qkv_oth, 256, 2, False),
            columns(qkv_oth, 512, 2, False),
        ],
        [
            head_out(per_head + (QK,), BF16), head_out(per_head + (QK,), BF16),
            head_out(per_head + (VH,), BF16), head_out(per_head + (length,), BF16),
            head_out(per_head + (VH,), F32),
            own_out(state_shape, F32), other_out(state_shape, F32),
        ],
        [pltpu.VMEM((tokens, 1024), F32)],
        10 * unit,
        "project",
        56,
    )
    go_part, go_got, ff_part, ff_got, sum_own, sum_oth = sync(
        go_part, go_got, ff_part, ff_got, sum_own, sum_oth
    )
    for turn in range(last - 3, 0, -1):
        go_part = join(go_part, go_got)
        go_got = step(go_part, turn, EDGE)
        ff_part = join(ff_part, ff_got)
        ff_got = step(ff_part, turn + 1, EDGE)
        go_part, go_got, ff_part, ff_got = sync(go_part, go_got, ff_part, ff_got)
    sum_near = swap(sum_oth, 1)
    sum_own, sum_near, go_part, go_got, ff_part, ff_got = sync(
        sum_own, sum_near, go_part, go_got, ff_part, ff_got
    )

    states = tuple(ahead) + (sum_own, sum_near)
    phases = phase_count(rows)
    arrivals = hop(states, [], 1, False)
    go_first = step(go_part, 0, EDGE)
    states, arrivals, go_part, go_got, go_first = sync(
        states, arrivals, go_part, go_got, go_first
    )
    arrived = [arrivals]

    arrivals = hop(states, arrived, 2, False)
    go_second = step(go_got, 0, EDGE)
    states, arrived, arrivals, pieces, ff_part, ff_got = sync(
        states, arrived, arrivals, [go_part, go_got, go_first, go_second], ff_part, ff_got
    )
    arrived = arrived + [arrivals]

    arrivals = hop(states, arrived, 3, False)
    ff_part = join(ff_part, ff_got)
    ff_got = step(ff_part, 1, EDGE)
    go_own = settle(info_edge, pieces, True)
    go_oth = swap(go_own, 1)
    states, arrived, arrivals, go_own, go_oth, normed, ff_part, ff_got = sync(
        states, arrived, arrivals, go_own, go_oth, normed, ff_part, ff_got
    )
    arrived = arrived + [arrivals]

    for phase in range(4, phases + 1):
        arrivals = hop(states, arrived, phase, False)
        if phase == 4:
            ff_first = step(ff_part, 0, EDGE)
            ff_others = [swap(ff_part, 1), swap(ff_got, 1)]
            (gate,) = call(
                gate_kernel,
                H,
                info,
                [whole(normed), columns(go_own, 512, 0, True), columns(go_oth, 512, 0, False)],
                [head_out(per_head + (VH,), F32)],
                [],
                4 * unit,
                "gate",
                20,
            )
        states, arrived, arrivals, gate, ff_part, ff_got, ff_first, ff_others = sync(
            states, arrived, arrivals, gate, ff_part, ff_got, ff_first, ff_others
        )
        arrived = arrived + [arrivals]
    state_own, state_oth = end_states(states, arrived, False)
    state_own, state_oth, ff_got, ff_first = sync(state_own, state_oth, ff_got, ff_first)
    ff_second = step(ff_got, 0, EDGE)
    ff_others = ff_others + [swap(ff_first, 1)]

    retained, mixed_t, hidden, normed_second, normed_second_t = call(
        mix_kernel,
        H,
        info,
        [
            rates_in, whole(x), real_in(group_gain), whole(second_gain), whole(second_bias),
            whole(tall_count), head_in(query), head_in(inner), head_in(gate),
            own_in(state_own), other_in(state_oth), tall(go_own), tall(go_oth),
        ],
        [
            head_out(per_head + (VH,), F32), head_out((H, VH, tokens), BF16),
            whole_out((tokens, width), F32), whole_out((tokens, width), BF16),
            whole_out((width, tokens), BF16),
        ],
        [],
        5 * unit,
        "mix",
        32,
    )
    ff_second, ff_others, hidden = sync(ff_second, ff_others, hidden)
    ff_others = ff_others + [swap(ff_second, 1)]
    ff_own = settle(info_edge, [ff_part, ff_got, ff_first, ff_second], True)
    ff_oth = settle(info_edge, ff_others, False)
    output, grad_hidden, grad_low, grad_second_gain, grad_second_bias, ff_g_own, ff_g_oth = call(
        feed_kernel,
        4,
        info_edge,
        [
            whole(hidden), whole(normed_second), whole(normed_second_t), whole(cot),
            whole(second_gain),
            columns(ff_own, 512, 0, True), columns(ff_oth, 512, 0, False),
            tall(ff_own), tall(ff_oth),
        ],
        [
            whole_out((tokens, width), BF16), whole_out((tokens, width), F32),
            whole_out((tokens, width), BF16), whole_out((1, width), F32),
            whole_out((1, width), F32),
            whole_out(grad_shape + (2048,), BF16), whole_out(grad_shape + (2048,), BF16),
        ],
        [
            pltpu.VMEM((tokens, 512), F32), pltpu.VMEM((tokens, width), F32),
            pltpu.VMEM((tokens, width), F32),
        ],
        24 * unit,
        "feed",
        48,
    )

    ff_g_got = swap(ff_g_oth, 1)
    grad_ret, grad_gate, grad_group_gain, gstate_own, gstate_oth = call(
        unmix_kernel,
        H,
        info,
        [
            rates_in, whole(grad_low), real_in(group_gain), whole(tall_count), head_in(query),
            head_in(retained), head_in(gate), tall(go_own), tall(go_oth),
        ],
        [
            head_out(per_head + (VH,), BF16), head_out(per_head + (VH,), BF16),
            (
                (H, 1, VH), F32, (1, 1, VH),
                lambda h, info: (real(h, info), 0, 0),
            ),
            own_out(state_shape, F32), other_out(state_shape, F32),
        ],
        [],
        5 * unit,
        "unmix",
        32,
    )
    ff_g_own, ff_g_got, gstate_own, gstate_oth, grad_gate, grad_ret = sync(
        ff_g_own, ff_g_got, gstate_own, gstate_oth, grad_gate, grad_ret
    )
    gstate_near = swap(gstate_oth, 1)
    ff_sum = [Piece(ff_g_own), Piece(ff_g_got)]
    ff_first = upper_part(ff_sum, 0, 1)
    gstate_own, gstate_near, grad_gate, grad_ret, ff_sum, ff_first = sync(
        gstate_own, gstate_near, grad_gate, grad_ret, ff_sum, ff_first
    )

    states = tuple(behind) + (gstate_own, gstate_near)
    arrived = []
    arrivals = hop(states, arrived, 1, True)
    ff_first = send(ff_first, 0, EDGE)
    ff_second = upper_part(ff_sum, 0, 0)
    grad_q, key_part, value_part = call(
        inside_kernel,
        H,
        info,
        [
            rates_in, head_in(grad_ret),
            head_in(query), head_in(key), head_in(value), head_in(mixing),
            whole(cosine), whole(sine), whole(tall_count), whole(wide_count),
            own_in(state_own), other_in(state_oth),
        ],
        [
            head_out(per_head + (QK,), BF16),
            head_out(per_head + (QK,), F32), head_out(per_head + (VH,), F32),
        ],
        [],
        3 * unit,
        "inside",
        24,
    )
    states, arrivals, ff_sum, ff_first, ff_second, grad_q, key_part, value_part = sync(
        states, arrivals, ff_sum, ff_first, ff_second, grad_q, key_part, value_part
    )
    arrived = arrived + [arrivals]

    arrivals = hop(states, arrived, 2, True)
    ff_sum = ff_sum + ff_first
    ff_second = send(ff_second, 0, EDGE)
    ff_next = upper_part(ff_sum, 1)
    go_g_own, go_g_oth = call(
        outer_kernel,
        H,
        info,
        [
            whole(grad_low), whole(normed_t), head_in(mixed_t), head_in(grad_gate),
            head_in(grad_q),
        ],
        [whole_out(grad_shape + (2560,), BF16), whole_out(grad_shape + (2560,), BF16)],
        [],
        11 * unit,
        "outer",
        44,
    )
    states, arrived, arrivals, ff_sum, ff_second, ff_next, go_g_own, go_g_oth = sync(
        states, arrived, arrivals, ff_sum, ff_second, ff_next, go_g_own, go_g_oth
    )
    ff_sum = ff_sum + ff_second
    arrived = arrived + [arrivals]

    arrivals = hop(states, arrived, 3, True)
    go_g_got = swap(go_g_oth, 1)
    ff_sum = ff_sum + send(ff_next, 1, EDGE)
    states, arrived, arrivals, go_g_own, go_g_got, ff_sum = sync(
        states, arrived, arrivals, go_g_own, go_g_got, ff_sum
    )
    arrived = arrived + [arrivals]

    go_sum = [Piece(go_g_own), Piece(go_g_got)]
    for phase in range(4, phases + 1):
        arrivals = hop(states, arrived, phase, True)
        if phase == 4:
            go_first = shrink(go_sum, 0, LONE, 1)
            go_second = upper_part(go_sum, 0, 0)
            ff_next = upper_part(ff_sum, 2)
        states, arrived, arrivals, go_sum, go_first, go_second, ff_sum, ff_next = sync(
            states, arrived, arrivals, go_sum, go_first, go_second, ff_sum, ff_next
        )
        arrived = arrived + [arrivals]
    after_own, after_oth = end_states(states, arrived, True)
    after_own, after_oth, go_sum, go_first, go_second, ff_sum, ff_next = sync(
        after_own, after_oth, go_sum, go_first, go_second, ff_sum, ff_next
    )
    go_sum = go_sum + go_first
    go_next = upper_part(go_sum, 1)
    go_second = send(go_second, 0, LONE)
    ff_sum = ff_sum + send(ff_next, 2, EDGE)

    grad_k, grad_v, kv_g_own, kv_g_oth = call(
        last_kernel,
        H,
        info,
        [
            rates_in, whole(normed_t), head_in(key), head_in(value), head_in(key_part),
            head_in(value_part), whole(cosine), whole(sine), whole(tall_count),
            own_in(after_own), other_in(after_oth),
        ],
        [
            head_out(per_head + (QK,), BF16), head_out(per_head + (VH,), BF16),
            whole_out(grad_shape + (1536,), BF16), whole_out(grad_shape + (1536,), BF16),
        ],
        [],
        8 * unit,
        "last",
        32,
    )
    ff_sum, go_sum, go_second, go_next, kv_g_own, kv_g_oth, grad_k, grad_v = sync(
        ff_sum, go_sum, go_second, go_next, kv_g_own, kv_g_oth, grad_k, grad_v
    )
    go_sum = go_sum + go_second
    kv_g_got = swap(kv_g_oth, 1)
    ff_next = upper_part(ff_sum, 3)
    kv_g_own, kv_g_got, go_sum, ff_sum, ff_next = sync(
        kv_g_own, kv_g_got, go_sum, ff_sum, ff_next
    )
    kv_sum = [Piece(kv_g_own), Piece(kv_g_got)]
    kv_first, kv_second = shrink(kv_sum, 0, LONE, 1), shrink(kv_sum, 0, LONE, 0)
    go_next = send(go_next, 1, LONE)
    ff_sum = ff_sum + send(ff_next, 3, EDGE)
    for turn in range(4, last + 1):
        ff_sum = ff_sum + shrink(ff_sum, turn, EDGE)
    input_grad, grad_first_gain, grad_first_bias = call(
        input_kernel,
        H,
        info,
        [
            whole(x), whole(first_gain), whole(grad_hidden), head_in(grad_q),
            head_in(grad_k), head_in(grad_v), head_in(grad_gate),
            columns(qkv_own, 256, 0, True), columns(qkv_oth, 256, 0, False),
            columns(qkv_own, 256, 2, True), columns(qkv_oth, 256, 2, False),
            columns(qkv_own, 512, 2, True), columns(qkv_oth, 512, 2, False),
            columns(go_own, 512, 0, True), columns(go_oth, 512, 0, False),
        ],
        [
            whole_out((tokens, width), F32), whole_out((1, width), F32),
            whole_out((1, width), F32),
        ],
        [pltpu.VMEM((tokens, width), F32)],
        6 * unit,
        "input",
        56,
    )
    kv_sum, kv_first, kv_second, go_sum, go_next, ff_sum, input_grad, sums = sync(
        kv_sum, kv_first, kv_second, go_sum, go_next, ff_sum, input_grad,
        (grad_first_gain, grad_first_bias),
    )
    grad_first_gain, grad_first_bias = sums
    small = jnp.concatenate(
        [
            grad_first_gain, grad_first_bias, grad_second_gain, grad_second_bias,
            grad_group_gain.reshape(-1, width), jnp.zeros((2, width), F32),
        ],
        axis=0,
    )

    kv_sum = kv_sum + kv_first + kv_second
    go_sum = go_sum + go_next
    kv_next = shrink(kv_sum, 1, LONE)
    go_next = shrink(go_sum, 2, LONE)
    small = small + swap(small, FAR)
    kv_sum, kv_next, go_sum, go_next, small = sync(kv_sum, kv_next, go_sum, go_next, small)
    kv_sum = kv_sum + kv_next
    go_sum = go_sum + go_next
    kv_next = shrink(kv_sum, 2, LONE)
    for turn in range(3, last + 1):
        go_sum = go_sum + shrink(go_sum, turn, LONE)
    small = small + swap(small, 2)
    ff_grad = summed(ff_sum, 0, 1)[0]
    kv_sum, kv_next, small, ff_grad = sync(kv_sum, kv_next, small, ff_grad)
    kv_sum = kv_sum + kv_next
    for turn in range(3, last + 1):
        kv_sum = kv_sum + shrink(kv_sum, turn, LONE)
    for bit in bits[3:] + bits[:1]:
        small = small + swap(small, bit)
    group = small[4:6].reshape(-1)
    small = lax.dynamic_slice_in_dim(small, place() * sizes[0], sizes[0], 1)
    group = lax.dynamic_slice_in_dim(group, place() * sizes[4], sizes[4], 0)

    go_grad, kv_grad = summed(go_sum, 0, 1)[0], summed(kv_sum, 0, 1)[0]
    ff_mine, ff_got = finish_wide(ff_grad[:, :1024])
    go_mine, go_got = finish_wide(jnp.concatenate([go_grad[:, :1024], go_grad[:, 2048:]], axis=1))
    kv_mine, kv_got = finish_wide(kv_grad)

    def wide(mine, got, start, stop):
        return ordered(mine[:, start:stop], got[:, start:stop], 1)

    return (
        output.reshape(inputs.shape),
        input_grad.reshape(inputs.shape),
        small[0],
        small[1],
        wide(go_mine, go_got, 1024, 1536),
        wide(kv_mine, kv_got, 0, 512),
        wide(kv_mine, kv_got, 512, 1536),
        wide(go_mine, go_got, 0, 1024),
        group,
        finish_tall(go_grad[:, 1024:2048]),
        small[2],
        small[3],
        wide(ff_mine, ff_got, 0, 1024),
        finish_tall(ff_grad[:, 1024:2048]),
    )


def solution(mesh):
    return jax.shard_map(
        per_device,
        mesh=mesh,
        in_specs=(
            P(None, "dp", "seq", None),
            P(None, "dp", "seq"),
            P(("dp", "seq")),
            P(("dp", "seq")),
            P(("dp", "seq"), None),
            P(("dp", "seq"), None),
            P(("dp", "seq"), None),
            P(("dp", "seq"), None),
            P(("dp", "seq")),
            P(("dp", "seq"), None),
            P(("dp", "seq")),
            P(("dp", "seq")),
            P(("dp", "seq"), None),
            P(("dp", "seq"), None),
            P(None, "dp", "seq", None),
        ),
        out_specs=(
            P(None, "dp", "seq", None),
            P(None, "dp", "seq", None),
            P(("dp", "seq")),
            P(("dp", "seq")),
            P(("dp", "seq"), None),
            P(("dp", "seq"), None),
            P(("dp", "seq"), None),
            P(("dp", "seq"), None),
            P(("dp", "seq")),
            P(("dp", "seq"), None),
            P(("dp", "seq")),
            P(("dp", "seq")),
            P(("dp", "seq"), None),
            P(("dp", "seq"), None),
        ),
        check_vma=False,
    )
```

```python
import jax
import jax.numpy as jnp
from jax import lax
from jax.experimental import pallas as pl
from jax.experimental.pallas import tpu as pltpu
from jax.sharding import PartitionSpec as P

H = 4
QK = 256
VH = 512
AXES = ("dp", "seq")
F32 = jnp.float32
BF16 = jnp.bfloat16
FAR = 4
LONE, EDGE, EVEN = range(3)
MIB = 1024 * 1024


def mm(left, right):
    return lax.dot_general(left, right, (((1,), (0,)), ((), ())), preferred_element_type=F32)


def nt(left, right):
    return lax.dot_general(left, right, (((1,), (1,)), ((), ())), preferred_element_type=F32)


def tn(left, right):
    return lax.dot_general(left, right, (((0,), (0,)), ((), ())), preferred_element_type=F32)


def devices():
    return lax.axis_size("dp") * lax.axis_size("seq")


def place():
    return lax.axis_index("dp") * lax.axis_size("seq") + lax.axis_index("seq")


def swap(values, bit):
    return lax.ppermute(values, AXES, [(i, i ^ bit) for i in range(devices())])


def upper_core():
    return lax.axis_index("seq") % 2 == 1


def sync(*values):
    return lax.optimization_barrier(values)


def orders(kind):
    bits = [1 << k for k in range(1, devices().bit_length() - 1)]
    near = [bit for bit in bits if bit not in (2, FAR)]
    turned = near[1:] + near[:1]
    return {
        LONE: (near[:1] + [2] + near[1:] + [FAR], turned + [2, FAR]),
        EDGE: (near + [2, FAR], turned + [2, FAR]),
        EVEN: (near[:1] + [2] + near[1:] + [FAR], turned[:1] + [2] + turned[1:] + [FAR]),
    }[kind]


def step(values, turn, kind):
    pairs = [(i, i ^ orders(kind)[i % 2][turn]) for i in range(devices())]
    return lax.ppermute(values, AXES, pairs)


def chip_tables(kind):
    count = devices() // 2
    me, core = place() // 2, lax.axis_index("seq") % 2
    every = jnp.arange(count, dtype=jnp.int32)

    def spread_bits(values, sources, targets):
        return sum(((values >> s) & 1) << t for s, t in zip(sources, targets))

    spots, chips = [], []
    for order in orders(kind):
        sources = [bit.bit_length() - 2 for bit in order]
        targets = list(range(len(order)))[::-1]
        spots.append(spread_bits(every ^ me, sources, targets))
        chips.append(spread_bits(every, targets, sources) ^ me)
    swapped = core == 1
    return jnp.concatenate(
        [
            jnp.stack([me, core]),
            jnp.where(swapped, spots[1], spots[0]),
            jnp.where(swapped, spots[0], spots[1]),
            jnp.where(swapped, chips[1], chips[0]),
            jnp.where(swapped, chips[0], chips[1]),
        ]
    ).astype(jnp.int32)


def local(body, outs, *arrays, name):
    size = sum(a.size * a.dtype.itemsize for a in arrays)
    for shape, dtype in outs:
        extent = jnp.dtype(dtype).itemsize
        for length in shape:
            extent *= length
        size += extent

    def spec(shape):
        zeros = (0,) * len(shape)
        return pl.BlockSpec(shape, lambda k: zeros)

    return pl.pallas_call(
        body,
        grid=(1,),
        out_shape=[jax.ShapeDtypeStruct(shape, dtype) for shape, dtype in outs],
        in_specs=[
            pl.BlockSpec(memory_space=pltpu.SMEM) if a.dtype == jnp.int32 else spec(a.shape)
            for a in arrays
        ],
        out_specs=[spec(shape) for shape, _ in outs],
        compiler_params=pltpu.CompilerParams(vmem_limit_bytes=2 * size + 4 * MIB),
        cost_estimate=pl.CostEstimate(flops=1, bytes_accessed=1, transcendentals=0),
        name=name,
    )(*arrays)


def pack(info, *weights):
    width = sum(w.shape[1] for w in weights) // 2
    shape = (weights[0].shape[0], width)

    def body(info_ref, *refs):
        keep, give = refs[-2:]
        at = 0
        for ref in refs[:-2]:
            half = ref.shape[1] // 2
            here = pl.multiple_of(info_ref[1] * half, 128)
            there = pl.multiple_of((1 - info_ref[1]) * half, 128)
            keep[:, at : at + half] = ref[:, pl.ds(here, half)]
            give[:, at : at + half] = ref[:, pl.ds(there, half)]
            at += half

    return local(body, [(shape, BF16)] * 2, info, *weights, name="pack")


def stack_rows(info, keep, got):
    rows, width = keep.shape

    def body(info_ref, keep_ref, got_ref, out):
        upper = info_ref[1] == 1
        out[:rows] = jnp.where(upper, got_ref[...], keep_ref[...])
        out[rows:] = jnp.where(upper, keep_ref[...], got_ref[...])

    return local(body, [((2 * rows, width), BF16)], info, keep, got, name="stack")[0]


def join(part, got):
    half = part.shape[0]

    def body(part_ref, got_ref, out):
        out[:half] = part_ref[...]
        out[half:] = got_ref[...]

    outs = [((2 * half,) + part.shape[1:], BF16)]
    return local(body, outs, part, got, name="join")[0]


def settle(info, pieces, own):
    lengths = [piece.shape[0] for piece in pieces]
    chips = sum(lengths)

    def body(info_ref, *refs):
        at = 0
        for ref, length in zip(refs, lengths):
            for block in range(length):
                refs[-1][info_ref[2 + (2 if own else 3) * chips + at]] = ref[block]
                at += 1

    outs = [((chips,) + pieces[0].shape[1:], BF16)]
    return local(body, outs, info, *pieces, name="settle")[0]


@jax.tree_util.register_pytree_node_class
class Piece:
    def __init__(self, array, start=0):
        self.array, self.start = array, start

    def tree_flatten(self):
        return (self.array,), self.start

    @classmethod
    def tree_unflatten(cls, start, children):
        return cls(children[0], start)


def summed(pieces, start, stop):
    total = None
    for piece in pieces:
        first, last = start - piece.start, stop - piece.start
        if 0 <= first and last <= piece.array.shape[0]:
            value = piece.array[first:last].astype(F32)
            total = value if total is None else total + value
    return total


def span(turn):
    length = devices() // 2 >> turn
    return length // 2, length


def upper_part(pieces, turn, part=None):
    start, stop = span(turn)
    shift = start
    if part is not None:
        middle = (start + stop) // 2
        start, stop = (middle, stop) if part else (start, middle)
    return Piece(summed(pieces, start, stop).astype(BF16), start - shift)


def send(piece, turn, kind):
    return [Piece(step(piece.array, turn, kind), piece.start)]


def shrink(pieces, turn, kind, part=None):
    return send(upper_part(pieces, turn, part), turn, kind)


def ordered(mine, other, axis):
    upper = upper_core()
    return jnp.concatenate(
        [jnp.where(upper, other, mine), jnp.where(upper, mine, other)], axis=axis
    )


def finish_wide(values):
    rows = values.shape[0] // 2
    upper = upper_core()
    low, high = values[:rows], values[rows:]
    mine, give = jnp.where(upper, high, low), jnp.where(upper, low, high)
    return mine, swap(give, 1)


def finish_tall(values):
    half = values.shape[1] // 2
    upper = upper_core()
    low, high = values[:, :half], values[:, half:]
    mine, give = jnp.where(upper, high, low), jnp.where(upper, low, high)
    return ordered(mine, swap(give, 1), 1)


def phase_count(rows):
    return lax.axis_size("seq") // 2 - 1 + rows - 1


def chip_place(reverse):
    chips = lax.axis_size("seq") // 2
    at = lax.axis_index("seq") // 2
    return chips - 1 - at if reverse else at


def row_at(phase, rows, reverse):
    return jnp.clip(phase - 1 - chip_place(reverse), 0, rows - 1)


def factors_of(carry, near_carry, reverse):
    rows = carry.shape[0]
    upper = upper_core()
    turned = jnp.logical_not(upper) if reverse else upper
    one, zero = jnp.ones_like(carry), jnp.zeros_like(carry)

    def either(yes, no):
        return jnp.where(turned, yes, no)

    table = (either(one, near_carry), either(carry, one), carry * near_carry)
    passed = []
    for phase in range(1, phase_count(rows) + 1):
        row = row_at(phase, rows, reverse)
        passed.append([
            sum(jnp.where(row == k, factor[k], 0.0) for k in range(rows))[:, None, None]
            for factor in table
        ])
    mine = (either(zero, zero), either(one, zero), either(near_carry, one))
    theirs = (either(zero, one), either(zero, zero), either(one, carry))
    return passed, [[f[:, :, None, None] for f in side] for side in (mine, theirs)]


def hop(states, arrived, phase, reverse):
    passed, _, own, near = states
    rows = own.shape[0]
    row = row_at(phase, rows, reverse)
    a, b, c = passed[phase - 1]
    message = a * lax.dynamic_index_in_dim(own, row, 0, False)
    message = message + b * lax.dynamic_index_in_dim(near, row, 0, False)
    if arrived:
        message = message + c * arrived[-1].astype(F32)
    chips = lax.axis_size("seq") // 2
    pairs = []
    for at in range(chips - 1):
        if 0 <= phase - 1 - at < rows:
            source, target = (chips - 1 - at, chips - 2 - at) if reverse else (at, at + 1)
            pairs += [(2 * source + core, 2 * target + core) for core in range(2)]
    return lax.ppermute(message.astype(BF16), "seq", pairs)


def end_states(states, arrived, reverse):
    _, (mine, theirs), own, near = states
    at = chip_place(reverse)
    chips = lax.axis_size("seq") // 2
    before = []
    for row in range(own.shape[0]):
        value = jnp.zeros_like(arrived[0])
        for other in range(1, chips):
            value = jnp.where(at == other, arrived[row + other - 1], value)
        before.append(value.astype(F32))
    before = jnp.stack(before)

    def taken(factors):
        a, b, c = factors
        return (a * own + b * near + c * before).astype(BF16)

    return taken(mine), swap(taken(theirs), 1)


def call(body, grid, info, ins, outs, scratch, flops, name, vmem):
    def spec(shape, block, index, once):
        if block is None:
            return pl.BlockSpec(memory_space=pltpu.SMEM)
        if once and block == shape and name == "feed":
            return pl.BlockSpec(block, index, pipeline_mode=pl.Buffered(1))
        return pl.BlockSpec(block, index)

    moved = sum(a.size * a.dtype.itemsize for a, _, _ in ins)
    for shape, dtype, _, _ in outs:
        size = jnp.dtype(dtype).itemsize
        for extent in shape:
            size *= extent
        moved += size
    return pl.pallas_call(
        body,
        grid_spec=pltpu.PrefetchScalarGridSpec(
            num_scalar_prefetch=1,
            grid=(grid,),
            in_specs=[spec(a.shape, block, index, True) for a, block, index in ins],
            out_specs=[spec(shape, block, index, False) for shape, _, block, index in outs],
            scratch_shapes=scratch,
        ),
        out_shape=[jax.ShapeDtypeStruct(shape, dtype) for shape, dtype, _, _ in outs],
        compiler_params=pltpu.CompilerParams(
            vmem_limit_bytes=vmem * MIB, dimension_semantics=("arbitrary",)
        ),
        cost_estimate=pl.CostEstimate(flops=1, bytes_accessed=1, transcendentals=0),
        name=name,
    )(info, *[a for a, _, _ in ins])


def whole(array):
    zeros = (0,) * array.ndim
    return (array, array.shape, lambda h, info: zeros)


def whole_out(shape, dtype):
    zeros = (0,) * len(shape)
    return (shape, dtype, shape, lambda h, info: zeros)


def head_in(array):
    rest = (0,) * (array.ndim - 1)
    return (array, (1,) + array.shape[1:], lambda h, info: (h,) + rest)


def head_out(shape, dtype):
    rest = (0,) * (len(shape) - 1)
    return (shape, dtype, (1,) + shape[1:], lambda h, info: (h,) + rest)


def state_block(shape, own):
    block = (shape[0], 1) + shape[2:]
    if own:
        return block, lambda h, info: (0, jnp.minimum(h, 1), 0, 0)
    return block, lambda h, info: (0, jnp.maximum(h - 2, 0), 0, 0)


def own_in(array):
    return (array,) + state_block(array.shape, True)


def other_in(array):
    return (array,) + state_block(array.shape, False)


def own_out(shape, dtype):
    return (shape, dtype) + state_block(shape, True)


def other_out(shape, dtype):
    return (shape, dtype) + state_block(shape, False)


def real(h, info):
    return lax.rem(h + 2 * info[1], 4)


def real_in(array):
    rest = (0,) * (array.ndim - 1)
    return (array, (1,) + array.shape[1:], lambda h, info: (real(h, info),) + rest)


def columns(array, width, first, own):
    block = array.shape[:2] + (width,)
    if own:
        return (array, block, lambda h, info: (0, 0, first + jnp.minimum(h, 1)))
    return (array, block, lambda h, info: (0, 0, first + jnp.maximum(h - 2, 0)))


def tall(array):
    block = (array.shape[0] // 4, array.shape[1], 1024)
    return (array, block, lambda h, info: (real(h, info), 0, 1))


def tall_rows(ref):
    chips = ref.shape[0]
    pieces = []
    for chip in range(chips):
        pieces += [ref[chip, :, :512], ref[chip, :, 512:]]
    return jnp.concatenate(pieces, axis=0)


def flat(ref):
    chips, rows, width = ref.shape
    return ref[...].reshape(chips * rows, width)


def side(info, own):
    return pl.multiple_of(512 * (info[1] if own else 1 - info[1]), 512)


def put_wide(target, info, values, start, own):
    chips, rows, _ = target.shape
    width = values.shape[1]
    values = values.astype(BF16)
    for chip in range(chips):
        target[info[(2 if own else 2 + chips) + chip], :, start : start + width] = values[chip * rows : (chip + 1) * rows]


def put_tall(target, info, values, block, start, own):
    chips, rows, _ = target.shape
    values = values.astype(BF16)
    share = chips // 4
    for chip in range(share):
        at = info[(2 if own else 2 + chips) + block * share + chip]
        base = 2 * rows * chip
        target[at, :, start : start + 512] = values[base : base + rows]
        target[at, :, start + 512 : start + 1024] = values[base + rows : base + 2 * rows]


def rotated(values, cosine, sine):
    a, b = values[:, :128], values[:, 128:]
    return jnp.concatenate([a * cosine - b * sine, b * cosine + a * sine], axis=1)


def unrotated(values, cosine, sine):
    a, b = values[:, :128], values[:, 128:]
    return jnp.concatenate([a * cosine + b * sine, b * cosine - a * sine], axis=1)


def mask_of(rate, tall_count, wide_count):
    length = tall_count.shape[0]
    i = lax.broadcasted_iota(jnp.int32, (length, length), 0)
    s = lax.broadcasted_iota(jnp.int32, (length, length), 1)
    decay = jnp.exp((i - s).astype(F32) * rate)
    return jnp.where((tall_count == wide_count) & (i >= s), decay, 0.0)


def enter_of(rate, tall_count):
    i = lax.broadcasted_iota(jnp.int32, tall_count.shape, 0)
    return jnp.where(tall_count == 0, jnp.exp((i + 1).astype(F32) * rate), 0.0)


def leave_of(rate, tall_count):
    length = tall_count.shape[0]
    i = lax.broadcasted_iota(jnp.int32, tall_count.shape, 0)
    last = tall_count[length - 1 :, :]
    return jnp.where(tall_count == last, jnp.exp((length - 1 - i).astype(F32) * rate), 0.0)


def norm_parts(values, eps):
    average = jnp.mean(values, axis=-1, keepdims=True)
    centred = values - average
    spread_ = jnp.mean(centred * centred, axis=-1, keepdims=True)
    scale = lax.rsqrt(spread_ + eps)
    return centred * scale, scale


def norm_back(grad, normal, scale):
    first = jnp.mean(grad, axis=-1, keepdims=True)
    second = jnp.mean(grad * normal, axis=-1, keepdims=True)
    return scale * (grad - first - normal * second)


CHUNK = 64


def norm_kernel(info, x, gain, bias, normed, normed_t):
    @pl.loop(0, x.shape[0] // CHUNK)
    def _(k):
        at = pl.ds(pl.multiple_of(k * CHUNK, CHUNK), CHUNK)
        normal, _ = norm_parts(x[at, :].astype(F32), 1e-05)
        normed[at, :] = (normal * gain[...].astype(F32) + bias[...].astype(F32)).astype(BF16)

    normed_t[...] = normed[...].T


def project_kernel(
    info, rates, normed, cosine, sine, tall_count, wide_count,
    q_own, k_own, v_own, q_oth, k_oth, v_oth,
    q_out, k_out, v_out, mix_out, inner_out, sum_own, sum_oth, pre,
):
    h = pl.program_id(0)

    def fill(wq, wk, wv):
        left = normed[...]
        pre[:, :256] = mm(left, flat(wq))
        pre[:, 256:512] = mm(left, flat(wk))
        pre[:, 512:] = mm(left, flat(wv))

    @pl.when(h < 2)
    def _():
        fill(q_own, k_own, v_own)

    @pl.when(h >= 2)
    def _():
        fill(q_oth, k_oth, v_oth)

    rate = rates[h]
    length = cosine.shape[0]
    for row in range(tall_count.shape[0]):
        at = slice(row * length, (row + 1) * length)
        count = tall_count[row]
        query = rotated(pre[at, :256], cosine[...], sine[...]).astype(BF16)
        key = (rotated(pre[at, 256:512], cosine[...], sine[...]) * QK**-0.5).astype(BF16)
        value = pre[at, 512:].astype(BF16)
        q_out[0, at] = query
        k_out[0, at] = key
        v_out[0, at] = value
        mixing = (nt(query, key) * mask_of(rate, count, wide_count[row])).astype(BF16)
        mix_out[0, at] = mixing
        inner_out[0, at] = mm(mixing, value)
        weighted = (key.astype(F32) * leave_of(rate, count)).astype(BF16)
        summary = tn(weighted, value)

        @pl.when(h < 2)
        def _():
            sum_own[row, 0] = summary

        @pl.when(h >= 2)
        def _():
            sum_oth[row, 0] = summary


def gate_kernel(info, normed, own, oth, out):
    h = pl.program_id(0)

    @pl.when(h < 2)
    def _():
        out[0] = mm(normed[...], flat(own))

    @pl.when(h >= 2)
    def _():
        out[0] = mm(normed[...], flat(oth))


def mix_kernel(
    info, rates, x, gain, second_gain, second_bias, tall_count, query, inner, gate,
    state_own, state_oth, wo_own, wo_oth,
    retained, mixed_t, hidden, normed, normed_t,
):
    h = pl.program_id(0)
    rate = rates[h]
    length = tall_count.shape[1]

    @pl.when(h == 0)
    def _():
        hidden[...] = x[...].astype(F32)

    for row in range(tall_count.shape[0]):
        at = slice(row * length, (row + 1) * length)
        entered = (query[0, at].astype(F32) * enter_of(rate, tall_count[row])).astype(BF16)

        @pl.when(h < 2)
        def _():
            retained[0, at] = inner[0, at] + mm(entered, state_own[row, 0])

        @pl.when(h >= 2)
        def _():
            retained[0, at] = inner[0, at] + mm(entered, state_oth[row, 0])

    normal, _ = norm_parts(retained[0], 1.0)
    pre = gate[0]
    mixed = (pre / (1.0 + jnp.exp(-pre)) * (normal * gain[0].astype(F32))).astype(BF16)
    mixed_t[0] = mixed.T
    hidden[:, pl.ds(side(info, True), 512)] += mm(mixed, tall_rows(wo_own))
    hidden[:, pl.ds(side(info, False), 512)] += mm(mixed, tall_rows(wo_oth))

    @pl.when(h == 3)
    def _():
        @pl.loop(0, x.shape[0] // CHUNK)
        def _(k):
            at = pl.ds(pl.multiple_of(k * CHUNK, CHUNK), CHUNK)
            normal, _ = norm_parts(hidden[at, :], 1e-05)
            normed[at, :] = (
                normal * second_gain[...].astype(F32) + second_bias[...].astype(F32)
            ).astype(BF16)

        normed_t[...] = normed[...].T


def feed_kernel(
    info, hidden, normed, normed_t, cot, second_gain,
    up_own, up_oth, down_own, down_oth,
    output, grad_hidden, grad_low, grad_gain, grad_bias, g_own, g_oth,
    upward, out_sum, norm_sum,
):
    f = pl.program_id(0)
    own_at = pl.ds(side(info, True), 512)
    oth_at = pl.ds(side(info, False), 512)

    @pl.when(f == 0)
    def _():
        out_sum[...] = hidden[...]
        norm_sum[...] = jnp.zeros_like(norm_sum)

    @pl.when(f < 2)
    def _():
        upward[...] = mm(normed[...], flat(up_own))

    @pl.when(f >= 2)
    def _():
        upward[...] = mm(normed[...], flat(up_oth))

    up = upward[...]
    root = 0.7978845608028654
    squared = up * up
    bent = jnp.tanh(root * (up + 0.044715 * (squared * up)))
    activated = (0.5 * up * (1.0 + bent)).astype(BF16)
    slope = 0.5 * (1.0 + bent) + 0.5 * up * (1.0 - bent * bent) * (
        root * (1.0 + 3 * 0.044715 * squared)
    )
    own, oth = tall_rows(down_own), tall_rows(down_oth)
    out_sum[:, own_at] += mm(activated, own)
    out_sum[:, oth_at] += mm(activated, oth)
    grad_up = (slope * (nt(cot[:, own_at], own) + nt(cot[:, oth_at], oth))).astype(BF16)
    block = real(f, info)
    act_t = activated.T
    put_tall(g_own, info, mm(act_t, cot[:, own_at]), block, 1024, True)
    put_tall(g_oth, info, mm(act_t, cot[:, oth_at]), block, 1024, False)
    grad_w = mm(normed_t[...], grad_up)
    for step in range(4):

        @pl.when(f == step)
        def _():
            put_wide(g_own if step < 2 else g_oth, info, grad_w, 512 * (step % 2), step < 2)

    @pl.when(f < 2)
    def _():
        norm_sum[...] += nt(grad_up, flat(up_own))

    @pl.when(f >= 2)
    def _():
        norm_sum[...] += nt(grad_up, flat(up_oth))

    @pl.when(f == 3)
    def _():
        grad_gain[...] = jnp.zeros_like(grad_gain)
        grad_bias[...] = jnp.zeros_like(grad_bias)

        @pl.loop(0, hidden.shape[0] // CHUNK)
        def _(k):
            at = pl.ds(pl.multiple_of(k * CHUNK, CHUNK), CHUNK)
            output[at, :] = out_sum[at, :].astype(BF16)
            normal, scale = norm_parts(hidden[at, :], 1e-05)
            grad = norm_sum[at, :]
            grad_gain[...] += jnp.sum(grad * normal, axis=0, keepdims=True)
            grad_bias[...] += jnp.sum(grad, axis=0, keepdims=True)
            total = cot[at, :].astype(F32) + norm_back(
                grad * second_gain[...].astype(F32), normal, scale
            )
            grad_hidden[at, :] = total
            grad_low[at, :] = total.astype(BF16)


def unmix_kernel(
    info, rates, grad_low, gain, tall_count, query, retained, gate, wo_own, wo_oth,
    grad_ret, grad_gate, grad_gain, state_own, state_oth,
):
    h = pl.program_id(0)
    rate = rates[h]
    length = tall_count.shape[1]
    grad = nt(grad_low[:, pl.ds(side(info, True), 512)], tall_rows(wo_own)) + nt(
        grad_low[:, pl.ds(side(info, False), 512)], tall_rows(wo_oth)
    )
    normal, scale = norm_parts(retained[0], 1.0)
    pre = gate[0]
    share = 1.0 / (1.0 + jnp.exp(-pre))
    curve = pre * share
    scaled = gain[0].astype(F32)
    grad_gate[0] = (grad * (normal * scaled) * (share * (1.0 + pre * (1.0 - share)))).astype(BF16)
    grad_normal = grad * curve
    grad_gain[0] = jnp.sum(grad_normal * normal, axis=0, keepdims=True)
    grad_ret[0] = norm_back(grad_normal * scaled, normal, scale).astype(BF16)
    for row in range(tall_count.shape[0]):
        at = slice(row * length, (row + 1) * length)
        entered = (query[0, at].astype(F32) * enter_of(rate, tall_count[row])).astype(BF16)
        state = tn(entered, grad_ret[0, at])

        @pl.when(h < 2)
        def _():
            state_own[row, 0] = state

        @pl.when(h >= 2)
        def _():
            state_oth[row, 0] = state


def inside_kernel(
    info, rates, grad_ret, query, key, value, mixing,
    cosine, sine, tall_count, wide_count, state_own, state_oth,
    grad_q, key_part, value_part,
):
    h = pl.program_id(0)
    rate = rates[h]
    length = cosine.shape[0]
    for row in range(tall_count.shape[0]):
        at = slice(row * length, (row + 1) * length)
        grad = grad_ret[0, at]
        mask = mask_of(rate, tall_count[row], wide_count[row])
        scores = (nt(grad, value[0, at]) * mask).astype(BF16)
        enter = enter_of(rate, tall_count[row])

        def set_query(state):
            total = mm(scores, key[0, at]) + nt(grad, state[row, 0]) * enter
            grad_q[0, at] = unrotated(total, cosine[...], sine[...]).astype(BF16)

        @pl.when(h < 2)
        def _():
            set_query(state_own)

        @pl.when(h >= 2)
        def _():
            set_query(state_oth)

        key_part[0, at] = tn(scores, query[0, at])
        value_part[0, at] = tn(mixing[0, at], grad)


def outer_kernel(
    info, grad_low, normed_t, mixed_t, grad_gate, grad_q, out_own, out_oth,
):
    h = pl.program_id(0)
    block = real(h, info)
    left = mixed_t[0]
    put_tall(out_own, info, mm(left, grad_low[:, pl.ds(side(info, True), 512)]), block, 1024, True)
    put_tall(out_oth, info, mm(left, grad_low[:, pl.ds(side(info, False), 512)]), block, 1024, False)
    grad_wg = mm(normed_t[...], grad_gate[0])
    grad_wq = mm(normed_t[...], grad_q[0])
    for step in range(4):

        @pl.when(h == step)
        def _():
            target = out_own if step < 2 else out_oth
            put_wide(target, info, grad_wg, 512 * (step % 2), step < 2)
            put_wide(target, info, grad_wq, 2048 + 256 * (step % 2), step < 2)


def last_kernel(
    info, rates, normed_t, key, value, key_part, value_part, cosine, sine, tall_count,
    state_own, state_oth,
    grad_k, grad_v, out_own, out_oth,
):
    h = pl.program_id(0)
    rate = rates[h]
    length = cosine.shape[0]
    for row in range(tall_count.shape[0]):
        at = slice(row * length, (row + 1) * length)
        leave = leave_of(rate, tall_count[row])
        weighted = (key[0, at].astype(F32) * leave).astype(BF16)

        def set_both(state):
            low = state[row, 0]
            grad_v[0, at] = (value_part[0, at] + mm(weighted, low)).astype(BF16)
            total = key_part[0, at] + nt(value[0, at], low) * leave
            grad_k[0, at] = (unrotated(total, cosine[...], sine[...]) * QK**-0.5).astype(BF16)

        @pl.when(h < 2)
        def _():
            set_both(state_own)

        @pl.when(h >= 2)
        def _():
            set_both(state_oth)

    grad_wk = mm(normed_t[...], grad_k[0])
    grad_wv = mm(normed_t[...], grad_v[0])
    for step in range(4):

        @pl.when(h == step)
        def _():
            target = out_own if step < 2 else out_oth
            put_wide(target, info, grad_wk, 256 * (step % 2), step < 2)
            put_wide(target, info, grad_wv, 512 + 512 * (step % 2), step < 2)


def input_kernel(
    info, x, gain, grad_hidden, grad_q, grad_k, grad_v, grad_gate,
    q_own, q_oth, k_own, k_oth, v_own, v_oth, g_own, g_oth,
    input_grad, grad_gain, grad_bias, norm_sum,
):
    h = pl.program_id(0)

    @pl.when(h == 0)
    def _():
        norm_sum[...] = jnp.zeros_like(norm_sum)

    def add(wq, wk, wv, wg):
        norm_sum[...] += (
            nt(grad_q[0], flat(wq)) + nt(grad_k[0], flat(wk))
            + nt(grad_v[0], flat(wv)) + nt(grad_gate[0], flat(wg))
        )

    @pl.when(h < 2)
    def _():
        add(q_own, k_own, v_own, g_own)

    @pl.when(h >= 2)
    def _():
        add(q_oth, k_oth, v_oth, g_oth)

    @pl.when(h == 3)
    def _():
        grad_gain[...] = jnp.zeros_like(grad_gain)
        grad_bias[...] = jnp.zeros_like(grad_bias)

        @pl.loop(0, x.shape[0] // CHUNK)
        def _(k):
            at = pl.ds(pl.multiple_of(k * CHUNK, CHUNK), CHUNK)
            normal, scale = norm_parts(x[at, :].astype(F32), 1e-05)
            grad = norm_sum[at, :]
            grad_gain[...] += jnp.sum(grad * normal, axis=0, keepdims=True)
            grad_bias[...] += jnp.sum(grad, axis=0, keepdims=True)
            input_grad[at, :] = grad_hidden[at, :] + norm_back(
                grad * gain[...].astype(F32), normal, scale
            )


def per_device(
    inputs,
    doc_flags,
    first_gain,
    first_bias,
    w_query,
    w_key,
    w_value,
    w_gate,
    group_gain,
    w_output,
    second_gain,
    second_bias,
    w_up,
    w_down,
    cotangent,
):
    batches, row_count, length, width = inputs.shape
    rows = batches * row_count
    tokens = rows * length
    count = devices()
    chips = count // 2
    info, info_edge = chip_tables(LONE), chip_tables(EDGE)
    x = inputs.reshape(tokens, width)
    cot = cotangent.reshape(tokens, width)

    upper = upper_core()
    share = w_query.shape[0]
    last = len(orders(LONE)[0]) - 1

    keep, give = pack(info, w_query, w_key, w_value)
    qkv = stack_rows(info, keep, swap(give, 1))
    vectors = [first_gain, first_bias, second_gain, second_bias, group_gain]
    qkv, vectors = sync(qkv, vectors)
    got_qkv = step(qkv[None], last, LONE)

    sizes = [v.shape[0] for v in vectors]
    edges = [sum(sizes[:k]) for k in range(len(sizes) + 1)]
    lanes = -(-edges[-1] // 128) * 128
    table = jnp.concatenate([v.reshape(1, -1) for v in vectors], axis=1)
    table = jnp.pad(table, ((0, 15), (0, lanes - edges[-1])))

    def table_step(table, done, bit):
        got = swap(table, bit)
        turned = (place() // bit) % 2 == 1
        spot = sum(1 for other in done if other > bit)
        done.append(bit)
        return jnp.stack(
            [jnp.where(turned, got, table), jnp.where(turned, table, got)], axis=spot
        )

    bits = [1 << k for k in range(count.bit_length() - 1)]
    done = []
    for bit in (1, FAR):
        table = table_step(table, done, bit)
    got_qkv, table = sync(got_qkv, table)
    part, got = qkv[None], got_qkv
    start = lax.axis_index("seq") * length
    for turn in range(last - 1, 1, -1):
        part = join(part, got)
        got = step(part, turn, LONE)
        if turn == last - 1:
            table = table_step(table, done, 2)
        part, got, table, w_gate, w_up, w_output, w_down, doc_flags, start = sync(
            part, got, table, w_gate, w_up, w_output, w_down, doc_flags, start
        )

    part = join(part, got)
    got = step(part, 1, LONE)
    for bit in bits[:2:-1]:
        table = table_step(table, done, bit)

    top_keep, top_give = pack(info, w_gate, w_up)
    tall_keep, tall_give = pack(info, w_output, w_down)
    top = stack_rows(info, top_keep, swap(top_give, 1))
    tall_got = swap(tall_give, 1)
    low, high = jnp.where(upper, tall_got, tall_keep), jnp.where(upper, tall_keep, tall_got)
    go = jnp.concatenate([top[:, :1024], low[:, :512], high[:, :512]], axis=1)
    ff = jnp.concatenate([top[:, 1024:], low[:, 512:], high[:, 512:]], axis=1)
    go_part, ff_part = go[None], ff[None]
    part, got, go_part, ff_part, table, doc_flags = sync(
        part, got, go_part, ff_part, table, doc_flags
    )

    pieces = [part, got, step(part, 0, LONE), step(got, 0, LONE)]
    go_got = step(go_part, last, EDGE)
    ff_got = step(ff_part, last, EDGE)
    vector = table.reshape(count, -1, lanes)[:, 0]
    first_gain, first_bias, second_gain, second_bias, group_gain = [
        vector[:, a:b].reshape(1, -1) for a, b in zip(edges[:-1], edges[1:])
    ]
    group_gain = group_gain.reshape(H, 1, VH)

    positions = start + jnp.arange(length, dtype=jnp.int32)
    frequency = 10000.0 ** (-jnp.arange(QK // 2, dtype=F32) / (QK // 2))
    angles = positions.astype(F32)[:, None] * frequency[None, :]
    cosine, sine = jnp.cos(angles), jnp.sin(angles)
    rates = jnp.log1p(-(2.0 ** (-5.0 - 3.0 * jnp.arange(H, dtype=F32))))
    rates = jnp.where(upper, jnp.roll(rates, 2), rates)
    counts = jnp.cumsum(doc_flags.reshape(rows, length), axis=-1, dtype=jnp.int32)
    tall_count, wide_count = counts[:, :, None], counts[:, None, :]
    open_row = (counts[:, -1] == 0).astype(F32)
    near_row = swap(open_row, 1)
    decay = jnp.exp(rates[:2] * float(length))
    carry, near_carry = decay[None] * open_row[:, None], decay[None] * near_row[:, None]
    ahead = factors_of(carry, near_carry, False)
    behind = factors_of(carry, near_carry, True)

    per_head = (H, tokens)
    state_shape = (rows, 2, QK, VH)
    grad_shape = (chips, 2 * share)
    rates_in = (rates, None, None)
    unit = 2.0 * tokens * width * 512

    normed, normed_t = call(
        norm_kernel,
        1,
        info,
        [whole(x), whole(first_gain), whole(first_bias)],
        [whole_out((tokens, width), BF16), whole_out((width, tokens), BF16)],
        [],
        unit / 100,
        "norm",
        16,
    )
    pieces, go_part, go_got, ff_part, ff_got, normed, normed_t, tables, gains = sync(
        pieces, go_part, go_got, ff_part, ff_got, normed, normed_t,
        (cosine, sine, tall_count, wide_count, ahead, behind, rates),
        (second_gain, second_bias, group_gain),
    )
    cosine, sine, tall_count, wide_count, ahead, behind, rates = tables
    second_gain, second_bias, group_gain = gains
    rates_in = (rates, None, None)

    qkv_own = settle(info, pieces, True)
    qkv_oth = swap(qkv_own, 1)
    go_part = join(go_part, go_got)
    go_got = step(go_part, last - 1, EDGE)
    qkv_own, qkv_oth, go_part, go_got, ff_part, ff_got = sync(
        qkv_own, qkv_oth, go_part, go_got, ff_part, ff_got
    )

    go_part = join(go_part, go_got)
    go_got = step(go_part, last - 2, EDGE)
    ff_part = join(ff_part, ff_got)
    ff_got = step(ff_part, last - 1, EDGE)
    (query, key, value, mixing, inner, sum_own, sum_oth) = call(
        project_kernel,
        H,
        info,
        [
            rates_in, whole(normed), whole(cosine), whole(sine),
            whole(tall_count), whole(wide_count),
            columns(qkv_own, 256, 0, True), columns(qkv_own, 256, 2, True),
            columns(qkv_own, 512, 2, True),
            columns(qkv_oth, 256, 0, False), columns(qkv_oth, 256, 2, False),
            columns(qkv_oth, 512, 2, False),
        ],
        [
            head_out(per_head + (QK,), BF16), head_out(per_head + (QK,), BF16),
            head_out(per_head + (VH,), BF16), head_out(per_head + (length,), BF16),
            head_out(per_head + (VH,), F32),
            own_out(state_shape, F32), other_out(state_shape, F32),
        ],
        [pltpu.VMEM((tokens, 1024), F32)],
        10 * unit,
        "project",
        56,
    )
    go_part, go_got, ff_part, ff_got, sum_own, sum_oth = sync(
        go_part, go_got, ff_part, ff_got, sum_own, sum_oth
    )
    for turn in range(last - 3, 0, -1):
        go_part = join(go_part, go_got)
        go_got = step(go_part, turn, EDGE)
        ff_part = join(ff_part, ff_got)
        ff_got = step(ff_part, turn + 1, EDGE)
        go_part, go_got, ff_part, ff_got = sync(go_part, go_got, ff_part, ff_got)
    sum_near = swap(sum_oth, 1)
    ff_part = join(ff_part, ff_got)
    sum_own, sum_near, go_part, go_got, ff_part = sync(
        sum_own, sum_near, go_part, go_got, ff_part
    )

    states = tuple(ahead) + (sum_own, sum_near)
    phases = phase_count(rows)
    arrivals = hop(states, [], 1, False)
    go_first = step(go_part, 0, EDGE)
    states, arrivals, go_part, go_got, go_first = sync(
        states, arrivals, go_part, go_got, go_first
    )
    arrived = [arrivals]

    arrivals = hop(states, arrived, 2, False)
    go_second = step(go_got, 0, EDGE)
    states, arrived, arrivals, pieces, ff_part = sync(
        states, arrived, arrivals, [go_part, go_got, go_first, go_second], ff_part
    )
    arrived = arrived + [arrivals]

    arrivals = hop(states, arrived, 3, False)
    ff_got = step(ff_part, 1, EDGE)
    go_own = settle(info_edge, pieces, True)
    go_oth = swap(go_own, 1)
    states, arrived, arrivals, go_own, go_oth, normed, ff_part, ff_got = sync(
        states, arrived, arrivals, go_own, go_oth, normed, ff_part, ff_got
    )
    arrived = arrived + [arrivals]

    for phase in range(4, phases + 1):
        arrivals = hop(states, arrived, phase, False)
        if phase == 4:
            ff_first = step(ff_part, 0, EDGE)
            ff_others = [swap(ff_part, 1), swap(ff_got, 1)]
            (gate,) = call(
                gate_kernel,
                H,
                info,
                [whole(normed), columns(go_own, 512, 0, True), columns(go_oth, 512, 0, False)],
                [head_out(per_head + (VH,), F32)],
                [],
                4 * unit,
                "gate",
                20,
            )
        states, arrived, arrivals, gate, ff_part, ff_got, ff_first, ff_others = sync(
            states, arrived, arrivals, gate, ff_part, ff_got, ff_first, ff_others
        )
        arrived = arrived + [arrivals]
    state_own, state_oth = end_states(states, arrived, False)
    state_own, state_oth, ff_got, ff_first = sync(state_own, state_oth, ff_got, ff_first)
    ff_second = step(ff_got, 0, EDGE)
    ff_others = ff_others + [swap(ff_first, 1)]

    retained, mixed_t, hidden, normed_second, normed_second_t = call(
        mix_kernel,
        H,
        info,
        [
            rates_in, whole(x), real_in(group_gain), whole(second_gain), whole(second_bias),
            whole(tall_count), head_in(query), head_in(inner), head_in(gate),
            own_in(state_own), other_in(state_oth), tall(go_own), tall(go_oth),
        ],
        [
            head_out(per_head + (VH,), F32), head_out((H, VH, tokens), BF16),
            whole_out((tokens, width), F32), whole_out((tokens, width), BF16),
            whole_out((width, tokens), BF16),
        ],
        [],
        5 * unit,
        "mix",
        32,
    )
    ff_second, ff_others, hidden = sync(ff_second, ff_others, hidden)
    ff_others = ff_others + [swap(ff_second, 1)]
    ff_own = settle(info_edge, [ff_part, ff_got, ff_first, ff_second], True)
    ff_oth = settle(info_edge, ff_others, False)
    output, grad_hidden, grad_low, grad_second_gain, grad_second_bias, ff_g_own, ff_g_oth = call(
        feed_kernel,
        4,
        info_edge,
        [
            whole(hidden), whole(normed_second), whole(normed_second_t), whole(cot),
            whole(second_gain),
            columns(ff_own, 512, 0, True), columns(ff_oth, 512, 0, False),
            tall(ff_own), tall(ff_oth),
        ],
        [
            whole_out((tokens, width), BF16), whole_out((tokens, width), F32),
            whole_out((tokens, width), BF16), whole_out((1, width), F32),
            whole_out((1, width), F32),
            whole_out(grad_shape + (2048,), BF16), whole_out(grad_shape + (2048,), BF16),
        ],
        [
            pltpu.VMEM((tokens, 512), F32), pltpu.VMEM((tokens, width), F32),
            pltpu.VMEM((tokens, width), F32),
        ],
        24 * unit,
        "feed",
        48,
    )

    ff_g_got = swap(ff_g_oth, 1)
    grad_ret, grad_gate, grad_group_gain, gstate_own, gstate_oth = call(
        unmix_kernel,
        H,
        info,
        [
            rates_in, whole(grad_low), real_in(group_gain), whole(tall_count), head_in(query),
            head_in(retained), head_in(gate), tall(go_own), tall(go_oth),
        ],
        [
            head_out(per_head + (VH,), BF16), head_out(per_head + (VH,), BF16),
            (
                (H, 1, VH), F32, (1, 1, VH),
                lambda h, info: (real(h, info), 0, 0),
            ),
            own_out(state_shape, F32), other_out(state_shape, F32),
        ],
        [],
        5 * unit,
        "unmix",
        32,
    )
    ff_g_own, ff_g_got, gstate_own, gstate_oth, grad_gate, grad_ret = sync(
        ff_g_own, ff_g_got, gstate_own, gstate_oth, grad_gate, grad_ret
    )
    gstate_near = swap(gstate_oth, 1)
    ff_sum = [Piece(ff_g_own), Piece(ff_g_got)]
    ff_first = upper_part(ff_sum, 0, 1)
    gstate_own, gstate_near, grad_gate, grad_ret, ff_sum, ff_first = sync(
        gstate_own, gstate_near, grad_gate, grad_ret, ff_sum, ff_first
    )

    states = tuple(behind) + (gstate_own, gstate_near)
    arrived = []
    arrivals = hop(states, arrived, 1, True)
    ff_first = send(ff_first, 0, EDGE)
    ff_second = upper_part(ff_sum, 0, 0)
    grad_q, key_part, value_part = call(
        inside_kernel,
        H,
        info,
        [
            rates_in, head_in(grad_ret),
            head_in(query), head_in(key), head_in(value), head_in(mixing),
            whole(cosine), whole(sine), whole(tall_count), whole(wide_count),
            own_in(state_own), other_in(state_oth),
        ],
        [
            head_out(per_head + (QK,), BF16),
            head_out(per_head + (QK,), F32), head_out(per_head + (VH,), F32),
        ],
        [],
        3 * unit,
        "inside",
        24,
    )
    states, arrivals, ff_sum, ff_first, ff_second, grad_q, key_part, value_part = sync(
        states, arrivals, ff_sum, ff_first, ff_second, grad_q, key_part, value_part
    )
    arrived = arrived + [arrivals]

    arrivals = hop(states, arrived, 2, True)
    ff_sum = ff_sum + ff_first
    ff_second = send(ff_second, 0, EDGE)
    ff_next = upper_part(ff_sum, 1)
    go_g_own, go_g_oth = call(
        outer_kernel,
        H,
        info,
        [
            whole(grad_low), whole(normed_t), head_in(mixed_t), head_in(grad_gate),
            head_in(grad_q),
        ],
        [whole_out(grad_shape + (2560,), BF16), whole_out(grad_shape + (2560,), BF16)],
        [],
        11 * unit,
        "outer",
        44,
    )
    states, arrived, arrivals, ff_sum, ff_second, ff_next, go_g_own, go_g_oth = sync(
        states, arrived, arrivals, ff_sum, ff_second, ff_next, go_g_own, go_g_oth
    )
    ff_sum = ff_sum + ff_second
    arrived = arrived + [arrivals]

    arrivals = hop(states, arrived, 3, True)
    go_g_got = swap(go_g_oth, 1)
    ff_sum = ff_sum + send(ff_next, 1, EDGE)
    go_sum = [Piece(go_g_own), Piece(go_g_got)]
    go_first = upper_part(go_sum, 0, 1)
    states, arrived, arrivals, go_sum, go_first, ff_sum = sync(
        states, arrived, arrivals, go_sum, go_first, ff_sum
    )
    arrived = arrived + [arrivals]

    for phase in range(4, phases + 1):
        arrivals = hop(states, arrived, phase, True)
        if phase == 4:
            go_first = send(go_first, 0, LONE)
            go_second = upper_part(go_sum, 0, 0)
            ff_next = upper_part(ff_sum, 2)
        states, arrived, arrivals, go_sum, go_first, go_second, ff_sum, ff_next = sync(
            states, arrived, arrivals, go_sum, go_first, go_second, ff_sum, ff_next
        )
        arrived = arrived + [arrivals]
    after_own, after_oth = end_states(states, arrived, True)
    after_own, after_oth, go_sum, go_first, go_second, ff_sum, ff_next = sync(
        after_own, after_oth, go_sum, go_first, go_second, ff_sum, ff_next
    )
    go_sum = go_sum + go_first
    go_next = upper_part(go_sum, 1)
    go_second = send(go_second, 0, LONE)
    ff_sum = ff_sum + send(ff_next, 2, EDGE)

    grad_k, grad_v, kv_g_own, kv_g_oth = call(
        last_kernel,
        H,
        info,
        [
            rates_in, whole(normed_t), head_in(key), head_in(value), head_in(key_part),
            head_in(value_part), whole(cosine), whole(sine), whole(tall_count),
            own_in(after_own), other_in(after_oth),
        ],
        [
            head_out(per_head + (QK,), BF16), head_out(per_head + (VH,), BF16),
            whole_out(grad_shape + (1536,), BF16), whole_out(grad_shape + (1536,), BF16),
        ],
        [],
        8 * unit,
        "last",
        32,
    )
    ff_sum, go_sum, go_second, go_next, kv_g_own, kv_g_oth, grad_k, grad_v = sync(
        ff_sum, go_sum, go_second, go_next, kv_g_own, kv_g_oth, grad_k, grad_v
    )
    go_sum = go_sum + go_second
    kv_g_got = swap(kv_g_oth, 1)
    ff_next = upper_part(ff_sum, 3)
    kv_g_own, kv_g_got, go_sum, ff_sum, ff_next = sync(
        kv_g_own, kv_g_got, go_sum, ff_sum, ff_next
    )
    kv_sum = [Piece(kv_g_own), Piece(kv_g_got)]
    kv_first, kv_second = shrink(kv_sum, 0, LONE, 1), shrink(kv_sum, 0, LONE, 0)
    go_next = send(go_next, 1, LONE)
    ff_sum = ff_sum + send(ff_next, 3, EDGE)
    for turn in range(4, last + 1):
        ff_sum = ff_sum + shrink(ff_sum, turn, EDGE)
    input_grad, grad_first_gain, grad_first_bias = call(
        input_kernel,
        H,
        info,
        [
            whole(x), whole(first_gain), whole(grad_hidden), head_in(grad_q),
            head_in(grad_k), head_in(grad_v), head_in(grad_gate),
            columns(qkv_own, 256, 0, True), columns(qkv_oth, 256, 0, False),
            columns(qkv_own, 256, 2, True), columns(qkv_oth, 256, 2, False),
            columns(qkv_own, 512, 2, True), columns(qkv_oth, 512, 2, False),
            columns(go_own, 512, 0, True), columns(go_oth, 512, 0, False),
        ],
        [
            whole_out((tokens, width), F32), whole_out((1, width), F32),
            whole_out((1, width), F32),
        ],
        [pltpu.VMEM((tokens, width), F32)],
        6 * unit,
        "input",
        56,
    )
    kv_sum, kv_first, kv_second, go_sum, go_next, ff_sum, input_grad, sums = sync(
        kv_sum, kv_first, kv_second, go_sum, go_next, ff_sum, input_grad,
        (grad_first_gain, grad_first_bias),
    )
    grad_first_gain, grad_first_bias = sums
    small = jnp.concatenate(
        [
            grad_first_gain, grad_first_bias, grad_second_gain, grad_second_bias,
            grad_group_gain.reshape(-1, width), jnp.zeros((2, width), F32),
        ],
        axis=0,
    )

    kv_sum = kv_sum + kv_first + kv_second
    go_sum = go_sum + go_next
    kv_next = shrink(kv_sum, 1, LONE)
    go_next = shrink(go_sum, 2, LONE)
    small = small + swap(small, FAR)
    kv_sum, kv_next, go_sum, go_next, small = sync(kv_sum, kv_next, go_sum, go_next, small)
    kv_sum = kv_sum + kv_next
    go_sum = go_sum + go_next
    kv_next = shrink(kv_sum, 2, LONE)
    for turn in range(3, last + 1):
        go_sum = go_sum + shrink(go_sum, turn, LONE)
    small = small + swap(small, 2)
    ff_grad = summed(ff_sum, 0, 1)[0]
    kv_sum, kv_next, small, ff_grad = sync(kv_sum, kv_next, small, ff_grad)
    kv_sum = kv_sum + kv_next
    for turn in range(3, last + 1):
        kv_sum = kv_sum + shrink(kv_sum, turn, LONE)
    for bit in bits[3:] + bits[:1]:
        small = small + swap(small, bit)
    group = small[4:6].reshape(-1)
    small = lax.dynamic_slice_in_dim(small, place() * sizes[0], sizes[0], 1)
    group = lax.dynamic_slice_in_dim(group, place() * sizes[4], sizes[4], 0)

    go_grad, kv_grad = summed(go_sum, 0, 1)[0], summed(kv_sum, 0, 1)[0]
    ff_mine, ff_got = finish_wide(ff_grad[:, :1024])
    go_mine, go_got = finish_wide(jnp.concatenate([go_grad[:, :1024], go_grad[:, 2048:]], axis=1))
    kv_mine, kv_got = finish_wide(kv_grad)

    def wide(mine, got, start, stop):
        return ordered(mine[:, start:stop], got[:, start:stop], 1)

    return (
        output.reshape(inputs.shape),
        input_grad.reshape(inputs.shape),
        small[0],
        small[1],
        wide(go_mine, go_got, 1024, 1536),
        wide(kv_mine, kv_got, 0, 512),
        wide(kv_mine, kv_got, 512, 1536),
        wide(go_mine, go_got, 0, 1024),
        group,
        finish_tall(go_grad[:, 1024:2048]),
        small[2],
        small[3],
        wide(ff_mine, ff_got, 0, 1024),
        finish_tall(ff_grad[:, 1024:2048]),
    )


def solution(mesh):
    return jax.shard_map(
        per_device,
        mesh=mesh,
        in_specs=(
            P(None, "dp", "seq", None),
            P(None, "dp", "seq"),
            P(("dp", "seq")),
            P(("dp", "seq")),
            P(("dp", "seq"), None),
            P(("dp", "seq"), None),
            P(("dp", "seq"), None),
            P(("dp", "seq"), None),
            P(("dp", "seq")),
            P(("dp", "seq"), None),
            P(("dp", "seq")),
            P(("dp", "seq")),
            P(("dp", "seq"), None),
            P(("dp", "seq"), None),
            P(None, "dp", "seq", None),
        ),
        out_specs=(
            P(None, "dp", "seq", None),
            P(None, "dp", "seq", None),
            P(("dp", "seq")),
            P(("dp", "seq")),
            P(("dp", "seq"), None),
            P(("dp", "seq"), None),
            P(("dp", "seq"), None),
            P(("dp", "seq"), None),
            P(("dp", "seq")),
            P(("dp", "seq"), None),
            P(("dp", "seq")),
            P(("dp", "seq")),
            P(("dp", "seq"), None),
            P(("dp", "seq"), None),
        ),
        check_vma=False,
    )
```

```python
import jax
import jax.numpy as jnp
from jax import lax
from jax.experimental import pallas as pl
from jax.experimental.pallas import tpu as pltpu
from jax.sharding import PartitionSpec as P

H = 4
QK = 256
VH = 512
AXES = ("dp", "seq")
F32 = jnp.float32
BF16 = jnp.bfloat16
FAR = 4
LONE, EDGE, EVEN = range(3)
MIB = 1024 * 1024


def mm(left, right):
    return lax.dot_general(left, right, (((1,), (0,)), ((), ())), preferred_element_type=F32)


def nt(left, right):
    return lax.dot_general(left, right, (((1,), (1,)), ((), ())), preferred_element_type=F32)


def tn(left, right):
    return lax.dot_general(left, right, (((0,), (0,)), ((), ())), preferred_element_type=F32)


def devices():
    return lax.axis_size("dp") * lax.axis_size("seq")


def place():
    return lax.axis_index("dp") * lax.axis_size("seq") + lax.axis_index("seq")


def swap(values, bit):
    return lax.ppermute(values, AXES, [(i, i ^ bit) for i in range(devices())])


def upper_core():
    return lax.axis_index("seq") % 2 == 1


def sync(*values):
    return lax.optimization_barrier(values)


def orders(kind):
    bits = [1 << k for k in range(1, devices().bit_length() - 1)]
    near = [bit for bit in bits if bit not in (2, FAR)]
    turned = near[1:] + near[:1]
    return {
        LONE: (near[:1] + [2] + near[1:] + [FAR], turned + [2, FAR]),
        EDGE: (near + [2, FAR], turned + [2, FAR]),
        EVEN: (near[:1] + [2] + near[1:] + [FAR], turned[:1] + [2] + turned[1:] + [FAR]),
    }[kind]


def step(values, turn, kind):
    pairs = [(i, i ^ orders(kind)[i % 2][turn]) for i in range(devices())]
    return lax.ppermute(values, AXES, pairs)


def chip_tables(kind):
    count = devices() // 2
    me, core = place() // 2, lax.axis_index("seq") % 2
    every = jnp.arange(count, dtype=jnp.int32)

    def spread_bits(values, sources, targets):
        return sum(((values >> s) & 1) << t for s, t in zip(sources, targets))

    spots, chips = [], []
    for order in orders(kind):
        sources = [bit.bit_length() - 2 for bit in order]
        targets = list(range(len(order)))[::-1]
        spots.append(spread_bits(every ^ me, sources, targets))
        chips.append(spread_bits(every, targets, sources) ^ me)
    swapped = core == 1
    return jnp.concatenate(
        [
            jnp.stack([me, core]),
            jnp.where(swapped, spots[1], spots[0]),
            jnp.where(swapped, spots[0], spots[1]),
            jnp.where(swapped, chips[1], chips[0]),
            jnp.where(swapped, chips[0], chips[1]),
        ]
    ).astype(jnp.int32)


def local(body, outs, *arrays, name):
    size = sum(a.size * a.dtype.itemsize for a in arrays)
    for shape, dtype in outs:
        extent = jnp.dtype(dtype).itemsize
        for length in shape:
            extent *= length
        size += extent

    def spec(shape):
        zeros = (0,) * len(shape)
        return pl.BlockSpec(shape, lambda k: zeros)

    return pl.pallas_call(
        body,
        grid=(1,),
        out_shape=[jax.ShapeDtypeStruct(shape, dtype) for shape, dtype in outs],
        in_specs=[
            pl.BlockSpec(memory_space=pltpu.SMEM) if a.dtype == jnp.int32 else spec(a.shape)
            for a in arrays
        ],
        out_specs=[spec(shape) for shape, _ in outs],
        compiler_params=pltpu.CompilerParams(vmem_limit_bytes=2 * size + 4 * MIB),
        cost_estimate=pl.CostEstimate(flops=1, bytes_accessed=1, transcendentals=0),
        name=name,
    )(*arrays)


def pack(info, *weights):
    width = sum(w.shape[1] for w in weights) // 2
    shape = (weights[0].shape[0], width)

    def body(info_ref, *refs):
        keep, give = refs[-2:]
        at = 0
        for ref in refs[:-2]:
            half = ref.shape[1] // 2
            here = pl.multiple_of(info_ref[1] * half, 128)
            there = pl.multiple_of((1 - info_ref[1]) * half, 128)
            keep[:, at : at + half] = ref[:, pl.ds(here, half)]
            give[:, at : at + half] = ref[:, pl.ds(there, half)]
            at += half

    return local(body, [(shape, BF16)] * 2, info, *weights, name="pack")


def stack_rows(info, keep, got):
    rows, width = keep.shape

    def body(info_ref, keep_ref, got_ref, out):
        upper = info_ref[1] == 1
        out[:rows] = jnp.where(upper, got_ref[...], keep_ref[...])
        out[rows:] = jnp.where(upper, keep_ref[...], got_ref[...])

    return local(body, [((2 * rows, width), BF16)], info, keep, got, name="stack")[0]


def join(part, got):
    half = part.shape[0]

    def body(part_ref, got_ref, out):
        out[:half] = part_ref[...]
        out[half:] = got_ref[...]

    outs = [((2 * half,) + part.shape[1:], BF16)]
    return local(body, outs, part, got, name="join")[0]


def settle(info, pieces, own):
    lengths = [piece.shape[0] for piece in pieces]
    chips = sum(lengths)

    def body(info_ref, *refs):
        at = 0
        for ref, length in zip(refs, lengths):
            for block in range(length):
                refs[-1][info_ref[2 + (2 if own else 3) * chips + at]] = ref[block]
                at += 1

    outs = [((chips,) + pieces[0].shape[1:], BF16)]
    return local(body, outs, info, *pieces, name="settle")[0]


@jax.tree_util.register_pytree_node_class
class Piece:
    def __init__(self, array, start=0):
        self.array, self.start = array, start

    def tree_flatten(self):
        return (self.array,), self.start

    @classmethod
    def tree_unflatten(cls, start, children):
        return cls(children[0], start)


def summed(pieces, start, stop):
    total = None
    for piece in pieces:
        first, last = start - piece.start, stop - piece.start
        if 0 <= first and last <= piece.array.shape[0]:
            value = piece.array[first:last].astype(F32)
            total = value if total is None else total + value
    return total


def span(turn):
    length = devices() // 2 >> turn
    return length // 2, length


def upper_part(pieces, turn, part=None):
    start, stop = span(turn)
    shift = start
    if part is not None:
        middle = (start + stop) // 2
        start, stop = (middle, stop) if part else (start, middle)
    return Piece(summed(pieces, start, stop).astype(BF16), start - shift)


def send(piece, turn, kind):
    return [Piece(step(piece.array, turn, kind), piece.start)]


def shrink(pieces, turn, kind, part=None):
    return send(upper_part(pieces, turn, part), turn, kind)


def ordered(mine, other, axis):
    upper = upper_core()
    return jnp.concatenate(
        [jnp.where(upper, other, mine), jnp.where(upper, mine, other)], axis=axis
    )


def finish_wide(values):
    rows = values.shape[0] // 2
    upper = upper_core()
    low, high = values[:rows], values[rows:]
    mine, give = jnp.where(upper, high, low), jnp.where(upper, low, high)
    return mine, swap(give, 1)


def finish_tall(values):
    half = values.shape[1] // 2
    upper = upper_core()
    low, high = values[:, :half], values[:, half:]
    mine, give = jnp.where(upper, high, low), jnp.where(upper, low, high)
    return ordered(mine, swap(give, 1), 1)


def phase_count(rows):
    return lax.axis_size("seq") // 2 - 1 + rows - 1


def chip_place(reverse):
    chips = lax.axis_size("seq") // 2
    at = lax.axis_index("seq") // 2
    return chips - 1 - at if reverse else at


def row_at(phase, rows, reverse):
    return jnp.clip(phase - 1 - chip_place(reverse), 0, rows - 1)


def factors_of(carry, near_carry, reverse):
    rows = carry.shape[0]
    upper = upper_core()
    turned = jnp.logical_not(upper) if reverse else upper
    one, zero = jnp.ones_like(carry), jnp.zeros_like(carry)

    def either(yes, no):
        return jnp.where(turned, yes, no)

    table = (either(one, near_carry), either(carry, one), carry * near_carry)
    passed = []
    for phase in range(1, phase_count(rows) + 1):
        row = row_at(phase, rows, reverse)
        passed.append([
            sum(jnp.where(row == k, factor[k], 0.0) for k in range(rows))[:, None, None]
            for factor in table
        ])
    mine = (either(zero, zero), either(one, zero), either(near_carry, one))
    theirs = (either(zero, one), either(zero, zero), either(one, carry))
    return passed, [[f[:, :, None, None] for f in side] for side in (mine, theirs)]


def hop(states, arrived, phase, reverse):
    passed, _, own, near = states
    rows = own.shape[0]
    row = row_at(phase, rows, reverse)
    a, b, c = passed[phase - 1]
    message = a * lax.dynamic_index_in_dim(own, row, 0, False)
    message = message + b * lax.dynamic_index_in_dim(near, row, 0, False)
    if arrived:
        message = message + c * arrived[-1].astype(F32)
    chips = lax.axis_size("seq") // 2
    pairs = []
    for at in range(chips - 1):
        if 0 <= phase - 1 - at < rows:
            source, target = (chips - 1 - at, chips - 2 - at) if reverse else (at, at + 1)
            pairs += [(2 * source + core, 2 * target + core) for core in range(2)]
    return lax.ppermute(message.astype(BF16), "seq", pairs)


def end_states(states, arrived, reverse):
    _, (mine, theirs), own, near = states
    at = chip_place(reverse)
    chips = lax.axis_size("seq") // 2
    before = []
    for row in range(own.shape[0]):
        value = jnp.zeros_like(arrived[0])
        for other in range(1, chips):
            value = jnp.where(at == other, arrived[row + other - 1], value)
        before.append(value.astype(F32))
    before = jnp.stack(before)

    def taken(factors):
        a, b, c = factors
        return (a * own + b * near + c * before).astype(BF16)

    return taken(mine), swap(taken(theirs), 1)


def call(body, grid, info, ins, outs, scratch, flops, name, vmem):
    def spec(shape, block, index, once):
        if block is None:
            return pl.BlockSpec(memory_space=pltpu.SMEM)
        if once and block == shape and name == "feed":
            return pl.BlockSpec(block, index, pipeline_mode=pl.Buffered(1))
        return pl.BlockSpec(block, index)

    moved = sum(a.size * a.dtype.itemsize for a, _, _ in ins)
    for shape, dtype, _, _ in outs:
        size = jnp.dtype(dtype).itemsize
        for extent in shape:
            size *= extent
        moved += size
    return pl.pallas_call(
        body,
        grid_spec=pltpu.PrefetchScalarGridSpec(
            num_scalar_prefetch=1,
            grid=(grid,),
            in_specs=[spec(a.shape, block, index, True) for a, block, index in ins],
            out_specs=[spec(shape, block, index, False) for shape, _, block, index in outs],
            scratch_shapes=scratch,
        ),
        out_shape=[jax.ShapeDtypeStruct(shape, dtype) for shape, dtype, _, _ in outs],
        compiler_params=pltpu.CompilerParams(
            vmem_limit_bytes=vmem * MIB, dimension_semantics=("arbitrary",)
        ),
        cost_estimate=pl.CostEstimate(flops=1, bytes_accessed=1, transcendentals=0),
        name=name,
    )(info, *[a for a, _, _ in ins])


def whole(array):
    zeros = (0,) * array.ndim
    return (array, array.shape, lambda h, info: zeros)


def whole_out(shape, dtype):
    zeros = (0,) * len(shape)
    return (shape, dtype, shape, lambda h, info: zeros)


def head_in(array):
    rest = (0,) * (array.ndim - 1)
    return (array, (1,) + array.shape[1:], lambda h, info: (h,) + rest)


def head_out(shape, dtype):
    rest = (0,) * (len(shape) - 1)
    return (shape, dtype, (1,) + shape[1:], lambda h, info: (h,) + rest)


def state_block(shape, own):
    block = (shape[0], 1) + shape[2:]
    if own:
        return block, lambda h, info: (0, jnp.minimum(h, 1), 0, 0)
    return block, lambda h, info: (0, jnp.maximum(h - 2, 0), 0, 0)


def own_in(array):
    return (array,) + state_block(array.shape, True)


def other_in(array):
    return (array,) + state_block(array.shape, False)


def own_out(shape, dtype):
    return (shape, dtype) + state_block(shape, True)


def other_out(shape, dtype):
    return (shape, dtype) + state_block(shape, False)


def real(h, info):
    return lax.rem(h + 2 * info[1], 4)


def real_in(array):
    rest = (0,) * (array.ndim - 1)
    return (array, (1,) + array.shape[1:], lambda h, info: (real(h, info),) + rest)


def columns(array, width, first, own):
    block = array.shape[:2] + (width,)
    if own:
        return (array, block, lambda h, info: (0, 0, first + jnp.minimum(h, 1)))
    return (array, block, lambda h, info: (0, 0, first + jnp.maximum(h - 2, 0)))


def tall(array):
    block = (array.shape[0] // 4, array.shape[1], 1024)
    return (array, block, lambda h, info: (real(h, info), 0, 1))


def tall_rows(ref):
    chips = ref.shape[0]
    pieces = []
    for chip in range(chips):
        pieces += [ref[chip, :, :512], ref[chip, :, 512:]]
    return jnp.concatenate(pieces, axis=0)


def flat(ref):
    chips, rows, width = ref.shape
    return ref[...].reshape(chips * rows, width)


def side(info, own):
    return pl.multiple_of(512 * (info[1] if own else 1 - info[1]), 512)


def put_wide(target, info, values, start, own):
    chips, rows, _ = target.shape
    width = values.shape[1]
    values = values.astype(BF16)
    for chip in range(chips):
        target[info[(2 if own else 2 + chips) + chip], :, start : start + width] = values[chip * rows : (chip + 1) * rows]


def put_tall(target, info, values, block, start, own):
    chips, rows, _ = target.shape
    values = values.astype(BF16)
    share = chips // 4
    for chip in range(share):
        at = info[(2 if own else 2 + chips) + block * share + chip]
        base = 2 * rows * chip
        target[at, :, start : start + 512] = values[base : base + rows]
        target[at, :, start + 512 : start + 1024] = values[base + rows : base + 2 * rows]


def rotated(values, cosine, sine):
    a, b = values[:, :128], values[:, 128:]
    return jnp.concatenate([a * cosine - b * sine, b * cosine + a * sine], axis=1)


def unrotated(values, cosine, sine):
    a, b = values[:, :128], values[:, 128:]
    return jnp.concatenate([a * cosine + b * sine, b * cosine - a * sine], axis=1)


def mask_of(rate, tall_count, wide_count):
    length = tall_count.shape[0]
    i = lax.broadcasted_iota(jnp.int32, (length, length), 0)
    s = lax.broadcasted_iota(jnp.int32, (length, length), 1)
    decay = jnp.exp((i - s).astype(F32) * rate)
    return jnp.where((tall_count == wide_count) & (i >= s), decay, 0.0)


def enter_of(rate, tall_count):
    i = lax.broadcasted_iota(jnp.int32, tall_count.shape, 0)
    return jnp.where(tall_count == 0, jnp.exp((i + 1).astype(F32) * rate), 0.0)


def leave_of(rate, tall_count):
    length = tall_count.shape[0]
    i = lax.broadcasted_iota(jnp.int32, tall_count.shape, 0)
    last = tall_count[length - 1 :, :]
    return jnp.where(tall_count == last, jnp.exp((length - 1 - i).astype(F32) * rate), 0.0)


def norm_parts(values, eps):
    average = jnp.mean(values, axis=-1, keepdims=True)
    centred = values - average
    spread_ = jnp.mean(centred * centred, axis=-1, keepdims=True)
    scale = lax.rsqrt(spread_ + eps)
    return centred * scale, scale


def norm_back(grad, normal, scale):
    first = jnp.mean(grad, axis=-1, keepdims=True)
    second = jnp.mean(grad * normal, axis=-1, keepdims=True)
    return scale * (grad - first - normal * second)


CHUNK = 64


def norm_kernel(info, x, gain, bias, normed, normed_t):
    @pl.loop(0, x.shape[0] // CHUNK)
    def _(k):
        at = pl.ds(pl.multiple_of(k * CHUNK, CHUNK), CHUNK)
        normal, _ = norm_parts(x[at, :].astype(F32), 1e-05)
        normed[at, :] = (normal * gain[...].astype(F32) + bias[...].astype(F32)).astype(BF16)

    normed_t[...] = normed[...].T


def project_kernel(
    info, rates, normed, cosine, sine, tall_count, wide_count,
    q_own, k_own, v_own, q_oth, k_oth, v_oth,
    q_out, k_out, v_out, mix_out, sum_own, sum_oth, pre,
):
    h = pl.program_id(0)

    def fill(wq, wk, wv):
        left = normed[...]
        pre[:, :256] = mm(left, flat(wq))
        pre[:, 256:512] = mm(left, flat(wk))
        pre[:, 512:] = mm(left, flat(wv))

    @pl.when(h < 2)
    def _():
        fill(q_own, k_own, v_own)

    @pl.when(h >= 2)
    def _():
        fill(q_oth, k_oth, v_oth)

    rate = rates[h]
    length = cosine.shape[0]
    for row in range(tall_count.shape[0]):
        at = slice(row * length, (row + 1) * length)
        count = tall_count[row]
        query = rotated(pre[at, :256], cosine[...], sine[...]).astype(BF16)
        key = (rotated(pre[at, 256:512], cosine[...], sine[...]) * QK**-0.5).astype(BF16)
        value = pre[at, 512:].astype(BF16)
        q_out[0, at] = query
        k_out[0, at] = key
        v_out[0, at] = value
        mixing = (nt(query, key) * mask_of(rate, count, wide_count[row])).astype(BF16)
        mix_out[0, at] = mixing
        weighted = (key.astype(F32) * leave_of(rate, count)).astype(BF16)
        summary = tn(weighted, value)

        @pl.when(h < 2)
        def _():
            sum_own[row, 0] = summary

        @pl.when(h >= 2)
        def _():
            sum_oth[row, 0] = summary


def gate_kernel(info, normed, own, oth, out):
    h = pl.program_id(0)

    @pl.when(h < 2)
    def _():
        out[0] = mm(normed[...], flat(own))

    @pl.when(h >= 2)
    def _():
        out[0] = mm(normed[...], flat(oth))


def mix_kernel(
    info, rates, x, gain, second_gain, second_bias, tall_count, query, value, mixing, gate,
    state_own, state_oth, wo_own, wo_oth,
    retained, mixed_t, hidden, normed, normed_t,
):
    h = pl.program_id(0)
    rate = rates[h]
    length = tall_count.shape[1]

    @pl.when(h == 0)
    def _():
        hidden[...] = x[...].astype(F32)

    for row in range(tall_count.shape[0]):
        at = slice(row * length, (row + 1) * length)
        entered = (query[0, at].astype(F32) * enter_of(rate, tall_count[row])).astype(BF16)

        inner = mm(mixing[0, at], value[0, at])

        @pl.when(h < 2)
        def _():
            retained[0, at] = inner + mm(entered, state_own[row, 0])

        @pl.when(h >= 2)
        def _():
            retained[0, at] = inner + mm(entered, state_oth[row, 0])

    normal, _ = norm_parts(retained[0], 1.0)
    pre = gate[0]
    mixed = (pre / (1.0 + jnp.exp(-pre)) * (normal * gain[0].astype(F32))).astype(BF16)
    mixed_t[0] = mixed.T
    hidden[:, pl.ds(side(info, True), 512)] += mm(mixed, tall_rows(wo_own))
    hidden[:, pl.ds(side(info, False), 512)] += mm(mixed, tall_rows(wo_oth))

    @pl.when(h == 3)
    def _():
        @pl.loop(0, x.shape[0] // CHUNK)
        def _(k):
            at = pl.ds(pl.multiple_of(k * CHUNK, CHUNK), CHUNK)
            normal, _ = norm_parts(hidden[at, :], 1e-05)
            normed[at, :] = (
                normal * second_gain[...].astype(F32) + second_bias[...].astype(F32)
            ).astype(BF16)

        normed_t[...] = normed[...].T


def feed_kernel(
    info, hidden, normed, normed_t, cot, second_gain,
    up_own, up_oth, down_own, down_oth,
    output, grad_hidden, grad_low, grad_gain, grad_bias, g_own, g_oth,
    upward, out_sum, norm_sum,
):
    f = pl.program_id(0)
    own_at = pl.ds(side(info, True), 512)
    oth_at = pl.ds(side(info, False), 512)

    @pl.when(f == 0)
    def _():
        out_sum[...] = hidden[...]
        norm_sum[...] = jnp.zeros_like(norm_sum)

    @pl.when(f < 2)
    def _():
        upward[...] = mm(normed[...], flat(up_own))

    @pl.when(f >= 2)
    def _():
        upward[...] = mm(normed[...], flat(up_oth))

    up = upward[...]
    root = 0.7978845608028654
    squared = up * up
    bent = jnp.tanh(root * (up + 0.044715 * (squared * up)))
    activated = (0.5 * up * (1.0 + bent)).astype(BF16)
    slope = 0.5 * (1.0 + bent) + 0.5 * up * (1.0 - bent * bent) * (
        root * (1.0 + 3 * 0.044715 * squared)
    )
    own, oth = tall_rows(down_own), tall_rows(down_oth)
    out_sum[:, own_at] += mm(activated, own)
    out_sum[:, oth_at] += mm(activated, oth)
    grad_up = (slope * (nt(cot[:, own_at], own) + nt(cot[:, oth_at], oth))).astype(BF16)
    block = real(f, info)
    act_t = activated.T
    put_tall(g_own, info, mm(act_t, cot[:, own_at]), block, 1024, True)
    put_tall(g_oth, info, mm(act_t, cot[:, oth_at]), block, 1024, False)
    grad_w = mm(normed_t[...], grad_up)
    for step in range(4):

        @pl.when(f == step)
        def _():
            put_wide(g_own if step < 2 else g_oth, info, grad_w, 512 * (step % 2), step < 2)

    @pl.when(f < 2)
    def _():
        norm_sum[...] += nt(grad_up, flat(up_own))

    @pl.when(f >= 2)
    def _():
        norm_sum[...] += nt(grad_up, flat(up_oth))

    @pl.when(f == 3)
    def _():
        grad_gain[...] = jnp.zeros_like(grad_gain)
        grad_bias[...] = jnp.zeros_like(grad_bias)

        @pl.loop(0, hidden.shape[0] // CHUNK)
        def _(k):
            at = pl.ds(pl.multiple_of(k * CHUNK, CHUNK), CHUNK)
            output[at, :] = out_sum[at, :].astype(BF16)
            normal, scale = norm_parts(hidden[at, :], 1e-05)
            grad = norm_sum[at, :]
            grad_gain[...] += jnp.sum(grad * normal, axis=0, keepdims=True)
            grad_bias[...] += jnp.sum(grad, axis=0, keepdims=True)
            total = cot[at, :].astype(F32) + norm_back(
                grad * second_gain[...].astype(F32), normal, scale
            )
            grad_hidden[at, :] = total
            grad_low[at, :] = total.astype(BF16)


def unmix_kernel(
    info, rates, grad_low, gain, tall_count, query, retained, gate, wo_own, wo_oth,
    grad_ret, grad_gate, grad_gain, state_own, state_oth,
):
    h = pl.program_id(0)
    rate = rates[h]
    length = tall_count.shape[1]
    grad = nt(grad_low[:, pl.ds(side(info, True), 512)], tall_rows(wo_own)) + nt(
        grad_low[:, pl.ds(side(info, False), 512)], tall_rows(wo_oth)
    )
    normal, scale = norm_parts(retained[0], 1.0)
    pre = gate[0]
    share = 1.0 / (1.0 + jnp.exp(-pre))
    curve = pre * share
    scaled = gain[0].astype(F32)
    grad_gate[0] = (grad * (normal * scaled) * (share * (1.0 + pre * (1.0 - share)))).astype(BF16)
    grad_normal = grad * curve
    grad_gain[0] = jnp.sum(grad_normal * normal, axis=0, keepdims=True)
    grad_ret[0] = norm_back(grad_normal * scaled, normal, scale).astype(BF16)
    for row in range(tall_count.shape[0]):
        at = slice(row * length, (row + 1) * length)
        entered = (query[0, at].astype(F32) * enter_of(rate, tall_count[row])).astype(BF16)
        state = tn(entered, grad_ret[0, at])

        @pl.when(h < 2)
        def _():
            state_own[row, 0] = state

        @pl.when(h >= 2)
        def _():
            state_oth[row, 0] = state


def inside_kernel(
    info, rates, grad_ret, query, key, value, mixing,
    cosine, sine, tall_count, wide_count, state_own, state_oth,
    grad_q, key_part, value_part,
):
    h = pl.program_id(0)
    rate = rates[h]
    length = cosine.shape[0]
    for row in range(tall_count.shape[0]):
        at = slice(row * length, (row + 1) * length)
        grad = grad_ret[0, at]
        mask = mask_of(rate, tall_count[row], wide_count[row])
        scores = (nt(grad, value[0, at]) * mask).astype(BF16)
        enter = enter_of(rate, tall_count[row])

        def set_query(state):
            total = mm(scores, key[0, at]) + nt(grad, state[row, 0]) * enter
            grad_q[0, at] = unrotated(total, cosine[...], sine[...]).astype(BF16)

        @pl.when(h < 2)
        def _():
            set_query(state_own)

        @pl.when(h >= 2)
        def _():
            set_query(state_oth)

        key_part[0, at] = tn(scores, query[0, at])
        value_part[0, at] = tn(mixing[0, at], grad)


def outer_kernel(
    info, grad_low, normed_t, mixed_t, grad_gate, grad_q, out_own, out_oth,
):
    h = pl.program_id(0)
    block = real(h, info)
    left = mixed_t[0]
    put_tall(out_own, info, mm(left, grad_low[:, pl.ds(side(info, True), 512)]), block, 1024, True)
    put_tall(out_oth, info, mm(left, grad_low[:, pl.ds(side(info, False), 512)]), block, 1024, False)
    grad_wg = mm(normed_t[...], grad_gate[0])
    grad_wq = mm(normed_t[...], grad_q[0])
    for step in range(4):

        @pl.when(h == step)
        def _():
            target = out_own if step < 2 else out_oth
            put_wide(target, info, grad_wg, 512 * (step % 2), step < 2)
            put_wide(target, info, grad_wq, 2048 + 256 * (step % 2), step < 2)


def last_kernel(
    info, rates, normed_t, key, value, key_part, value_part, cosine, sine, tall_count,
    state_own, state_oth,
    grad_k, grad_v, out_own, out_oth,
):
    h = pl.program_id(0)
    rate = rates[h]
    length = cosine.shape[0]
    for row in range(tall_count.shape[0]):
        at = slice(row * length, (row + 1) * length)
        leave = leave_of(rate, tall_count[row])
        weighted = (key[0, at].astype(F32) * leave).astype(BF16)

        def set_both(state):
            low = state[row, 0]
            grad_v[0, at] = (value_part[0, at] + mm(weighted, low)).astype(BF16)
            total = key_part[0, at] + nt(value[0, at], low) * leave
            grad_k[0, at] = (unrotated(total, cosine[...], sine[...]) * QK**-0.5).astype(BF16)

        @pl.when(h < 2)
        def _():
            set_both(state_own)

        @pl.when(h >= 2)
        def _():
            set_both(state_oth)

    grad_wk = mm(normed_t[...], grad_k[0])
    grad_wv = mm(normed_t[...], grad_v[0])
    for step in range(4):

        @pl.when(h == step)
        def _():
            target = out_own if step < 2 else out_oth
            put_wide(target, info, grad_wk, 256 * (step % 2), step < 2)
            put_wide(target, info, grad_wv, 512 + 512 * (step % 2), step < 2)


def input_kernel(
    info, x, gain, grad_hidden, grad_q, grad_k, grad_v, grad_gate,
    q_own, q_oth, k_own, k_oth, v_own, v_oth, g_own, g_oth,
    input_grad, grad_gain, grad_bias, norm_sum,
):
    h = pl.program_id(0)

    @pl.when(h == 0)
    def _():
        norm_sum[...] = jnp.zeros_like(norm_sum)

    def add(wq, wk, wv, wg):
        norm_sum[...] += (
            nt(grad_q[0], flat(wq)) + nt(grad_k[0], flat(wk))
            + nt(grad_v[0], flat(wv)) + nt(grad_gate[0], flat(wg))
        )

    @pl.when(h < 2)
    def _():
        add(q_own, k_own, v_own, g_own)

    @pl.when(h >= 2)
    def _():
        add(q_oth, k_oth, v_oth, g_oth)

    @pl.when(h == 3)
    def _():
        grad_gain[...] = jnp.zeros_like(grad_gain)
        grad_bias[...] = jnp.zeros_like(grad_bias)

        @pl.loop(0, x.shape[0] // CHUNK)
        def _(k):
            at = pl.ds(pl.multiple_of(k * CHUNK, CHUNK), CHUNK)
            normal, scale = norm_parts(x[at, :].astype(F32), 1e-05)
            grad = norm_sum[at, :]
            grad_gain[...] += jnp.sum(grad * normal, axis=0, keepdims=True)
            grad_bias[...] += jnp.sum(grad, axis=0, keepdims=True)
            input_grad[at, :] = grad_hidden[at, :] + norm_back(
                grad * gain[...].astype(F32), normal, scale
            )


def per_device(
    inputs,
    doc_flags,
    first_gain,
    first_bias,
    w_query,
    w_key,
    w_value,
    w_gate,
    group_gain,
    w_output,
    second_gain,
    second_bias,
    w_up,
    w_down,
    cotangent,
):
    batches, row_count, length, width = inputs.shape
    rows = batches * row_count
    tokens = rows * length
    count = devices()
    chips = count // 2
    info, info_edge = chip_tables(LONE), chip_tables(EDGE)
    x = inputs.reshape(tokens, width)
    cot = cotangent.reshape(tokens, width)

    upper = upper_core()
    share = w_query.shape[0]
    last = len(orders(LONE)[0]) - 1

    keep, give = pack(info, w_query, w_key, w_value)
    qkv = stack_rows(info, keep, swap(give, 1))
    vectors = [first_gain, first_bias, second_gain, second_bias, group_gain]
    qkv, vectors = sync(qkv, vectors)
    got_qkv = step(qkv[None], last, LONE)

    sizes = [v.shape[0] for v in vectors]
    edges = [sum(sizes[:k]) for k in range(len(sizes) + 1)]
    lanes = -(-edges[-1] // 128) * 128
    table = jnp.concatenate([v.reshape(1, -1) for v in vectors], axis=1)
    table = jnp.pad(table, ((0, 15), (0, lanes - edges[-1])))

    def table_step(table, done, bit):
        got = swap(table, bit)
        turned = (place() // bit) % 2 == 1
        spot = sum(1 for other in done if other > bit)
        done.append(bit)
        return jnp.stack(
            [jnp.where(turned, got, table), jnp.where(turned, table, got)], axis=spot
        )

    bits = [1 << k for k in range(count.bit_length() - 1)]
    done = []
    for bit in (1, FAR):
        table = table_step(table, done, bit)
    got_qkv, table = sync(got_qkv, table)
    part, got = qkv[None], got_qkv
    start = lax.axis_index("seq") * length
    for turn in range(last - 1, 1, -1):
        part = join(part, got)
        got = step(part, turn, LONE)
        if turn == last - 1:
            table = table_step(table, done, 2)
        part, got, table, w_gate, w_up, w_output, w_down, doc_flags, start = sync(
            part, got, table, w_gate, w_up, w_output, w_down, doc_flags, start
        )

    part = join(part, got)
    got = step(part, 1, LONE)
    for bit in bits[:2:-1]:
        table = table_step(table, done, bit)

    top_keep, top_give = pack(info, w_gate, w_up)
    tall_keep, tall_give = pack(info, w_output, w_down)
    top = stack_rows(info, top_keep, swap(top_give, 1))
    tall_got = swap(tall_give, 1)
    low, high = jnp.where(upper, tall_got, tall_keep), jnp.where(upper, tall_keep, tall_got)
    go = jnp.concatenate([top[:, :1024], low[:, :512], high[:, :512]], axis=1)
    ff = jnp.concatenate([top[:, 1024:], low[:, 512:], high[:, 512:]], axis=1)
    go_part, ff_part = go[None], ff[None]
    part, got, go_part, ff_part, table, doc_flags = sync(
        part, got, go_part, ff_part, table, doc_flags
    )

    pieces = [part, got, step(part, 0, LONE), step(got, 0, LONE)]
    go_got = step(go_part, last, EDGE)
    ff_got = step(ff_part, last, EDGE)
    vector = table.reshape(count, -1, lanes)[:, 0]
    first_gain, first_bias, second_gain, second_bias, group_gain = [
        vector[:, a:b].reshape(1, -1) for a, b in zip(edges[:-1], edges[1:])
    ]
    group_gain = group_gain.reshape(H, 1, VH)

    positions = start + jnp.arange(length, dtype=jnp.int32)
    frequency = 10000.0 ** (-jnp.arange(QK // 2, dtype=F32) / (QK // 2))
    angles = positions.astype(F32)[:, None] * frequency[None, :]
    cosine, sine = jnp.cos(angles), jnp.sin(angles)
    rates = jnp.log1p(-(2.0 ** (-5.0 - 3.0 * jnp.arange(H, dtype=F32))))
    rates = jnp.where(upper, jnp.roll(rates, 2), rates)
    counts = jnp.cumsum(doc_flags.reshape(rows, length), axis=-1, dtype=jnp.int32)
    tall_count, wide_count = counts[:, :, None], counts[:, None, :]
    open_row = (counts[:, -1] == 0).astype(F32)
    near_row = swap(open_row, 1)
    decay = jnp.exp(rates[:2] * float(length))
    carry, near_carry = decay[None] * open_row[:, None], decay[None] * near_row[:, None]
    ahead = factors_of(carry, near_carry, False)
    behind = factors_of(carry, near_carry, True)

    per_head = (H, tokens)
    state_shape = (rows, 2, QK, VH)
    grad_shape = (chips, 2 * share)
    rates_in = (rates, None, None)
    unit = 2.0 * tokens * width * 512

    normed, normed_t = call(
        norm_kernel,
        1,
        info,
        [whole(x), whole(first_gain), whole(first_bias)],
        [whole_out((tokens, width), BF16), whole_out((width, tokens), BF16)],
        [],
        unit / 100,
        "norm",
        16,
    )
    pieces, go_part, go_got, ff_part, ff_got, normed, normed_t, tables, gains = sync(
        pieces, go_part, go_got, ff_part, ff_got, normed, normed_t,
        (cosine, sine, tall_count, wide_count, ahead, behind, rates),
        (second_gain, second_bias, group_gain),
    )
    cosine, sine, tall_count, wide_count, ahead, behind, rates = tables
    second_gain, second_bias, group_gain = gains
    rates_in = (rates, None, None)

    qkv_own = settle(info, pieces, True)
    qkv_oth = swap(qkv_own, 1)
    go_part = join(go_part, go_got)
    go_got = step(go_part, last - 1, EDGE)
    qkv_own, qkv_oth, go_part, go_got, ff_part, ff_got = sync(
        qkv_own, qkv_oth, go_part, go_got, ff_part, ff_got
    )

    go_part = join(go_part, go_got)
    go_got = step(go_part, last - 2, EDGE)
    ff_part = join(ff_part, ff_got)
    ff_got = step(ff_part, last - 1, EDGE)
    (query, key, value, mixing, sum_own, sum_oth) = call(
        project_kernel,
        H,
        info,
        [
            rates_in, whole(normed), whole(cosine), whole(sine),
            whole(tall_count), whole(wide_count),
            columns(qkv_own, 256, 0, True), columns(qkv_own, 256, 2, True),
            columns(qkv_own, 512, 2, True),
            columns(qkv_oth, 256, 0, False), columns(qkv_oth, 256, 2, False),
            columns(qkv_oth, 512, 2, False),
        ],
        [
            head_out(per_head + (QK,), BF16), head_out(per_head + (QK,), BF16),
            head_out(per_head + (VH,), BF16), head_out(per_head + (length,), BF16),
            own_out(state_shape, F32), other_out(state_shape, F32),
        ],
        [pltpu.VMEM((tokens, 1024), F32)],
        10 * unit,
        "project",
        56,
    )
    go_part, go_got, ff_part, ff_got, sum_own, sum_oth = sync(
        go_part, go_got, ff_part, ff_got, sum_own, sum_oth
    )
    for turn in range(last - 3, 0, -1):
        go_part = join(go_part, go_got)
        go_got = step(go_part, turn, EDGE)
        ff_part = join(ff_part, ff_got)
        ff_got = step(ff_part, turn + 1, EDGE)
        go_part, go_got, ff_part, ff_got = sync(go_part, go_got, ff_part, ff_got)
    sum_near = swap(sum_oth, 1)
    ff_part = join(ff_part, ff_got)
    sum_own, sum_near, go_part, go_got, ff_part = sync(
        sum_own, sum_near, go_part, go_got, ff_part
    )

    states = tuple(ahead) + (sum_own, sum_near)
    phases = phase_count(rows)
    arrivals = hop(states, [], 1, False)
    go_first = step(go_part, 0, EDGE)
    states, arrivals, go_part, go_got, go_first = sync(
        states, arrivals, go_part, go_got, go_first
    )
    arrived = [arrivals]

    arrivals = hop(states, arrived, 2, False)
    go_second = step(go_got, 0, EDGE)
    states, arrived, arrivals, pieces, ff_part = sync(
        states, arrived, arrivals, [go_part, go_got, go_first, go_second], ff_part
    )
    arrived = arrived + [arrivals]

    arrivals = hop(states, arrived, 3, False)
    ff_got = step(ff_part, 1, EDGE)
    go_own = settle(info_edge, pieces, True)
    go_oth = swap(go_own, 1)
    states, arrived, arrivals, go_own, go_oth, normed, ff_part, ff_got = sync(
        states, arrived, arrivals, go_own, go_oth, normed, ff_part, ff_got
    )
    arrived = arrived + [arrivals]

    for phase in range(4, phases + 1):
        arrivals = hop(states, arrived, phase, False)
        if phase == 4:
            ff_first = step(ff_part, 0, EDGE)
            ff_others = [swap(ff_part, 1), swap(ff_got, 1)]
            (gate,) = call(
                gate_kernel,
                H,
                info,
                [whole(normed), columns(go_own, 512, 0, True), columns(go_oth, 512, 0, False)],
                [head_out(per_head + (VH,), F32)],
                [],
                4 * unit,
                "gate",
                20,
            )
        states, arrived, arrivals, gate, ff_part, ff_got, ff_first, ff_others = sync(
            states, arrived, arrivals, gate, ff_part, ff_got, ff_first, ff_others
        )
        arrived = arrived + [arrivals]
    state_own, state_oth = end_states(states, arrived, False)
    state_own, state_oth, ff_got, ff_first = sync(state_own, state_oth, ff_got, ff_first)
    ff_second = step(ff_got, 0, EDGE)
    ff_others = ff_others + [swap(ff_first, 1)]

    retained, mixed_t, hidden, normed_second, normed_second_t = call(
        mix_kernel,
        H,
        info,
        [
            rates_in, whole(x), real_in(group_gain), whole(second_gain), whole(second_bias),
            whole(tall_count), head_in(query), head_in(value),
            head_in(mixing), head_in(gate),
            own_in(state_own), other_in(state_oth), tall(go_own), tall(go_oth),
        ],
        [
            head_out(per_head + (VH,), F32), head_out((H, VH, tokens), BF16),
            whole_out((tokens, width), F32), whole_out((tokens, width), BF16),
            whole_out((width, tokens), BF16),
        ],
        [],
        5 * unit,
        "mix",
        32,
    )
    ff_second, ff_others, hidden = sync(ff_second, ff_others, hidden)
    ff_others = ff_others + [swap(ff_second, 1)]
    ff_own = settle(info_edge, [ff_part, ff_got, ff_first, ff_second], True)
    ff_oth = settle(info_edge, ff_others, False)
    output, grad_hidden, grad_low, grad_second_gain, grad_second_bias, ff_g_own, ff_g_oth = call(
        feed_kernel,
        4,
        info_edge,
        [
            whole(hidden), whole(normed_second), whole(normed_second_t), whole(cot),
            whole(second_gain),
            columns(ff_own, 512, 0, True), columns(ff_oth, 512, 0, False),
            tall(ff_own), tall(ff_oth),
        ],
        [
            whole_out((tokens, width), BF16), whole_out((tokens, width), F32),
            whole_out((tokens, width), BF16), whole_out((1, width), F32),
            whole_out((1, width), F32),
            whole_out(grad_shape + (2048,), BF16), whole_out(grad_shape + (2048,), BF16),
        ],
        [
            pltpu.VMEM((tokens, 512), F32), pltpu.VMEM((tokens, width), F32),
            pltpu.VMEM((tokens, width), F32),
        ],
        24 * unit,
        "feed",
        48,
    )

    ff_g_got = swap(ff_g_oth, 1)
    grad_ret, grad_gate, grad_group_gain, gstate_own, gstate_oth = call(
        unmix_kernel,
        H,
        info,
        [
            rates_in, whole(grad_low), real_in(group_gain), whole(tall_count), head_in(query),
            head_in(retained), head_in(gate), tall(go_own), tall(go_oth),
        ],
        [
            head_out(per_head + (VH,), BF16), head_out(per_head + (VH,), BF16),
            (
                (H, 1, VH), F32, (1, 1, VH),
                lambda h, info: (real(h, info), 0, 0),
            ),
            own_out(state_shape, F32), other_out(state_shape, F32),
        ],
        [],
        5 * unit,
        "unmix",
        32,
    )
    ff_g_own, ff_g_got, gstate_own, gstate_oth, grad_gate, grad_ret = sync(
        ff_g_own, ff_g_got, gstate_own, gstate_oth, grad_gate, grad_ret
    )
    gstate_near = swap(gstate_oth, 1)
    ff_sum = [Piece(ff_g_own), Piece(ff_g_got)]
    ff_first = upper_part(ff_sum, 0, 1)
    gstate_own, gstate_near, grad_gate, grad_ret, ff_sum, ff_first = sync(
        gstate_own, gstate_near, grad_gate, grad_ret, ff_sum, ff_first
    )

    states = tuple(behind) + (gstate_own, gstate_near)
    arrived = []
    arrivals = hop(states, arrived, 1, True)
    ff_first = send(ff_first, 0, EDGE)
    ff_second = upper_part(ff_sum, 0, 0)
    grad_q, key_part, value_part = call(
        inside_kernel,
        H,
        info,
        [
            rates_in, head_in(grad_ret),
            head_in(query), head_in(key), head_in(value), head_in(mixing),
            whole(cosine), whole(sine), whole(tall_count), whole(wide_count),
            own_in(state_own), other_in(state_oth),
        ],
        [
            head_out(per_head + (QK,), BF16),
            head_out(per_head + (QK,), F32), head_out(per_head + (VH,), F32),
        ],
        [],
        3 * unit,
        "inside",
        24,
    )
    states, arrivals, ff_sum, ff_first, ff_second, grad_q, key_part, value_part = sync(
        states, arrivals, ff_sum, ff_first, ff_second, grad_q, key_part, value_part
    )
    arrived = arrived + [arrivals]

    arrivals = hop(states, arrived, 2, True)
    ff_sum = ff_sum + ff_first
    ff_second = send(ff_second, 0, EDGE)
    ff_next = upper_part(ff_sum, 1)
    go_g_own, go_g_oth = call(
        outer_kernel,
        H,
        info,
        [
            whole(grad_low), whole(normed_t), head_in(mixed_t), head_in(grad_gate),
            head_in(grad_q),
        ],
        [whole_out(grad_shape + (2560,), BF16), whole_out(grad_shape + (2560,), BF16)],
        [],
        11 * unit,
        "outer",
        44,
    )
    states, arrived, arrivals, ff_sum, ff_second, ff_next, go_g_own, go_g_oth = sync(
        states, arrived, arrivals, ff_sum, ff_second, ff_next, go_g_own, go_g_oth
    )
    ff_sum = ff_sum + ff_second
    arrived = arrived + [arrivals]

    arrivals = hop(states, arrived, 3, True)
    go_g_got = swap(go_g_oth, 1)
    ff_sum = ff_sum + send(ff_next, 1, EDGE)
    go_sum = [Piece(go_g_own), Piece(go_g_got)]
    go_first = upper_part(go_sum, 0, 1)
    states, arrived, arrivals, go_sum, go_first, ff_sum = sync(
        states, arrived, arrivals, go_sum, go_first, ff_sum
    )
    arrived = arrived + [arrivals]

    for phase in range(4, phases + 1):
        arrivals = hop(states, arrived, phase, True)
        if phase == 4:
            go_first = send(go_first, 0, LONE)
            go_second = upper_part(go_sum, 0, 0)
            ff_next = upper_part(ff_sum, 2)
        states, arrived, arrivals, go_sum, go_first, go_second, ff_sum, ff_next = sync(
            states, arrived, arrivals, go_sum, go_first, go_second, ff_sum, ff_next
        )
        arrived = arrived + [arrivals]
    after_own, after_oth = end_states(states, arrived, True)
    after_own, after_oth, go_sum, go_first, go_second, ff_sum, ff_next = sync(
        after_own, after_oth, go_sum, go_first, go_second, ff_sum, ff_next
    )
    go_sum = go_sum + go_first
    go_next = upper_part(go_sum, 1)
    go_second = send(go_second, 0, LONE)
    ff_sum = ff_sum + send(ff_next, 2, EDGE)

    grad_k, grad_v, kv_g_own, kv_g_oth = call(
        last_kernel,
        H,
        info,
        [
            rates_in, whole(normed_t), head_in(key), head_in(value), head_in(key_part),
            head_in(value_part), whole(cosine), whole(sine), whole(tall_count),
            own_in(after_own), other_in(after_oth),
        ],
        [
            head_out(per_head + (QK,), BF16), head_out(per_head + (VH,), BF16),
            whole_out(grad_shape + (1536,), BF16), whole_out(grad_shape + (1536,), BF16),
        ],
        [],
        8 * unit,
        "last",
        32,
    )
    ff_sum, go_sum, go_second, go_next, kv_g_own, kv_g_oth, grad_k, grad_v = sync(
        ff_sum, go_sum, go_second, go_next, kv_g_own, kv_g_oth, grad_k, grad_v
    )
    go_sum = go_sum + go_second
    kv_g_got = swap(kv_g_oth, 1)
    ff_next = upper_part(ff_sum, 3)
    kv_g_own, kv_g_got, go_sum, ff_sum, ff_next = sync(
        kv_g_own, kv_g_got, go_sum, ff_sum, ff_next
    )
    kv_sum = [Piece(kv_g_own), Piece(kv_g_got)]
    kv_first, kv_second = shrink(kv_sum, 0, LONE, 1), shrink(kv_sum, 0, LONE, 0)
    go_next = send(go_next, 1, LONE)
    ff_sum = ff_sum + send(ff_next, 3, EDGE)
    for turn in range(4, last + 1):
        ff_sum = ff_sum + shrink(ff_sum, turn, EDGE)
    input_grad, grad_first_gain, grad_first_bias = call(
        input_kernel,
        H,
        info,
        [
            whole(x), whole(first_gain), whole(grad_hidden), head_in(grad_q),
            head_in(grad_k), head_in(grad_v), head_in(grad_gate),
            columns(qkv_own, 256, 0, True), columns(qkv_oth, 256, 0, False),
            columns(qkv_own, 256, 2, True), columns(qkv_oth, 256, 2, False),
            columns(qkv_own, 512, 2, True), columns(qkv_oth, 512, 2, False),
            columns(go_own, 512, 0, True), columns(go_oth, 512, 0, False),
        ],
        [
            whole_out((tokens, width), F32), whole_out((1, width), F32),
            whole_out((1, width), F32),
        ],
        [pltpu.VMEM((tokens, width), F32)],
        6 * unit,
        "input",
        56,
    )
    kv_sum, kv_first, kv_second, go_sum, go_next, ff_sum, input_grad, sums = sync(
        kv_sum, kv_first, kv_second, go_sum, go_next, ff_sum, input_grad,
        (grad_first_gain, grad_first_bias),
    )
    grad_first_gain, grad_first_bias = sums
    small = jnp.concatenate(
        [
            grad_first_gain, grad_first_bias, grad_second_gain, grad_second_bias,
            grad_group_gain.reshape(-1, width), jnp.zeros((2, width), F32),
        ],
        axis=0,
    )

    kv_sum = kv_sum + kv_first + kv_second
    go_sum = go_sum + go_next
    kv_next = shrink(kv_sum, 1, LONE)
    go_next = shrink(go_sum, 2, LONE)
    small = small + swap(small, FAR)
    kv_sum, kv_next, go_sum, go_next, small = sync(kv_sum, kv_next, go_sum, go_next, small)
    kv_sum = kv_sum + kv_next
    go_sum = go_sum + go_next
    kv_next = shrink(kv_sum, 2, LONE)
    for turn in range(3, last + 1):
        go_sum = go_sum + shrink(go_sum, turn, LONE)
    small = small + swap(small, 2)
    ff_grad = summed(ff_sum, 0, 1)[0]
    kv_sum, kv_next, small, ff_grad = sync(kv_sum, kv_next, small, ff_grad)
    kv_sum = kv_sum + kv_next
    for turn in range(3, last + 1):
        kv_sum = kv_sum + shrink(kv_sum, turn, LONE)
    for bit in bits[3:] + bits[:1]:
        small = small + swap(small, bit)
    group = small[4:6].reshape(-1)
    small = lax.dynamic_slice_in_dim(small, place() * sizes[0], sizes[0], 1)
    group = lax.dynamic_slice_in_dim(group, place() * sizes[4], sizes[4], 0)

    go_grad, kv_grad = summed(go_sum, 0, 1)[0], summed(kv_sum, 0, 1)[0]
    ff_mine, ff_got = finish_wide(ff_grad[:, :1024])
    go_mine, go_got = finish_wide(jnp.concatenate([go_grad[:, :1024], go_grad[:, 2048:]], axis=1))
    kv_mine, kv_got = finish_wide(kv_grad)

    def wide(mine, got, start, stop):
        return ordered(mine[:, start:stop], got[:, start:stop], 1)

    return (
        output.reshape(inputs.shape),
        input_grad.reshape(inputs.shape),
        small[0],
        small[1],
        wide(go_mine, go_got, 1024, 1536),
        wide(kv_mine, kv_got, 0, 512),
        wide(kv_mine, kv_got, 512, 1536),
        wide(go_mine, go_got, 0, 1024),
        group,
        finish_tall(go_grad[:, 1024:2048]),
        small[2],
        small[3],
        wide(ff_mine, ff_got, 0, 1024),
        finish_tall(ff_grad[:, 1024:2048]),
    )


def solution(mesh):
    return jax.shard_map(
        per_device,
        mesh=mesh,
        in_specs=(
            P(None, "dp", "seq", None),
            P(None, "dp", "seq"),
            P(("dp", "seq")),
            P(("dp", "seq")),
            P(("dp", "seq"), None),
            P(("dp", "seq"), None),
            P(("dp", "seq"), None),
            P(("dp", "seq"), None),
            P(("dp", "seq")),
            P(("dp", "seq"), None),
            P(("dp", "seq")),
            P(("dp", "seq")),
            P(("dp", "seq"), None),
            P(("dp", "seq"), None),
            P(None, "dp", "seq", None),
        ),
        out_specs=(
            P(None, "dp", "seq", None),
            P(None, "dp", "seq", None),
            P(("dp", "seq")),
            P(("dp", "seq")),
            P(("dp", "seq"), None),
            P(("dp", "seq"), None),
            P(("dp", "seq"), None),
            P(("dp", "seq"), None),
            P(("dp", "seq")),
            P(("dp", "seq"), None),
            P(("dp", "seq")),
            P(("dp", "seq")),
            P(("dp", "seq"), None),
            P(("dp", "seq"), None),
        ),
        check_vma=False,
    )
```
